32 devices in a mesh: dp: 4 (over y, x), filt: 8 (over z, core).
Axes of the slice: x: 2, y: 2, z: 4, core: 2. Of those that a mesh axis runs over, the one named last changes fastest.
Arguments:
- images: bfloat16 [576, 3, 1024], P('filt'), may hold values from -4 to 4
- labels: int32 [576], P('filt'), may hold values from 0 to 9
- corners: int32 [576, 2], P('filt'), may hold values from -8 to 24
- partners: int32 [576], P('filt'), may hold values from 0 to 575, each once
- stem_w: float32 [27, 16], replicated, may hold values from -1.25 to 1.25
- stem_w_m: float32 [27, 16], replicated, may hold values from -1.1444092e-05 to 1.1444092e-05
- stem_w_v: float32 [27, 16], replicated, may hold values from 3.271381e-13 to 1.3085524e-12
- proj_a: float32 [16, 160], replicated, may hold values from -1.5 to 1.5
- proj_a_m: float32 [16, 160], replicated, may hold values from -1.1444092e-05 to 1.1444092e-05
- proj_a_v: float32 [16, 160], replicated, may hold values from 3.271381e-13 to 1.3085524e-12
- proj_b: float32 [160, 320], replicated, may hold values from -0.5 to 0.5
- proj_b_m: float32 [160, 320], replicated, may hold values from -1.1444092e-05 to 1.1444092e-05
- proj_b_v: float32 [160, 320], replicated, may hold values from 3.271381e-13 to 1.3085524e-12
- proj_c: float32 [320, 640], P(None, 'dp'), may hold values from -0.3125 to 0.3125
- proj_c_m: float32 [320, 640], P(None, 'dp'), may hold values from -1.1444092e-05 to 1.1444092e-05
- proj_c_v: float32 [320, 640], P(None, 'dp'), may hold values from 3.271381e-13 to 1.3085524e-12
- conv_w: float32 [2, 640, 5760], P(None, 'dp'), may hold values from -0.078125 to 0.078125
- conv_w_m: float32 [2, 640, 5760], P(None, 'dp'), may hold values from -1.1444092e-05 to 1.1444092e-05
- conv_w_v: float32 [2, 640, 5760], P(None, 'dp'), may hold values from 3.271381e-13 to 1.3085524e-12
- head_w: float32 [640, 10], P('dp'), may hold values from -0.625 to 0.625
- head_w_m: float32 [640, 10], P('dp'), may hold values from -0.00015258789 to 0.00015258789
- head_w_v: float32 [640, 10], P('dp'), may hold values from 9.375e-11 to 3.75e-10
- norm_p: float32 [6, 640], P(None, 'dp'), may hold values from -0.5 to 7, as said below
- norm_p_m: float32 [6, 640], P(None, 'dp'), may hold values from -4.5776367e-05 to 4.5776367e-05
- norm_p_v: float32 [6, 640], P(None, 'dp'), may hold values from 5.2342098e-12 to 2.0936839e-11
Outputs:
- stem_w_mom: float32 [27, 16], replicated
- stem_w_sq: float32 [27, 16], replicated
- stem_w_new: float32 [27, 16], replicated
- proj_a_mom: float32 [16, 160], replicated
- proj_a_sq: float32 [16, 160], replicated
- proj_a_new: float32 [16, 160], replicated
- proj_b_mom: float32 [160, 320], replicated
- proj_b_sq: float32 [160, 320], replicated
- proj_b_new: float32 [160, 320], replicated
- proj_c_mom: float32 [320, 640], P(None, 'dp')
- proj_c_sq: float32 [320, 640], P(None, 'dp')
- proj_c_new: float32 [320, 640], P(None, 'dp')
- conv_w_mom: float32 [2, 640, 5760], P(None, 'dp')
- conv_w_sq: float32 [2, 640, 5760], P(None, 'dp')
- conv_w_new: float32 [2, 640, 5760], P(None, 'dp')
- head_w_mom: float32 [640, 10], P('dp')
- head_w_sq: float32 [640, 10], P('dp')
- head_w_new: float32 [640, 10], P('dp')
- norm_p_mom: float32 [6, 640], P(None, 'dp')
- norm_p_sq: float32 [6, 640], P(None, 'dp')
- norm_p_new: float32 [6, 640], P(None, 'dp')
- loss_sum: float32 [], replicated
- grad_norm: float32 [], replicated
The draws below stay inside these ranges and needn't reach their ends.
Inputs may be any that keep to these rules, and one draw needn't show every extreme that they name: `partners`: a permutation of the 576 images. `corners`: a square may reach past the image's border. `norm_p`: rows 0, 2 and 4 are positive gains, rows 1, 3 and 5 biases.
All inputs are finite; a program needn't handle non-finite values.
Results may differ from the reference program's by a relative error of at most 0.03.
Values may be sent and summed in bfloat16 or wider, within the bound.
No kernel may reach another device: no remote copies, remote signals or barrier semaphores. Data moves between devices by JAX's collectives and lax.ppermute only.
A program may use at most 256 MiB of HBM per device.

```python
import math
import jax
import jax.numpy as jnp
from jax import lax

C0 = 16
C1 = 160
C2 = 320
C3 = 640
NCLS = 10
SIDE = 32
CUT = 16
STEP = 10
GRID = 8
IMAGES = 576
NPARAM = 7642032


def draw_norm_p(key, part):
    key = jax.random.fold_in(key, 5)
    first_key, second_key = jax.random.split(key)
    position = jnp.arange(C3, dtype=jnp.float32) / C3
    rising = 1.0 + 2.0 * position
    gains = rising[None, :] * jax.random.uniform(first_key, (3, C3), jnp.float32, 0.6, 1.4)
    biases = jax.random.uniform(second_key, (3, C3), jnp.float32, -0.5, 0.5)
    return jnp.stack([gains, biases], axis=1).reshape(6, C3)


def place_ends(values, key, least, largest):
    extent = values.shape
    spot = [jax.random.randint(jax.random.fold_in(key, axis), (), 0, extent[axis]) for axis in range(len(extent))]
    values = values.at[tuple(spot)].set(least)
    longest = extent.index(max(extent))
    spot[longest] = (spot[longest] + 1) % extent[longest]
    return values.at[tuple(spot)].set(largest)


def levels(own_key, dims, cuts, least, largest):
    def one(axis_at, shards_of):
        draws = jax.random.uniform(jax.random.fold_in(jax.random.fold_in(own_key, 6), axis_at), (shards_of,), jnp.float32, least / len(cuts), largest / len(cuts))
        return jnp.repeat(jnp.exp(draws), dims[axis_at] // shards_of).reshape((-1,) + (1,) * (len(dims) - axis_at - 1))

    loudness = one(*cuts[0])
    for cut in cuts[1:]:
        loudness = loudness * one(*cut)
    return loudness


def scatter_about(key, dims, deviation, bound, cuts=(), kind=jnp.bfloat16):
    entries = deviation * jax.random.normal(key, dims, jnp.float32)
    if cuts:
        entries = entries * levels(key, dims, cuts, -0.22, 0.18)
    return jnp.clip(entries, -bound, bound).astype(kind)


def setup_inputs(seed: int = 0) -> dict:
    key_list = jax.random.split(jax.random.key(seed), 26)
    return {
        "images": scatter_about(key_list[0], (IMAGES, 3, SIDE * SIDE), 1.0, 4.0, ((0, 8),)),
        "labels": place_ends(jax.random.randint(key_list[1], (IMAGES,), 0, NCLS), jax.random.fold_in(key_list[1], 1), 0, NCLS - 1).astype(jnp.int32),
        "corners": place_ends(jax.random.randint(key_list[2], (IMAGES, 2), 0 - CUT // 2, SIDE - CUT // 2 + 1), jax.random.fold_in(key_list[2], 1), 0 - CUT // 2, (SIDE - CUT // 2 + 1) - 1).astype(jnp.int32),
        "partners": jax.random.permutation(key_list[3], IMAGES).astype(jnp.int32),
        "stem_w": scatter_about(key_list[4], (27, C0), 27 ** -0.5, 1.25, (), jnp.float32),
        "stem_w_m": scatter_about(key_list[5], (27, C0), (0.11 * 0.05 / NPARAM ** 0.5), 1.1444091796875e-05, (), jnp.float32),
        "stem_w_v": jnp.clip(jnp.exp(jax.random.uniform(key_list[6], (27, C0), jnp.float32, math.log(3.2713811043763585e-13), math.log(1.3085524417505434e-12))), 3.2713811043763585e-13, 1.3085524417505434e-12),
        "proj_a": scatter_about(key_list[7], (C0, C1), C0 ** -0.5, 1.5, (), jnp.float32),
        "proj_a_m": scatter_about(key_list[8], (C0, C1), (0.11 * 0.05 / NPARAM ** 0.5), 1.1444091796875e-05, (), jnp.float32),
        "proj_a_v": jnp.clip(jnp.exp(jax.random.uniform(key_list[9], (C0, C1), jnp.float32, math.log(3.2713811043763585e-13), math.log(1.3085524417505434e-12))), 3.2713811043763585e-13, 1.3085524417505434e-12),
        "proj_b": scatter_about(key_list[10], (C1, C2), C1 ** -0.5, 0.5, (), jnp.float32),
        "proj_b_m": scatter_about(key_list[11], (C1, C2), (0.11 * 0.05 / NPARAM ** 0.5), 1.1444091796875e-05, (), jnp.float32),
        "proj_b_v": jnp.clip(jnp.exp(jax.random.uniform(key_list[12], (C1, C2), jnp.float32, math.log(3.2713811043763585e-13), math.log(1.3085524417505434e-12))), 3.2713811043763585e-13, 1.3085524417505434e-12),
        "proj_c": scatter_about(key_list[13], (C2, C3), C2 ** -0.5, 0.3125, ((1, 4),), jnp.float32),
        "proj_c_m": scatter_about(key_list[14], (C2, C3), (0.11 * 0.05 / NPARAM ** 0.5), 1.1444091796875e-05, ((1, 4),), jnp.float32),
        "proj_c_v": jnp.clip(jnp.exp(math.log(1.3085524417505434e-12) - 1.3862944 * jax.random.uniform(key_list[15], (C2, C3), jnp.float32) ** levels(key_list[15], (C2, C3), ((1, 4),), -0.2, 0.2)), 3.2713811043763585e-13, 1.3085524417505434e-12),
        "conv_w": scatter_about(key_list[16], (2, C3, 9 * C3), (9 * C3) ** -0.5, 0.078125, ((1, 4),), jnp.float32),
        "conv_w_m": scatter_about(key_list[17], (2, C3, 9 * C3), (0.11 * 0.05 / NPARAM ** 0.5), 1.1444091796875e-05, ((1, 4),), jnp.float32),
        "conv_w_v": jnp.clip(jnp.exp(math.log(1.3085524417505434e-12) - 1.3862944 * jax.random.uniform(key_list[18], (2, C3, 9 * C3), jnp.float32) ** levels(key_list[18], (2, C3, 9 * C3), ((1, 4),), -0.2, 0.2)), 3.2713811043763585e-13, 1.3085524417505434e-12),
        "head_w": scatter_about(key_list[19], (C3, NCLS), (C3 // 8) ** -0.5, 0.625, ((0, 4),), jnp.float32),
        "head_w_m": scatter_about(key_list[20], (C3, NCLS), (0.11 * 0.02 / (C3 * NCLS) ** 0.5), 0.00015258789, ((0, 4),), jnp.float32),
        "head_w_v": jnp.clip(jnp.exp(math.log(3.750000032720635e-10) - 1.3862944 * jax.random.uniform(key_list[21], (C3, NCLS), jnp.float32) ** levels(key_list[21], (C3, NCLS), ((0, 4),), -0.2, 0.2)), 9.375000081801588e-11, 3.750000032720635e-10),
        "norm_p": draw_norm_p(jax.random.fold_in(key_list[25], 71), 0),
        "norm_p_m": scatter_about(key_list[23], (6, C3), (0.44 * 0.05 / NPARAM ** 0.5), 4.57763671875e-05, ((1, 4),), jnp.float32),
        "norm_p_v": jnp.clip(jnp.exp(math.log(2.0936839068008695e-11) - 1.3862944 * jax.random.uniform(key_list[24], (6, C3), jnp.float32) ** levels(key_list[24], (6, C3), ((1, 4),), -0.2, 0.2)), 5.234209767002174e-12, 2.0936839068008695e-11),
    }


@jax.custom_vjp
def low(v):
    return lax.optimization_barrier(v.astype(jnp.bfloat16)).astype(jnp.float32)

@jax.custom_vjp
def low_back(v):
    return v

def low_keep(v):
    return (low(v), None)

def low_pass(kept, grad):
    return (grad,)

def back_keep(v):
    return (v, None)

def back_low(kept, grad):
    return (low(grad),)
low.defvjp(low_keep, low_pass)
low_back.defvjp(back_keep, back_low)
beta_one = 0.9
beta_two = 0.999
adam_eps = 1e-08
weight_decay = 0.0005
clip_limit = 0.05
norm_eps = 1e-05
highest = lax.Precision.HIGHEST

def blend_inputs(images, corners, partners, source_images, source_labels):
    partner_images = jnp.take(source_images, partners, axis=0)
    partner_labels = jnp.take(source_labels, partners, axis=0)
    places = jnp.arange(images.shape[1], dtype=jnp.int32)
    inside_rows = (places[None, :] >= corners[:, 0:1]) & (places[None, :] < corners[:, 0:1] + CUT)
    inside_cols = (places[None, :] >= corners[:, 1:2]) & (places[None, :] < corners[:, 1:2] + CUT)
    square = inside_rows[:, :, None] & inside_cols[:, None, :]
    blended = jnp.where(square[:, :, :, None], partner_images, images)
    area = lax.optimization_barrier(jnp.sum(inside_rows.astype(jnp.int32), axis=1)) * lax.optimization_barrier(jnp.sum(inside_cols.astype(jnp.int32), axis=1))
    own_share = 1.0 - area.astype(jnp.float32) / float(images.shape[1] * images.shape[2])
    return (blended, partner_labels, own_share)

def stem_patches(blended):
    padded = jnp.pad(blended, ((0, 0), (1, 1), (1, 1), (0, 0)))
    length = blended.shape[1]
    pieces = [padded[:, row_shift:row_shift + length:4, col_shift:col_shift + length:4, :] for row_shift in range(3) for col_shift in range(3)]
    stacked = jnp.concatenate(pieces, axis=3)
    return stacked.reshape(-1, stacked.shape[3])

def matmul(left, right):
    return jnp.dot(left, right, precision=highest, preferred_element_type=jnp.float32)

def conv_taps(field, weight):
    side_cells = field.shape[1]
    padded = jnp.pad(field, ((0, 0), (1, 1), (1, 1), (0, 0)))
    result = jnp.zeros(field.shape[:3] + (weight.shape[2],), jnp.float32)
    for neighbour in range(9):
        row_shift, col_shift = (neighbour // 3, neighbour % 3)
        window = padded[:, row_shift:row_shift + side_cells, col_shift:col_shift + side_cells, :]
        result = result + jnp.einsum('bhwc,co->bhwo', window, weight[neighbour], precision=highest, preferred_element_type=jnp.float32)
    return result

def batch_norm(values, gain, bias):
    mean = lax.optimization_barrier(jnp.mean(values, axis=0))
    meansq = lax.optimization_barrier(jnp.mean(values * values, axis=0))
    rstd = lax.rsqrt(meansq - mean * mean + norm_eps)
    return (values - mean) * rstd * gain + bias

def forward(weights, patches, own_share, own_hot, other_hot):
    stem_w, proj_a, proj_b, proj_c, conv_w, head_w, norm_p = weights
    row_count = patches.shape[0]
    gelu = jax.nn.gelu
    stem_out = low_back(matmul(patches, low(stem_w)))
    mid_one = low_back(matmul(low(gelu(stem_out)), low(proj_a)))
    mid_two = low_back(matmul(low(gelu(mid_one)), low(proj_b)))
    base = low_back(matmul(low(gelu(mid_two)), low(proj_c)))
    kernels = low(conv_w).reshape(2, C3, 9, C3).transpose(0, 2, 3, 1)
    field_one = low(gelu(batch_norm(base, norm_p[0], norm_p[1])))
    conv_one = low_back(conv_taps(field_one.reshape(-1, GRID, GRID, C3), kernels[0]).reshape(row_count, C3))
    field_two = low(gelu(batch_norm(conv_one, norm_p[2], norm_p[3])))
    conv_two = low_back(conv_taps(field_two.reshape(-1, GRID, GRID, C3), kernels[1]).reshape(row_count, C3))
    summed = base + conv_two
    pooled = lax.optimization_barrier(jnp.mean(gelu(batch_norm(summed, norm_p[4], norm_p[5])).reshape(-1, GRID * GRID, C3), axis=1))
    logits = low_back(matmul(low(pooled), low(head_w)))
    target = own_share[:, None] * own_hot + (1.0 - own_share[:, None]) * other_hot
    lse = jax.nn.logsumexp(logits, axis=1)
    total_loss = jnp.sum(lse - lax.optimization_barrier(jnp.sum(target * logits, axis=1)))
    return (total_loss / IMAGES, total_loss)

def adamw(weight, gradient, first, second, step_rate):
    first_new = beta_one * first + (1.0 - beta_one) * gradient
    second_new = beta_two * second + (1.0 - beta_two) * gradient * gradient
    first_hat = first_new / (1.0 - beta_one ** STEP)
    second_hat = second_new / (1.0 - beta_two ** STEP)
    weight_new = weight - step_rate * (first_hat / (jnp.sqrt(second_hat) + adam_eps) + weight_decay * weight)
    return (first_new, second_new, weight_new)

def step_rates():
    return (0.7 / math.sqrt(27.0), 0.7 / math.sqrt(C0), 0.7 / math.sqrt(C1), 0.7 / math.sqrt(C2), 0.7 / math.sqrt(9.0 * C3), 0.7 / math.sqrt(C3 / 8.0), 0.8)

def reference(images, labels, corners, partners, stem_w, stem_w_m, stem_w_v, proj_a, proj_a_m, proj_a_v, proj_b, proj_b_m, proj_b_v, proj_c, proj_c_m, proj_c_v, conv_w, conv_w_m, conv_w_v, head_w, head_w_m, head_w_v, norm_p, norm_p_m, norm_p_v):
    pictures = images.astype(jnp.float32).reshape(-1, 3, SIDE, SIDE).transpose(0, 2, 3, 1)
    blended, partner_labels, own_share = blend_inputs(pictures, corners, partners, pictures, labels)
    patches = stem_patches(blended)
    classes = jnp.arange(NCLS, dtype=jnp.int32)
    own_hot = (labels[:, None] == classes[None, :]).astype(jnp.float32)
    other_hot = (partner_labels[:, None] == classes[None, :]).astype(jnp.float32)
    params = (stem_w, proj_a, proj_b, proj_c, conv_w, head_w, norm_p)

    def objective(*weights):
        return forward(weights, patches, own_share, own_hot, other_hot)
    mean_loss, pullback, total_loss = jax.vjp(objective, *params, has_aux=True)
    gradients = pullback(jnp.ones_like(mean_loss))
    squares = sum((jnp.sum(gradient * gradient) for gradient in gradients))
    grad_norm = jnp.sqrt(squares)
    scale = jnp.minimum(1.0, clip_limit / grad_norm)
    firsts = (stem_w_m, proj_a_m, proj_b_m, proj_c_m, conv_w_m, head_w_m, norm_p_m)
    seconds = (stem_w_v, proj_a_v, proj_b_v, proj_c_v, conv_w_v, head_w_v, norm_p_v)
    updated = [adamw(params[index], gradients[index] * scale, firsts[index], seconds[index], step_rates()[index]) for index in range(7)]
    return (updated[0][0], updated[0][1], updated[0][2], updated[1][0], updated[1][1], updated[1][2], updated[2][0], updated[2][1], updated[2][2], updated[3][0], updated[3][1], updated[3][2], updated[4][0], updated[4][1], updated[4][2], updated[5][0], updated[5][1], updated[5][2], updated[6][0], updated[6][1], updated[6][2], total_loss, grad_norm)
```

```python
import functools
import math

import jax
import jax.numpy as jnp
from jax import lax
from jax.experimental import pallas as pl
from jax.experimental.pallas import tpu as pltpu
from jax.sharding import PartitionSpec as P

C0 = 16
C1 = 160
C2 = 320
C3 = 640
WIDE = 384
TRIPLE = 3 * C3
SIDE = 32
CUT = 16
STEP = 10
PLANE = 640
META = 576
CHUNK = 48

beta_one = 0.9
beta_two = 0.999
adam_eps = 1e-08
weight_decay = 0.0005
clip_limit = 0.05
norm_eps = 1e-05
gelu_one = math.sqrt(2.0 / math.pi)
gelu_three = 0.044715 * gelu_one

half = jnp.bfloat16
full = jnp.float32
NT = (((1,), (1,)), ((), ()))
NN = (((1,), (0,)), ((), ()))
TN = (((0,), (0,)), ((), ()))
VMEM = pl.BlockSpec(memory_space=pltpu.VMEM)
SMEM = pl.BlockSpec(memory_space=pltpu.SMEM)
ANY = pl.BlockSpec(memory_space=pl.ANY)
MIB = 2**20


def shape(dims, kind=full):
    return jax.ShapeDtypeStruct(dims, kind)


def dot(left, right, dims=NN):
    return lax.dot_general(left, right, dims, preferred_element_type=full)


def iota(dims, axis):
    return lax.broadcasted_iota(jnp.int32, dims, axis)


def hot(condition):
    return condition.astype(full).astype(half)


def call(kernel, ins, outs, scratch, flops, bytes_moved, limit):
    return pl.pallas_call(
        kernel,
        out_shape=[item[0] for item in outs],
        in_specs=ins,
        out_specs=[item[1] for item in outs],
        scratch_shapes=scratch,
        cost_estimate=pl.CostEstimate(flops=flops, bytes_accessed=bytes_moved, transcendentals=0),
        compiler_params=pltpu.CompilerParams(vmem_limit_bytes=limit * MIB),
    )


def gelu_pair(values):
    square = values * values
    bent = jnp.tanh(values * (gelu_one + gelu_three * square))
    gate = 0.5 + 0.5 * bent
    slope = gate + (0.5 * values) * (1.0 - bent * bent) * (gelu_one + (3.0 * gelu_three) * square)
    return (values * gate, slope)


def adamw(weight, gradient, first, second, step_rate):
    first_new = beta_one * first + (1.0 - beta_one) * gradient
    second_new = beta_two * second + (1.0 - beta_two) * gradient * gradient
    first_hat = first_new / (1.0 - beta_one**STEP)
    second_hat = second_new / (1.0 - beta_two**STEP)
    weight_new = weight - step_rate * (
        first_hat / (jnp.sqrt(second_hat) + adam_eps) + weight_decay * weight
    )
    return (first_new, second_new, weight_new)


def lane_pixel(lanes):
    tap = lanes // 64
    cell = lanes % 64
    row = 4 * (cell // 8) + tap // 3 - 1
    col = 4 * (cell % 8) + tap % 3 - 1
    return (tap, row, col)


def image_kernel(planes, numbers, out):
    tap, row, col = lane_pixel(iota((1, PLANE), 1))
    pixel = jnp.where((row >= 0) & (col >= 0) & (tap < 9), row * SIDE + col, -1)
    pick = hot(iota((SIDE * SIDE, PLANE), 0) == pixel)
    lanes = iota((1, PLANE), 1)
    for colour in range(3):
        taken = dot(planes[colour], pick)
        if colour == 0:
            for item in range(5):
                value = numbers[:, item : item + 1].astype(full)
                taken = jnp.where(lanes == META + item, value, taken)
        out[:, colour * PLANE : (colour + 1) * PLANE] = taken.astype(half)


def pack_kernel(proj_c, head, norm, out):
    width = proj_c.shape[1]
    place = hot(iota((C2, WIDE), 0) == iota((C2, WIDE), 1))
    total = dot(proj_c[...].astype(half), place, TN)
    classes = head.shape[1]
    place = hot(iota((classes, WIDE), 0) + C2 == iota((classes, WIDE), 1))
    total = total + dot(head[...].astype(half), place)
    rest = norm[...]
    for part in range(3):
        piece = rest.astype(half)
        rest = rest - piece.astype(full)
        place = hot(iota((6, WIDE), 0) + (C2 + 16 + 8 * part) == iota((6, WIDE), 1))
        total = total + dot(piece, place, TN)
    out[...] = total.astype(half)


def cast_kernel(ids, weights, out):
    out[...] = weights[0].astype(half)


def cast_half(ids, conv_w, layer):
    rows = conv_w.shape[1] // 2
    cols = conv_w.shape[2]
    wide = cols // 5
    return pl.pallas_call(
        cast_kernel,
        grid_spec=pltpu.PrefetchScalarGridSpec(
            num_scalar_prefetch=1,
            grid=(5,),
            in_specs=[pl.BlockSpec((1, rows, wide), lambda step, ids: (layer, ids[2], step))],
            out_specs=pl.BlockSpec((rows, wide), lambda step, ids: (0, step)),
        ),
        out_shape=shape((rows, cols), half),
        compiler_params=pltpu.CompilerParams(vmem_limit_bytes=16 * MIB),
        cost_estimate=pl.CostEstimate(
            flops=rows * cols, bytes_accessed=6 * rows * cols, transcendentals=0
        ),
    )(ids, conv_w)


def front_kernel(sizes, *refs):
    per, count, groups, devices, split = sizes
    rows = per * 64
    band = per * 8
    ids = refs[0]
    images = refs[1 : 1 + groups]
    packs = refs[1 + groups : 1 + groups + split]
    stem_w, proj_a, proj_b = refs[1 + groups + split : 4 + groups + split]
    (
        patches,
        stem_out,
        mid_one,
        mid_two,
        act_three,
        base,
        stats,
        norm_rows,
        head_all,
        proj_t,
        facts,
        gathered,
        tiles,
        loose,
        stem_pad,
        proj_b_pad,
        totals,
        sems,
    ) = refs[4 + groups + split :]
    quarter = gathered.shape[0] // split
    copies = []
    for turn in range(split):
        spot = pl.multiple_of((ids[0] ^ turn) * quarter, 16)
        copy = pltpu.make_async_copy(
            packs[turn], gathered.at[pl.ds(spot, quarter)], sems.at[turn]
        )
        copy.start()
        copies.append(copy)
    slot = iota((per, count), 0)
    column = iota((per, count), 1)
    own = dot(hot(column == slot + ids[0] * per), images[0][...])
    group_of = own[:, META + 3 : META + 4].astype(jnp.int32)
    local_of = own[:, META + 4 : META + 5].astype(jnp.int32)
    turn_of = group_of ^ ids[1]
    other = jnp.zeros((per, 3 * PLANE), full)
    for turn in range(groups):
        other = other + dot(hot((turn_of == turn) & (column == local_of)), images[turn][...])
    top = own[:, META + 1 : META + 2]
    left = own[:, META + 2 : META + 3]
    tap, row, col = lane_pixel(iota((1, 3 * PLANE), 1) % PLANE)
    row = row.astype(full)
    col = col.astype(full)
    inside = (row >= top) & (row < top + CUT) & (col >= left) & (col < left + CUT) & (tap < 9)
    blended = jnp.where(inside, other, own)
    tall = jnp.maximum(jnp.minimum(top + CUT, float(SIDE)) - jnp.maximum(top, 0.0), 0.0)
    broad = jnp.maximum(jnp.minimum(left + CUT, float(SIDE)) - jnp.maximum(left, 0.0), 0.0)
    share = 1.0 - tall * broad / float(SIDE * SIDE)
    lanes = iota((per, 128), 1)
    facts[...] = jnp.where(
        lanes == 0,
        own[:, META : META + 1],
        jnp.where(lanes == 1, other[:, META : META + 1], share),
    )
    tiles[...] = jnp.zeros(tiles.shape, full)
    for piece in range(15):
        tiles[:, piece, :] = blended[:, piece * 128 : (piece + 1) * 128]
    tiles[:, 16:32, :] = pltpu.roll(tiles[:, 0:16, :], 64, 2)
    spot = iota((32, 32), 0)
    tap_at = ((spot % 16) % 5) * 2 + spot // 16
    colour_at = (spot % 16) // 5
    order = hot(
        (iota((32, 32), 1) == tap_at * 3 + colour_at) & (tap_at < 9) & (spot % 16 < 15)
    )
    for image in range(per):
        cells = dot(tiles[image].astype(half), order, TN)
        for line in range(8):
            loose[line * band + image * 8 : line * band + image * 8 + 8, :] = cells[
                line * 8 : line * 8 + 8
            ]
    patches[...] = loose[...].astype(half)
    stem_pad[...] = jnp.zeros(stem_pad.shape, full)
    stem_pad[0:27, :] = stem_w[...]
    proj_b_pad[...] = jnp.zeros(proj_b_pad.shape, half)
    proj_b_pad[:, 0:C2] = proj_b[...].astype(half)
    for copy in copies:
        copy.wait()
    lanes = iota((1, WIDE), 1)
    packed = gathered[...]
    proj_t[...] = jnp.where(lanes < C2, packed.astype(full), 0.0).astype(half)
    place = hot(iota((WIDE, 16), 0) == iota((WIDE, 16), 1) + C2)
    head_all[...] = dot(packed, place).astype(half)
    column = iota((8, WIDE), 1)
    name = iota((8, WIDE), 0)
    pieces = [
        dot(hot((column == name + (C2 + 16 + 8 * part)) & (name < 6)), packed, NT)
        for part in range(3)
    ]
    norm_rows[...] = pieces[0] + (pieces[1] + pieces[2])
    stem_half = stem_pad[...].astype(half)
    proj_a_half = proj_a[...].astype(half)
    totals[...] = jnp.zeros(totals.shape, full)
    tall_chunk = 2 * band

    def step(index, carry):
        at = pl.ds(pl.multiple_of(index * tall_chunk, 16), tall_chunk)
        stem = dot(patches[at], stem_half)
        stem_out[at] = stem
        one = dot(gelu_pair(stem)[0].astype(half), proj_a_half)
        mid_one[at] = one
        two = dot(gelu_pair(one)[0].astype(half), proj_b_pad[...])
        mid_two[at] = two
        three = gelu_pair(two)[0].astype(half)
        act_three[at] = three
        result = dot(three, proj_t[...], NT)
        base[at] = result
        totals[0:1] += jnp.sum(result, axis=0, keepdims=True)
        totals[1:2] += jnp.sum(result * result, axis=0, keepdims=True)
        return carry

    lax.fori_loop(0, rows // tall_chunk, step, 0)
    spread_stats(stats, [totals[0:1], totals[1:2]])


def spread_stats(out, parts):
    line = jnp.concatenate(parts, axis=1)
    out[...] = jnp.broadcast_to(line[None], out.shape)


def moments(stats, row_total):
    line = jnp.sum(stats[...], axis=0)
    mean = line[:, 0:C3] / row_total
    rstd = lax.rsqrt(line[:, C3 : 2 * C3] / row_total - mean * mean + norm_eps)
    return (mean, rstd)


def start_weights(ids, pieces, weights, sems):
    count = len(pieces) // 2
    rows = pieces[0].shape[0]
    copies = []
    for turn in range(count):
        for side in range(2):
            spot = pl.multiple_of(
                (ids[0] ^ turn) * (2 * rows) + (ids[2] ^ side) * rows, 16
            )
            copy = pltpu.make_async_copy(
                pieces[2 * turn + side],
                weights.at[pl.ds(spot, rows)],
                sems.at[2 * turn + side],
            )
            copy.start()
            copies.append(copy)
    return copies


def shifted(values, by):
    block = values.reshape(CHUNK // 8, 8, C3)
    place = iota((1, 8, 1), 1)
    if by == 1:
        moved = jnp.where(place == 0, 0.0, pltpu.roll(block, 1, 1))
    else:
        moved = jnp.where(place == 7, 0.0, pltpu.roll(block, 7, 1))
    return moved.reshape(CHUNK, C3)


def conv_kernel(sizes, layer, *refs):
    per, row_total, split = sizes
    rows = per * 64
    band = per * 8
    ids, source, stats_in, norm_rows = refs[0:4]
    offset = 4
    if layer == 1:
        base = refs[4]
        offset = 5
    pieces = refs[offset : offset + 2 * split]
    (result, field_out, slope_out, stats, weights, field, slope, sems, out_sems) = refs[
        offset + 2 * split :
    ]
    copies = start_weights(ids, pieces, weights, sems)
    mean, rstd = moments(stats_in, row_total)
    factor = rstd * norm_rows[2 * layer : 2 * layer + 1]
    shift = norm_rows[2 * layer + 1 : 2 * layer + 2] - mean * factor

    def prepare(index, carry):
        at = pl.ds(pl.multiple_of(index * CHUNK, 16), CHUNK)
        value, gradient = gelu_pair(source[at] * factor + shift)
        slope[at] = gradient
        field[at, 0:C3] = shifted(value, 1).astype(half)
        field[at, C3 : 2 * C3] = value.astype(half)
        field[at, 2 * C3 : TRIPLE] = shifted(value, -1).astype(half)
        return carry

    lax.fori_loop(0, rows // CHUNK, prepare, 0)
    keep_field = pltpu.make_async_copy(field, field_out, out_sems.at[0])
    keep_field.start()
    keep_slope = pltpu.make_async_copy(slope, slope_out, out_sems.at[1])
    keep_slope.start()
    for copy in copies:
        copy.wait()
    inner = rows - band
    result[...] = dot(field[...], weights[:, TRIPLE : 2 * TRIPLE], NT)
    result[band:rows] += dot(field[0:inner], weights[:, 0:TRIPLE], NT)
    result[0:inner] += dot(field[band:rows], weights[:, 2 * TRIPLE : 3 * TRIPLE], NT)

    def count(index, carry):
        at = pl.ds(pl.multiple_of(index * CHUNK, 16), CHUNK)
        value = result[at]
        if layer == 1:
            value = value + base[at]
            result[at] = value
        return (
            carry[0] + jnp.sum(value.reshape(CHUNK // 8, 8, C3), axis=0),
            carry[1] + jnp.sum((value * value).reshape(CHUNK // 8, 8, C3), axis=0),
        )

    zero = jnp.zeros((8, C3), full)
    sums = lax.fori_loop(0, rows // CHUNK, count, (zero, zero))
    spread_stats(stats, [jnp.sum(item, axis=0, keepdims=True) for item in sums])
    keep_field.wait()
    keep_slope.wait()


def head_kernel(sizes, *refs):
    per, row_total, image_total, classes = sizes
    rows = per * 64
    band = per * 8
    (
        summed,
        stats_in,
        norm_rows,
        head_all,
        facts,
        slope,
        spread,
        stats,
        grad_head,
        sum_value,
        sum_slope,
        sum_cross,
    ) = refs
    mean, rstd = moments(stats_in, row_total)
    gain = norm_rows[4:5]
    bias = norm_rows[5:6]
    sum_value[...] = jnp.zeros((band, C3), full)
    sum_slope[...] = jnp.zeros((band, C3), full)
    sum_cross[...] = jnp.zeros((band, C3), full)

    def walk(index, carry):
        for part in range(band // CHUNK):
            at = pl.ds(pl.multiple_of(index * band + part * CHUNK, 16), CHUNK)
            here = slice(part * CHUNK, part * CHUNK + CHUNK)
            unit = (summed[at] - mean) * rstd
            value, gradient = gelu_pair(unit * gain + bias)
            slope[at] = gradient
            sum_value[here] += value
            sum_slope[here] += gradient
            sum_cross[here] += gradient * unit
        return carry

    lax.fori_loop(0, 8, walk, 0)

    def by_image(ref):
        return jnp.sum(ref[...].reshape(per, 8, C3), axis=1)

    pooled = (by_image(sum_value) / 64.0).astype(half)
    logits = dot(pooled, head_all[...])
    lanes = iota((per, 16), 1)
    inside = lanes < classes
    own = facts[:, 0:1].astype(jnp.int32)
    other = facts[:, 1:2].astype(jnp.int32)
    share = facts[:, 2:3]
    target = jnp.where(lanes == own, share, 0.0) + jnp.where(lanes == other, 1.0 - share, 0.0)
    top = jnp.max(jnp.where(inside, logits, -3e38), axis=1, keepdims=True)
    powers = jnp.where(inside, jnp.exp(jnp.where(inside, logits - top, 0.0)), 0.0)
    lse = top + jnp.log(jnp.sum(powers, axis=1, keepdims=True))
    losses = lse - jnp.sum(target * logits, axis=1, keepdims=True)
    loss = jnp.sum(losses, axis=0, keepdims=True)
    soft = jnp.where(inside, jnp.exp(jnp.where(inside, logits - lse, 0.0)), 0.0)
    grad_logits = ((soft - target) / image_total).astype(half)
    grad_head[...] = dot(pooled, grad_logits, TN)
    pull = dot(grad_logits, head_all[...], NT) / 64.0
    spread[...] = jnp.broadcast_to(pull[:, None, :], (per, 8, C3)).reshape(band, C3)
    bias_sum = jnp.sum(pull * by_image(sum_slope), axis=0, keepdims=True)
    gain_sum = jnp.sum(pull * by_image(sum_cross), axis=0, keepdims=True)
    spread_stats(stats, [bias_sum, gain_sum, jnp.broadcast_to(loss, (1, 128))])


def grad_moments(stats, row_total):
    line = jnp.sum(stats[...], axis=0)
    return (line[:, 0:C3] / row_total, line[:, C3 : 2 * C3] / row_total)


def input_grad(gradient, weights, out, band):
    rows = gradient.shape[0]
    inner = rows - band
    spans = (
        (1, slice(0, rows), slice(0, rows)),
        (0, slice(0, inner), slice(band, rows)),
        (2, slice(band, rows), slice(0, inner)),
    )
    for line, to, of in spans:
        for col in range(3):
            tap = 3 * line + col
            part = dot(
                gradient[of, col * C3 : (col + 1) * C3], weights[:, tap * C3 : (tap + 1) * C3]
            )
            if line == 1 and col == 0:
                out[to] = part
            else:
                out[to] += part


def close_input_grad(out, slope, source, mean, rstd, stats, rows):
    def finish(index, carry):
        at = pl.ds(pl.multiple_of(index * CHUNK, 16), CHUNK)
        value = out[at] * slope[at]
        out[at] = value
        unit = (source[at] - mean) * rstd
        return (
            carry[0] + jnp.sum(value.reshape(CHUNK // 8, 8, C3), axis=0),
            carry[1] + jnp.sum((value * unit).reshape(CHUNK // 8, 8, C3), axis=0),
        )

    zero = jnp.zeros((8, C3), full)
    sums = lax.fori_loop(0, rows // CHUNK, finish, (zero, zero))
    spread_stats(stats, [jnp.sum(item, axis=0, keepdims=True) for item in sums])


def put_shifted(gradient, at, value):
    gradient[at, 0:C3] = shifted(value, -1).astype(half)
    gradient[at, C3 : 2 * C3] = value.astype(half)
    gradient[at, 2 * C3 : TRIPLE] = shifted(value, 1).astype(half)


def back_two_kernel(sizes, *refs):
    per, row_total, split = sizes
    rows = per * 64
    band = per * 8
    (
        ids,
        summed,
        slope_three,
        spread,
        stats_three,
        stats_four,
        norm_rows,
        conv_one,
        slope_two,
        stats_two,
    ) = refs[0:10]
    pieces = refs[10 : 10 + 2 * split]
    (result, grad_summed, grad_half, stats, weights, gradient, sems) = refs[10 + 2 * split :]
    copies = start_weights(ids, pieces, weights, sems)
    mean, rstd = moments(stats_three, row_total)
    low, high = grad_moments(stats_four, row_total)
    factor = rstd * norm_rows[4:5]

    def prepare(index, carry):
        for part in range(band // CHUNK):
            at = pl.ds(pl.multiple_of(index * band + part * CHUNK, 16), CHUNK)
            here = slice(part * CHUNK, part * CHUNK + CHUNK)
            unit = (summed[at] - mean) * rstd
            value = factor * (slope_three[at] * spread[here] - low - unit * high)
            grad_summed[at] = value
            grad_half[at] = value.astype(half)
            put_shifted(gradient, at, value)
        return carry

    lax.fori_loop(0, 8, prepare, 0)
    for copy in copies:
        copy.wait()
    input_grad(gradient, weights, result, band)
    mean, rstd = moments(stats_two, row_total)
    close_input_grad(result, slope_two, conv_one, mean, rstd, stats, rows)


def norm_back_kernel(sizes, *refs):
    row_total = sizes
    (incoming, source, stats_two, stats_five, norm_rows, grad_half) = refs
    rows = incoming.shape[0]
    mean, rstd = moments(stats_two, row_total)
    low, high = grad_moments(stats_five, row_total)
    factor = rstd * norm_rows[2:3]

    def prepare(index, carry):
        at = pl.ds(pl.multiple_of(index * CHUNK, 16), CHUNK)
        unit = (source[at] - mean) * rstd
        grad_half[at] = (factor * (incoming[at] - low - unit * high)).astype(half)
        return carry

    lax.fori_loop(0, rows // CHUNK, prepare, 0)


def back_one_kernel(sizes, *refs):
    per, row_total, split = sizes
    rows = per * 64
    band = per * 8
    (ids, grad_half, base, slope_one, stats_one) = refs[0:5]
    pieces = refs[5 : 5 + 2 * split]
    (result, stats, weights, gradient, sems) = refs[5 + 2 * split :]
    copies = start_weights(ids, pieces, weights, sems)

    def prepare(index, carry):
        at = pl.ds(pl.multiple_of(index * CHUNK, 16), CHUNK)
        put_shifted(gradient, at, grad_half[at].astype(full))
        return carry

    lax.fori_loop(0, rows // CHUNK, prepare, 0)
    for copy in copies:
        copy.wait()
    input_grad(gradient, weights, result, band)
    mean, rstd = moments(stats_one, row_total)
    close_input_grad(result, slope_one, base, mean, rstd, stats, rows)


def weight_grad_kernel(sizes, *refs):
    lines, split, band, blocks = sizes
    (ids, grad_half, field, mine, other, held, sems) = refs
    rows = field.shape[0]
    inner = rows - band
    spans = {
        0: (slice(band, rows), slice(0, inner)),
        1: (slice(0, rows), slice(0, rows)),
        2: (slice(0, inner), slice(band, rows)),
    }
    used = 15 * len(lines)
    for spare in range(used, blocks):
        held[spare] = jnp.zeros(held.shape[1:], half)
    for place, line in enumerate(lines):
        left, right = spans[line]
        part = dot(grad_half[left], field[right], TN).astype(half)
        for block in range(15):
            held[place * 15 + block] = part[:, block * 128 : (block + 1) * 128]
    tall = mine.shape[2]
    copies = []
    for turn in range(split):
        for side, target in ((0, mine), (1, other)):
            spot = pl.multiple_of(
                (ids[0] ^ turn) * (2 * tall) + (ids[2] ^ side) * tall, 16
            )
            copy = pltpu.make_async_copy(
                held.at[:, pl.ds(spot, tall), :], target.at[turn], sems.at[2 * turn + side]
            )
            copy.start()
            copies.append(copy)
    for copy in copies:
        copy.wait()


def trunk_kernel(sizes, *refs):
    per, row_total, split = sizes
    rows = per * 64
    band = per * 8
    (
        ids,
        incoming,
        grad_summed,
        base,
        stats_one,
        stats_six,
        norm_rows,
        proj_t,
        act_three,
        mid_two,
        mid_one,
        stem_out,
        patches,
        proj_a,
        proj_b,
        grad_head,
        mine,
        other,
        trunk,
        grad_two,
        act_two,
        grad_one,
        act_one,
        grad_stem,
        proj_b_pad,
        split_part,
        shared_part,
        sems,
    ) = refs
    mean, rstd = moments(stats_one, row_total)
    low, high = grad_moments(stats_six, row_total)
    factor = rstd * norm_rows[0:1]
    proj_b_pad[...] = jnp.zeros(proj_b_pad.shape, half)
    proj_b_pad[:, 0:C2] = proj_b[...].astype(half)
    proj_a_half = proj_a[...].astype(half)

    def prepare(index, carry):
        at = pl.ds(pl.multiple_of(index * CHUNK, 16), CHUNK)
        unit = (base[at] - mean) * rstd
        value = grad_summed[at] + factor * (incoming[at] - low - unit * high)
        trunk[at] = value.astype(half)
        return carry

    lax.fori_loop(0, rows // CHUNK, prepare, 0)
    tall_chunk = 2 * band

    def step(index, carry):
        at = pl.ds(pl.multiple_of(index * tall_chunk, 16), tall_chunk)
        three = dot(trunk[at], proj_t[...])
        two = (three * gelu_pair(mid_two[at])[1]).astype(half)
        grad_two[at] = two
        value, slope = gelu_pair(mid_one[at])
        act_two[at] = value.astype(half)
        one = (dot(two, proj_b_pad[...], NT) * slope).astype(half)
        grad_one[at] = one
        value, slope = gelu_pair(stem_out[at])
        act_one[at] = value.astype(half)
        grad_stem[at] = (dot(one, proj_a_half, NT) * slope).astype(half)
        return carry

    lax.fori_loop(0, rows // tall_chunk, step, 0)
    place = hot(iota((16, WIDE), 0) + C2 == iota((16, WIDE), 1))
    split_part[...] = (
        dot(trunk[...], act_three[...], TN) + dot(grad_head[...].astype(half), place)
    ).astype(half)
    shared = dot(act_two[...], grad_two[...], TN)
    shared = shared + dot(dot(grad_one[...], act_one[...], TN).astype(half), place)
    stem = dot(patches[...], grad_stem[...], TN).astype(half)
    tall = split_part.shape[0] // (2 * split)
    spot = iota((C1, 32), 0)
    twice = hot((spot % tall == iota((C1, 32), 1)) & (spot % tall < 27))
    place = hot(iota((16, WIDE), 0) + (C2 + 16) == iota((16, WIDE), 1))
    shared = shared + dot(dot(twice, stem).astype(half), place)
    shared_part[...] = shared.astype(half)
    copies = []
    for turn in range(split):
        for side, target in ((0, mine), (1, other)):
            place = pl.multiple_of((ids[2] ^ side) * tall, 16)
            spot = pl.multiple_of((ids[0] ^ turn) * (2 * tall) + (ids[2] ^ side) * tall, 16)
            number = 2 * (2 * turn + side)
            copy = pltpu.make_async_copy(
                split_part.at[pl.ds(spot, tall)], target.at[turn, 0:tall], sems.at[number]
            )
            copy.start()
            copies.append(copy)
            copy = pltpu.make_async_copy(
                shared_part.at[pl.ds(place, tall)],
                target.at[turn, tall : 2 * tall],
                sems.at[number + 1],
            )
            copy.start()
            copies.append(copy)
    for copy in copies:
        copy.wait()


def clip_scale(squares):
    total = jnp.sum(jnp.sum(squares[...], axis=0), axis=1, keepdims=True)
    size = jnp.sqrt(total[:, 0:1] / 128.0)
    return (size, jnp.minimum(1.0, clip_limit / size))


def conv_update_kernel(sizes, *refs):
    pieces_count, places, blocks, step_rate = sizes
    ids = refs[0]
    squares, weight, first, second = refs[1:5]
    pieces = refs[5 : 5 + pieces_count]
    (first_new, second_new, weight_new, held, sems) = refs[5 + pieces_count :]
    layer = pl.program_id(0)
    line = pl.program_id(1)

    def copies():
        made = []
        for number, (owner, start, per_piece, turn, side) in enumerate(places):
            tall = pieces[number].shape[1]
            spot = start + (ids[3] ^ turn) * per_piece
            row = pl.multiple_of((ids[2] ^ side) * tall, 16)
            made.append(
                pltpu.make_async_copy(
                    pieces[number],
                    held.at[owner, pl.ds(spot, per_piece), pl.ds(row, tall), :],
                    sems.at[number],
                )
            )
        return made

    @pl.when((layer == 0) & (line == 0))
    def _():
        made = copies()
        for copy in made:
            copy.start()
        for copy in made:
            copy.wait()

    size, scale = clip_scale(squares)
    for part in range(5):
        lanes = slice(part * 128, part * 128 + 128)
        block = line * 5 + part + line // 3 * (blocks - 15)
        gradient = held[layer, block].astype(full) * scale
        results = adamw(
            weight[0, :, lanes], gradient, first[0, :, lanes], second[0, :, lanes], step_rate
        )
        first_new[0, :, lanes] = results[0]
        second_new[0, :, lanes] = results[1]
        weight_new[0, :, lanes] = results[2]


def small_update_kernel(rates, *refs):
    ids, squares, mine, other, grad_norm_p = refs[0:5]
    states = refs[5:23]
    outs = refs[23:41]
    size_out = refs[41]
    size, scale = clip_scale(squares)
    size_out[...] = jnp.broadcast_to(size, size_out.shape)
    first_core = ids[2] == 0
    tall = mine.shape[0] // 2
    here = mine[...].astype(full)
    there = other[...].astype(full)
    even = jnp.where(first_core, here, there)
    odd = jnp.where(first_core, there, here)
    split_part = jnp.concatenate([even[0:tall], odd[0:tall]], axis=0).astype(half)
    shared = jnp.concatenate([even[tall:], odd[tall:]], axis=0).astype(half)
    eye = hot(iota((2 * tall, 2 * tall), 0) == iota((2 * tall, 2 * tall), 1))
    grad_c = dot(split_part, eye, TN)[0:C2]
    classes = states[12].shape[1]
    pick = hot(iota((WIDE, classes), 0) == iota((WIDE, classes), 1) + C2)
    grad_head = dot(split_part, pick)
    grad_b = shared[:, 0:C2].astype(full)
    pick = hot(iota((C0, WIDE), 0) + C2 == iota((C0, WIDE), 1))
    grad_a = dot(pick, shared, NT)
    pick = hot(iota((WIDE, C0), 0) == iota((WIDE, C0), 1) + (C2 + 16))
    grad_stem = dot(shared[0:32], pick)[0:27]
    gradients = (grad_stem, grad_a, grad_b, grad_c, grad_head, grad_norm_p[...])
    for index in range(6):
        weight, first, second = states[3 * index : 3 * index + 3]
        results = adamw(
            weight[...], gradients[index] * scale, first[...], second[...], rates[index]
        )
        for item in range(3):
            outs[3 * index + item][...] = results[item]


def xor_pairs(size, turn):
    return [(index, index ^ turn) for index in range(size)]


def shards(
    images,
    labels,
    corners,
    partners,
    stem_w,
    stem_w_m,
    stem_w_v,
    proj_a,
    proj_a_m,
    proj_a_v,
    proj_b,
    proj_b_m,
    proj_b_v,
    proj_c,
    proj_c_m,
    proj_c_v,
    conv_w,
    conv_w_m,
    conv_w_v,
    head_w,
    head_w_m,
    head_w_v,
    norm_p,
    norm_p_m,
    norm_p_v,
):
    split = lax.axis_size("dp")
    groups = lax.axis_size("filt")
    chips = groups // 2
    devices = split * groups
    count = images.shape[0]
    per = count // split
    rows = per * 64
    band = per * 8
    image_total = float(count * groups)
    row_total = image_total * 64.0
    tall = conv_w.shape[1] // 2
    spot_d = lax.axis_index("dp")
    spot_f = lax.axis_index("filt")
    ids = jnp.stack([spot_d, spot_f, spot_f % 2, spot_f // 2]).astype(jnp.int32)

    def over_dp(value, turn):
        return lax.ppermute(value, "dp", xor_pairs(split, turn))

    def over_filt(value, turn):
        return lax.ppermute(value, "filt", xor_pairs(groups, turn))

    def exchange(stats):
        return lax.all_to_all(stats, ("dp", "filt"), 0, 0)

    numbers = jnp.stack(
        [labels, corners[:, 0], corners[:, 1], partners // count, partners % count], axis=1
    )
    (own_images,) = call(
        image_kernel,
        [VMEM, VMEM],
        [(shape((count, 3 * PLANE), half), VMEM)],
        [],
        2 * 3 * count * 1024 * PLANE,
        2**20,
        24,
    )(images.transpose(1, 0, 2), numbers)
    (own_pack,) = call(
        pack_kernel, [VMEM] * 3, [(shape((2 * tall, WIDE), half), VMEM)], [], 10**8, 2**19, 16
    )(proj_c, head_w, norm_p)
    packs = [own_pack] + [over_dp(own_pack, turn) for turn in range(1, split)]
    far_images = [own_images] + [over_filt(own_images, 2 * turn) for turn in range(1, chips)]
    all_images = []
    for piece in far_images:
        all_images += [piece, over_filt(piece, 1)]
    kernels = []
    for layer in range(2):
        own = cast_half(ids, conv_w, layer)
        pieces = []
        for turn in range(split):
            piece = own if turn == 0 else over_dp(own, turn)
            pieces += [piece, over_filt(piece, 1)]
        kernels.append(pieces)

    line = shape((devices, 1, 2 * C3))
    (
        patches,
        stem_out,
        mid_one,
        mid_two,
        act_three,
        base,
        stats,
        norm_rows,
        head_all,
        proj_t,
        facts,
    ) = call(
        functools.partial(front_kernel, (per, count, groups, devices, split)),
        [SMEM] + [VMEM] * groups + [ANY] * split + [VMEM] * 3,
        [
            (shape((rows, 32), half), VMEM),
            (shape((rows, C0)), VMEM),
            (shape((rows, C1)), VMEM),
            (shape((rows, WIDE)), VMEM),
            (shape((rows, WIDE), half), VMEM),
            (shape((rows, C3)), VMEM),
            (line, VMEM),
            (shape((8, C3)), VMEM),
            (shape((C3, 16), half), VMEM),
            (shape((C3, WIDE), half), VMEM),
            (shape((per, 128)), VMEM),
        ],
        [
            pltpu.VMEM((C3, WIDE), half),
            pltpu.VMEM((per, 32, 128), full),
            pltpu.VMEM((rows, 32), full),
            pltpu.VMEM((32, C0), full),
            pltpu.VMEM((C1, WIDE), half),
            pltpu.VMEM((8, C3), full),
            pltpu.SemaphoreType.DMA((split,)),
        ],
        2 * rows * (32 * 16 + 16 * 160 + 160 * 320 + 320 * 640) * 8,
        10**7,
        48,
    )(ids, *all_images, *packs, stem_w, proj_a, proj_b)
    stats_one = exchange(stats)

    conv_flops = 2 * rows * 9 * C3 * C3
    weight_scratch = [pltpu.VMEM((C3, 9 * C3), half)]
    conv_outs = [
        (shape((rows, C3)), VMEM),
        (shape((rows, TRIPLE), half), ANY),
        (shape((rows, C3)), ANY),
        (line, VMEM),
    ]
    conv_scratch = weight_scratch + [
        pltpu.VMEM((rows, TRIPLE), half),
        pltpu.VMEM((rows, C3), full),
        pltpu.SemaphoreType.DMA((2 * split,)),
        pltpu.SemaphoreType.DMA((2,)),
    ]
    conv_one, field_one, slope_one, stats = call(
        functools.partial(conv_kernel, (per, row_total, split), 0),
        [SMEM] + [VMEM] * 3 + [ANY] * (2 * split),
        conv_outs,
        conv_scratch,
        conv_flops,
        2 * 10**7,
        48,
    )(ids, base, stats_one, norm_rows, *kernels[0])
    stats_two = exchange(stats)
    summed, field_two, slope_two, stats = call(
        functools.partial(conv_kernel, (per, row_total, split), 1),
        [SMEM] + [VMEM] * 4 + [ANY] * (2 * split),
        conv_outs,
        conv_scratch,
        conv_flops,
        2 * 10**7,
        48,
    )(ids, conv_one, stats_two, norm_rows, base, *kernels[1])
    stats_three = exchange(stats)
    slope_three, spread, stats, grad_head = call(
        functools.partial(head_kernel, (per, row_total, image_total, head_w.shape[1])),
        [VMEM] * 5,
        [
            (shape((rows, C3)), VMEM),
            (shape((band, C3)), VMEM),
            (shape((devices, 1, 2 * C3 + 128)), VMEM),
            (shape((C3, 16)), VMEM),
        ],
        [pltpu.VMEM((band, C3), full)] * 3,
        20 * rows * C3,
        8 * 10**6,
        32,
    )(summed, stats_three, norm_rows, head_all, facts)
    stats_four = exchange(stats)
    loss = jnp.sum(stats_four[:, 0, 2 * C3])

    back_scratch = weight_scratch + [
        pltpu.VMEM((rows, TRIPLE), half),
        pltpu.SemaphoreType.DMA((2 * split,)),
    ]
    grad_conv_one, grad_summed, grad_two_half, stats = call(
        functools.partial(back_two_kernel, (per, row_total, split)),
        [SMEM] + [VMEM] * 9 + [ANY] * (2 * split),
        [
            (shape((rows, C3)), VMEM),
            (shape((rows, C3)), VMEM),
            (shape((rows, C3), half), VMEM),
            (line, VMEM),
        ],
        back_scratch,
        conv_flops,
        2 * 10**7,
        52,
    )(
        ids,
        summed,
        slope_three,
        spread,
        stats_three,
        stats_four,
        norm_rows,
        conv_one,
        slope_two,
        stats_two,
        *kernels[1],
    )
    stats_five = exchange(stats)

    def weight_grad(grad_half, field, lines):
        blocks = -(-15 * len(lines) // chips) * chips
        piece = shape((split, blocks, tall, 128), half)
        return call(
            functools.partial(weight_grad_kernel, (lines, split, band, blocks)),
            [SMEM, VMEM, VMEM],
            [(piece, ANY), (piece, ANY)],
            [pltpu.VMEM((blocks, C3, 128), half), pltpu.SemaphoreType.DMA((2 * split,))],
            conv_flops * len(lines) // 3,
            10**7 * len(lines) // 3,
            40,
        )(ids, grad_half, field)

    def add(values):
        return sum(value.astype(full) for value in values).astype(half)

    def reduce_grad(mine, other):
        crossed = over_filt(other, 1)
        pair = [add([mine[turn], crossed[turn]]) for turn in range(split)]
        parts = [pair[0]] + [over_dp(pair[turn], turn) for turn in range(1, split)]
        wide = pair[0].shape[0] // chips
        pieces = []
        for turn in range(chips):
            start = (ids[3] ^ turn) * wide
            pieces.append(
                add([lax.dynamic_slice_in_dim(part, start, wide, axis=0) for part in parts])
            )
        return add(
            [pieces[0]] + [over_filt(pieces[turn], 2 * turn) for turn in range(1, chips)]
        )

    def share_grad(mine):
        pieces = []
        for turn in range(chips):
            piece = mine if turn == 0 else over_filt(mine, 2 * turn)
            pieces += [piece, over_filt(piece, 1)]
        return pieces

    def square_sum(value):
        wide = value.astype(full)
        return jnp.sum(wide * wide)

    mine, other = weight_grad(grad_two_half, field_two, (0, 1, 2))
    reduced_two = reduce_grad(mine, other)

    (grad_one_half,) = call(
        functools.partial(norm_back_kernel, row_total),
        [VMEM] * 5,
        [(shape((rows, C3), half), VMEM)],
        [],
        8 * rows * C3,
        8 * 10**6,
        24,
    )(grad_conv_one, conv_one, stats_two, stats_five, norm_rows)
    mine, other = weight_grad(grad_one_half, field_one, (0, 1, 2))
    reduced_one = reduce_grad(mine, other)
    grad_base, stats = call(
        functools.partial(back_one_kernel, (per, row_total, split)),
        [SMEM] + [VMEM] * 4 + [ANY] * (2 * split),
        [(shape((rows, C3)), VMEM), (line, VMEM)],
        back_scratch,
        conv_flops,
        2 * 10**7,
        48,
    )(ids, grad_one_half, base, slope_one, stats_one, *kernels[0])
    stats_six = exchange(stats)
    small = shape((split, 2 * tall, WIDE), half)
    small_mine, small_other = call(
        functools.partial(trunk_kernel, (per, row_total, split)),
        [SMEM] + [VMEM] * 15,
        [(small, ANY), (small, ANY)],
        [
            pltpu.VMEM((rows, C3), half),
            pltpu.VMEM((rows, WIDE), half),
            pltpu.VMEM((rows, C1), half),
            pltpu.VMEM((rows, C1), half),
            pltpu.VMEM((rows, C0), half),
            pltpu.VMEM((rows, C0), half),
            pltpu.VMEM((C1, WIDE), half),
            pltpu.VMEM((C3, WIDE), half),
            pltpu.VMEM((C1, WIDE), half),
            pltpu.SemaphoreType.DMA((4 * split,)),
        ],
        4 * rows * 320 * 640,
        2 * 10**7,
        48,
    )(
        ids,
        grad_base,
        grad_summed,
        base,
        stats_one,
        stats_six,
        norm_rows,
        proj_t,
        act_three,
        mid_two,
        mid_one,
        stem_out,
        patches,
        proj_a,
        proj_b,
        grad_head,
    )
    crossed = over_filt(small_other, 1)
    pair = [add([small_mine[turn], crossed[turn]]) for turn in range(split)]
    small_sum = add([pair[0]] + [over_dp(pair[turn], turn) for turn in range(1, split)])
    small_sum = add(
        [small_sum] + [over_filt(small_sum, 2 * turn) for turn in range(1, chips)]
    )
    small_far = over_filt(small_sum, 1)

    norm_sums = []
    for stats in (stats_six, stats_five, stats_four):
        sums = jnp.sum(stats[:, 0, :], axis=0)
        norm_sums += [sums[C3 : 2 * C3], sums[0:C3]]
    grad_norm_all = jnp.stack(norm_sums)
    grad_norm_p = lax.dynamic_slice_in_dim(grad_norm_all, spot_d * 2 * tall, 2 * tall, axis=1)
    squares = (
        square_sum(reduced_one)
        + square_sum(reduced_two)
        + square_sum(small_sum[0:tall, 0 : C2 + 16]) / chips
        + square_sum(small_sum[tall:, 0 : C2 + 16]) / (chips * split)
        + square_sum(small_sum[tall:, C2 + 16 :]) / (2 * chips * split)
        + jnp.sum(grad_norm_all * grad_norm_all) / devices
    )
    squares = exchange(jnp.broadcast_to(squares, (devices, 1, 128)))

    pieces = share_grad(reduced_one) + share_grad(reduced_two)
    wide = reduced_one.shape[0]
    places = [
        (owner, 0, wide, turn, side) for owner in range(2) for turn in range(chips) for side in range(2)
    ]
    whole_spec = pl.BlockSpec((1, 2 * tall, C3), lambda layer, line: (layer, 0, line))
    conv_shape = shape(conv_w.shape)
    conv_new = pl.pallas_call(
        functools.partial(
            conv_update_kernel, (len(pieces), places, 15, 0.7 / math.sqrt(9.0 * C3))
        ),
        grid=(2, 9),
        in_specs=[SMEM, VMEM, whole_spec, whole_spec, whole_spec] + [ANY] * len(pieces),
        out_specs=[whole_spec] * 3,
        out_shape=[conv_shape] * 3,
        scratch_shapes=[
            pltpu.VMEM((2, wide * chips, 2 * tall, 128), half),
            pltpu.SemaphoreType.DMA((len(pieces),)),
        ],
        compiler_params=pltpu.CompilerParams(vmem_limit_bytes=40 * MIB),
        cost_estimate=pl.CostEstimate(
            flops=20 * conv_w.size, bytes_accessed=26 * conv_w.size, transcendentals=0
        ),
    )(ids, squares, conv_w, conv_w_m, conv_w_v, *pieces)
    states = (
        (stem_w, stem_w_m, stem_w_v),
        (proj_a, proj_a_m, proj_a_v),
        (proj_b, proj_b_m, proj_b_v),
        (proj_c, proj_c_m, proj_c_v),
        (head_w, head_w_m, head_w_v),
        (norm_p, norm_p_m, norm_p_v),
    )
    rates = (
        0.7 / math.sqrt(27.0),
        0.7 / math.sqrt(C0),
        0.7 / math.sqrt(C1),
        0.7 / math.sqrt(C2),
        0.7 / math.sqrt(C3 / 8.0),
        0.8,
    )
    flat = [item for group in states for item in group]
    small_new = call(
        functools.partial(small_update_kernel, rates),
        [SMEM] + [VMEM] * 22,
        [(shape(item.shape), VMEM) for item in flat] + [(shape((1, 128)), VMEM)],
        [],
        10**7,
        4 * 10**6,
        32,
    )(ids, squares, small_sum, small_far, grad_norm_p, *flat)
    size = small_new[18][0, 0]
    return (
        *small_new[0:12],
        *conv_new,
        *small_new[12:18],
        loss,
        size,
    )


def solution(mesh):
    placed = (
        P("filt", None, None),
        P("filt"),
        P("filt", None),
        P("filt"),
        *([P()] * 9),
        *([P(None, "dp")] * 3),
        *([P(None, "dp", None)] * 3),
        *([P("dp", None)] * 3),
        *([P(None, "dp")] * 3),
    )
    return jax.shard_map(
        shards,
        mesh=mesh,
        in_specs=placed,
        out_specs=(
            *([P()] * 9),
            *([P(None, "dp")] * 3),
            *([P(None, "dp", None)] * 3),
            *([P("dp", None)] * 3),
            *([P(None, "dp")] * 3),
            P(),
            P(),
        ),
        check_vma=False,
    )
```

```python
import functools
import math

import jax
import jax.numpy as jnp
from jax import lax
from jax.experimental import pallas as pl
from jax.experimental.pallas import tpu as pltpu
from jax.sharding import PartitionSpec as P

C0 = 16
C1 = 160
C2 = 320
C3 = 640
WIDE = 384
TRIPLE = 3 * C3
SIDE = 32
CUT = 16
STEP = 10
PLANE = 640
META = 576
CHUNK = 48
QUARTERS = 4

beta_one = 0.9
beta_two = 0.999
adam_eps = 1e-08
weight_decay = 0.0005
clip_limit = 0.05
norm_eps = 1e-05
gelu_one = math.sqrt(2.0 / math.pi)
gelu_three = 0.044715 * gelu_one

half = jnp.bfloat16
full = jnp.float32
NT = (((1,), (1,)), ((), ()))
NN = (((1,), (0,)), ((), ()))
TN = (((0,), (0,)), ((), ()))
VMEM = pl.BlockSpec(memory_space=pltpu.VMEM)
SMEM = pl.BlockSpec(memory_space=pltpu.SMEM)
ANY = pl.BlockSpec(memory_space=pl.ANY)
MIB = 2**20


def shape(dims, kind=full):
    return jax.ShapeDtypeStruct(dims, kind)


def dot(left, right, dims=NN):
    return lax.dot_general(left, right, dims, preferred_element_type=full)


def iota(dims, axis):
    return lax.broadcasted_iota(jnp.int32, dims, axis)


def hot(condition):
    return condition.astype(full).astype(half)


def call(kernel, ins, outs, scratch, micros, after=0):
    used = len(ins)

    def body(*refs):
        kernel(*refs[:used], *refs[used + after :])

    return pl.pallas_call(
        body,
        out_shape=[item[0] for item in outs],
        in_specs=ins + [ANY] * after,
        out_specs=[item[1] for item in outs],
        scratch_shapes=scratch,
        cost_estimate=pl.CostEstimate(
            flops=int(micros * 35 * 10**7), bytes_accessed=1, transcendentals=0
        ),
        compiler_params=pltpu.CompilerParams(vmem_limit_bytes=60 * MIB),
    )


def gelu_pair(values):
    square = values * values
    bent = jnp.tanh(values * (gelu_one + gelu_three * square))
    gate = 0.5 + 0.5 * bent
    slope = gate + (0.5 * values) * (1.0 - bent * bent) * (gelu_one + (3.0 * gelu_three) * square)
    return (values * gate, slope)


def adamw(weight, gradient, first, second, step_rate):
    first_new = beta_one * first + (1.0 - beta_one) * gradient
    second_new = beta_two * second + (1.0 - beta_two) * (gradient * gradient)
    second_hat = second_new * (1.0 / (1.0 - beta_two**STEP))
    root = second_hat * lax.rsqrt(second_hat) + adam_eps
    weight_new = weight * (1.0 - step_rate * weight_decay) - (
        step_rate / (1.0 - beta_one**STEP)
    ) * (first_new / root)
    return (first_new, second_new, weight_new)


def fetch(source, target, sem):
    copy = pltpu.make_async_copy(source, target, sem)
    copy.start()
    return copy


def lane_pixel(lanes):
    tap = lanes // 64
    cell = lanes % 64
    row = 4 * (cell // 8) + tap // 3 - 1
    col = 4 * (cell % 8) + tap % 3 - 1
    return (tap, row, col)


def image_kernel(planes, labels, corners, partners, out, numbers):
    count = planes.shape[1]
    tap, row, col = lane_pixel(iota((1, PLANE), 1))
    pixel = jnp.where((row >= 0) & (col >= 0) & (tap < 9), row * SIDE + col, -1)
    pick = hot(iota((SIDE * SIDE, PLANE), 0) == pixel)
    numbers[...] = jnp.zeros(numbers.shape, full)
    numbers[0:1] = labels[...].astype(full)
    numbers[1:3] = corners[...].astype(full)
    numbers[3:4] = (partners[...] // count).astype(full)
    numbers[4:5] = (partners[...] % count).astype(full)
    place = hot(iota((8, PLANE), 0) + META == iota((8, PLANE), 1))
    for colour in range(3):
        taken = dot(planes[colour], pick)
        if colour == 0:
            taken = taken + dot(numbers[...].astype(half), place, TN)
        out[:, colour * PLANE : (colour + 1) * PLANE] = taken.astype(half)


def pack_kernel(proj_c, head, norm, out):
    place = hot(iota((C2, WIDE), 0) == iota((C2, WIDE), 1))
    total = dot(proj_c[...].astype(half), place)
    classes = head.shape[0]
    place = hot(iota((classes, WIDE), 0) + C2 == iota((classes, WIDE), 1))
    total = total + dot(head[...].astype(half), place, TN)
    rest = norm[...]
    for part in range(3):
        piece = rest.astype(half)
        rest = rest - piece.astype(full)
        place = hot(iota((6, WIDE), 0) + (C2 + 16 + 8 * part) == iota((6, WIDE), 1))
        total = total + dot(piece, place, TN)
    out[...] = total.astype(half)


def cast_kernel(layer, ids, weights, out, wide, narrow, in_sems, out_sems):
    rows = out.shape[0]
    parts = rows // 16
    inputs = []
    for part in range(parts):
        spot = pl.multiple_of(ids[2] * rows + part * 16, 16)
        inputs.append(
            fetch(
                weights.at[layer, pl.ds(spot, 16)],
                wide.at[part * 16 : part * 16 + 16],
                in_sems.at[part],
            )
        )
    outputs = []
    for part in range(parts):
        here = slice(part * 16, part * 16 + 16)
        inputs[part].wait()
        narrow[here] = wide[here].astype(half)
        outputs.append(fetch(narrow.at[here], out.at[here], out_sems.at[part]))
    for copy in outputs:
        copy.wait()


def cast_half(ids, conv_w, layer, after):
    rows = conv_w.shape[1] // 2
    cols = conv_w.shape[2]
    (result,) = call(
        functools.partial(cast_kernel, layer),
        [SMEM, ANY],
        [(shape((rows, cols), half), ANY)],
        [
            pltpu.VMEM((rows, cols), full),
            pltpu.VMEM((rows, cols), half),
            pltpu.SemaphoreType.DMA((rows // 16,)),
            pltpu.SemaphoreType.DMA((rows // 16,)),
        ],
        3,
        len(after),
    )(ids, conv_w, *after)
    return result


def merge_spans(plan):
    spans = []
    for out, (size, terms) in enumerate(plan):
        edges = {0, size}
        for _, _, start, length in terms:
            edges |= {start, start + length}
        edges = sorted(edges)
        for low, high in zip(edges[:-1], edges[1:]):
            used = [
                (source, first - start)
                for source, first, start, length in terms
                if start <= low and high <= start + length
            ]
            for begin in range(low, high, 8):
                spans.append((out, begin, min(8, high - begin), used))
    return spans


def merge_kernel(plan, count, *refs):
    values = refs[:count]
    results = refs[count : count + len(plan)]
    held = refs[count + len(plan) : 2 * count + len(plan)]
    kept = refs[2 * count + len(plan) : 2 * (count + len(plan))]
    in_sems, out_sems = refs[2 * (count + len(plan)) :]
    arrivals = []
    number = 0
    for _, begin, size, used in merge_spans(plan):
        copies = []
        for source, shift in used:
            here = slice(begin + shift, begin + shift + size)
            copies.append(
                fetch(values[source].at[here], held[source].at[here], in_sems.at[number])
            )
            number += 1
        arrivals.append(copies)
    departures = []
    for (out, begin, size, used), copies in zip(merge_spans(plan), arrivals):
        for copy in copies:
            copy.wait()
        total = None
        for source, shift in used:
            value = held[source][begin + shift : begin + shift + size].astype(full)
            total = value if total is None else total + value
        here = slice(begin, begin + size)
        kept[out][here] = total.astype(half)
        departures.append(
            fetch(kept[out].at[here], results[out].at[here], out_sems.at[len(departures)])
        )
    for copy in departures:
        copy.wait()


def merge(values, plan, after, micros):
    dims = values[0].shape[1:]
    spans = merge_spans(plan)
    return call(
        functools.partial(merge_kernel, plan, len(values)),
        [ANY] * len(values),
        [(shape((size,) + dims, half), ANY) for size, _ in plan],
        [pltpu.VMEM(value.shape, half) for value in values]
        + [pltpu.VMEM((size,) + dims, half) for size, _ in plan]
        + [
            pltpu.SemaphoreType.DMA((sum(len(used) for _, _, _, used in spans),)),
            pltpu.SemaphoreType.DMA((len(spans),)),
        ],
        micros,
        len(after),
    )(*values, *after)


def cut_kernel(places, *refs):
    count = len(places)
    outs = refs[count : 2 * count]
    sems = refs[2 * count]
    copies = []
    for index, (start, size) in enumerate(places):
        copies.append(
            fetch(refs[index].at[start : start + size], outs[index], sems.at[index])
        )
    for copy in copies:
        copy.wait()


def cut_rows(values, places, after):
    cols = values[0].shape[1]
    return call(
        functools.partial(cut_kernel, places),
        [ANY] * len(values),
        [(shape((size, cols), half), VMEM) for _, size in places],
        [pltpu.SemaphoreType.DMA((len(values),))],
        1,
        len(after),
    )(*values, *after)


def stack_kernel(places, *refs):
    count = len(places)
    out, sems = refs[count:]
    copies = []
    for index, (slot, start, size) in enumerate(places):
        copy = pltpu.make_async_copy(
            refs[index], out.at[slot, start : start + size], sems.at[index]
        )
        copy.start()
        copies.append(copy)
    for copy in copies:
        copy.wait()


def stack(pieces, places, dims, after):
    (result,) = call(
        functools.partial(stack_kernel, places),
        [ANY] * len(pieces),
        [(shape(dims, half), VMEM)],
        [pltpu.SemaphoreType.DMA((len(pieces),))],
        3,
        len(after),
    )(*pieces, *after)
    return result


def front_kernel(sizes, *refs):
    per, count, groups, devices, split = sizes
    rows = per * 64
    band = per * 8
    ids = refs[0]
    images, far_images = refs[1:3]
    packs = refs[3 : 3 + split]
    stem_w, proj_a, proj_b = refs[3 + split : 6 + split]
    (
        patches,
        stem_out,
        mid_one,
        mid_two,
        act_three,
        base,
        stats,
        norm_rows,
        head_all,
        proj_t,
        facts,
        gathered,
        tiles,
        loose,
        stem_pad,
        proj_b_pad,
        totals,
        sems,
    ) = refs[6 + split :]
    quarter = gathered.shape[0] // split
    copies = []
    for turn in range(split):
        spot = pl.multiple_of((ids[0] ^ turn) * quarter, 16)
        copies.append(fetch(packs[turn], gathered.at[pl.ds(spot, quarter)], sems.at[turn]))
    slot = iota((per, count), 0)
    column = iota((per, count), 1)
    own = dot(hot(column == slot + ids[0] * per), images[0])
    group_of = own[:, META + 3 : META + 4].astype(jnp.int32)
    local_of = own[:, META + 4 : META + 5].astype(jnp.int32)
    turn_of = group_of ^ ids[1]
    other = jnp.zeros((per, 3 * PLANE), full)
    for turn in range(groups):
        source = far_images[turn // 2] if turn % 2 else images[turn // 2]
        other = other + dot(hot((turn_of == turn) & (column == local_of)), source)
    top = own[:, META + 1 : META + 2]
    left = own[:, META + 2 : META + 3]
    tap, row, col = lane_pixel(iota((1, 3 * PLANE), 1) % PLANE)
    row = row.astype(full)
    col = col.astype(full)
    inside = (row >= top) & (row < top + CUT) & (col >= left) & (col < left + CUT) & (tap < 9)
    blended = jnp.where(inside, other, own)
    tall = jnp.maximum(jnp.minimum(top + CUT, float(SIDE)) - jnp.maximum(top, 0.0), 0.0)
    broad = jnp.maximum(jnp.minimum(left + CUT, float(SIDE)) - jnp.maximum(left, 0.0), 0.0)
    share = 1.0 - tall * broad / float(SIDE * SIDE)
    lanes = iota((per, 128), 1)
    facts[...] = jnp.where(
        lanes == 0,
        own[:, META : META + 1],
        jnp.where(lanes == 1, other[:, META : META + 1], share),
    )
    tiles[...] = jnp.zeros(tiles.shape, full)
    for piece in range(15):
        tiles[:, piece, :] = blended[:, piece * 128 : (piece + 1) * 128]
    tiles[:, 16:32, :] = pltpu.roll(tiles[:, 0:16, :], 64, 2)
    spot = iota((32, 32), 0)
    tap_at = ((spot % 16) % 5) * 2 + spot // 16
    colour_at = (spot % 16) // 5
    order = hot(
        (iota((32, 32), 1) == tap_at * 3 + colour_at) & (tap_at < 9) & (spot % 16 < 15)
    )
    for image in range(per):
        cells = dot(tiles[image].astype(half), order, TN)
        for line in range(8):
            loose[line * band + image * 8 : line * band + image * 8 + 8, :] = cells[
                line * 8 : line * 8 + 8
            ]
    patches[...] = loose[...].astype(half)
    stem_pad[...] = jnp.zeros(stem_pad.shape, full)
    stem_pad[:, 0:27] = stem_w[...]
    proj_b_pad[...] = jnp.zeros(proj_b_pad.shape, half)
    proj_b_pad[:, 0:C2] = proj_b[...].astype(half)
    for copy in copies:
        copy.wait()
    lanes = iota((1, WIDE), 1)
    packed = gathered[...]
    proj_t[...] = jnp.where(lanes < C2, packed.astype(full), 0.0).astype(half)
    place = hot(iota((WIDE, 16), 0) == iota((WIDE, 16), 1) + C2)
    head_all[...] = dot(packed, place).astype(half)
    column = iota((8, WIDE), 1)
    name = iota((8, WIDE), 0)
    pieces = [
        dot(hot((column == name + (C2 + 16 + 8 * part)) & (name < 6)), packed, NT)
        for part in range(3)
    ]
    norm_rows[...] = pieces[0] + (pieces[1] + pieces[2])
    stem_half = stem_pad[...].astype(half)
    proj_a_half = proj_a[...].astype(half)
    totals[...] = jnp.zeros(totals.shape, full)
    tall_chunk = 2 * band

    def step(index, carry):
        at = pl.ds(pl.multiple_of(index * tall_chunk, 16), tall_chunk)
        stem = dot(patches[at], stem_half, NT)
        stem_out[at] = stem
        one = dot(gelu_pair(stem)[0].astype(half), proj_a_half)
        mid_one[at] = one
        two = dot(gelu_pair(one)[0].astype(half), proj_b_pad[...])
        mid_two[at] = two
        three = gelu_pair(two)[0].astype(half)
        act_three[at] = three
        result = dot(three, proj_t[...], NT)
        base[at] = result
        totals[0:1] += jnp.sum(result, axis=0, keepdims=True)
        totals[1:2] += jnp.sum(result * result, axis=0, keepdims=True)
        return carry

    lax.fori_loop(0, rows // tall_chunk, step, 0)
    spread_stats(stats, [totals[0:1], totals[1:2]])


def spread_stats(out, parts):
    line = jnp.concatenate(parts, axis=1)
    out[...] = jnp.broadcast_to(line[None], out.shape)


def moments(stats, row_total):
    line = jnp.sum(stats[...], axis=0)
    mean = line[:, 0:C3] / row_total
    rstd = lax.rsqrt(line[:, C3 : 2 * C3] / row_total - mean * mean + norm_eps)
    return (mean, rstd)


def quarter_rows(rows, part):
    step = rows // QUARTERS
    return pl.ds(part * step, step)


def fetch_quarter(source, target, sem, part):
    here = quarter_rows(source.shape[0], part)
    return fetch(source.at[here], target.at[here], sem)


def walk_quarter(rows, part, body, carry):
    step = rows // QUARTERS // CHUNK
    return lax.fori_loop(part * step, (part + 1) * step, body, carry)


def start_weights(ids, pieces, weights, sems):
    rows = pieces[0].shape[0]
    low = pieces[3].shape[0]
    copies = []
    for side in range(2):
        for place in range(5):
            piece = pieces[5 * side + place]
            turn = min(place, 3)
            spot = (ids[0] ^ turn) * (2 * rows) + (ids[2] ^ side) * rows
            if place == 4:
                spot = spot + low
            spot = pl.multiple_of(spot, 16)
            copies.append(
                fetch(piece, weights.at[pl.ds(spot, piece.shape[0])], sems.at[5 * side + place])
            )
    return copies


def shifted(values, by):
    block = values.reshape(CHUNK // 8, 8, C3)
    place = iota((1, 8, 1), 1)
    if by == 1:
        moved = jnp.where(place == 0, 0.0, pltpu.roll(block, 1, 1))
    else:
        moved = jnp.where(place == 7, 0.0, pltpu.roll(block, 7, 1))
    return moved.reshape(CHUNK, C3)


def conv_kernel(sizes, layer, *refs):
    per, row_total, split = sizes
    rows = per * 64
    band = per * 8
    ids, source, stats_in, norm_rows = refs[0:4]
    offset = 4
    if layer == 1:
        base = refs[4]
        offset = 5
    pieces = refs[offset : offset + 10]
    offset += 10
    (result, field_out, slope_out, stats, held, weights, field, slope, total) = refs[
        offset : offset + 9
    ]
    weight_sems, in_sems, out_sems = refs[offset + 9 : offset + 12]
    inputs = [fetch_quarter(source, held, in_sems.at[part], part) for part in range(QUARTERS)]
    copies = start_weights(ids, pieces, weights, weight_sems)
    mean, rstd = moments(stats_in, row_total)
    factor = rstd * norm_rows[2 * layer : 2 * layer + 1]
    shift = norm_rows[2 * layer + 1 : 2 * layer + 2] - mean * factor

    def prepare(index, carry):
        at = pl.ds(pl.multiple_of(index * CHUNK, 16), CHUNK)
        value, gradient = gelu_pair(held[at] * factor + shift)
        slope[at] = gradient
        field[at, 0:C3] = shifted(value, 1).astype(half)
        field[at, C3 : 2 * C3] = value.astype(half)
        field[at, 2 * C3 : TRIPLE] = shifted(value, -1).astype(half)
        return carry

    for part in range(QUARTERS):
        inputs[part].wait()
        walk_quarter(rows, part, prepare, 0)
    outputs = [
        fetch(field.at[:, C3 : 2 * C3], field_out, out_sems.at[QUARTERS]),
        fetch(slope, slope_out, out_sems.at[QUARTERS + 1]),
    ]
    if layer == 1:
        inputs = [fetch_quarter(base, held, in_sems.at[part], part) for part in range(QUARTERS)]
    for copy in copies:
        copy.wait()
    inner = rows - band
    total[...] = dot(field[...], weights[:, TRIPLE : 2 * TRIPLE], NT)
    total[band:rows] += dot(field[0:inner], weights[:, 0:TRIPLE], NT)
    total[0:inner] += dot(field[band:rows], weights[:, 2 * TRIPLE : 3 * TRIPLE], NT)

    def count(index, carry):
        at = pl.ds(pl.multiple_of(index * CHUNK, 16), CHUNK)
        value = total[at]
        if layer == 1:
            value = value + held[at]
            total[at] = value
        return (
            carry[0] + jnp.sum(value.reshape(CHUNK // 8, 8, C3), axis=0),
            carry[1] + jnp.sum((value * value).reshape(CHUNK // 8, 8, C3), axis=0),
        )

    zero = jnp.zeros((8, C3), full)
    sums = (zero, zero)
    for part in range(QUARTERS):
        if layer == 1:
            inputs[part].wait()
        else:
            outputs.append(fetch_quarter(total, result, out_sems.at[part], part))
        sums = walk_quarter(rows, part, count, sums)
        if layer == 1:
            outputs.append(fetch_quarter(total, result, out_sems.at[part], part))
    spread_stats(stats, [jnp.sum(item, axis=0, keepdims=True) for item in sums])
    for copy in outputs:
        copy.wait()


def head_kernel(sizes, *refs):
    per, row_total, image_total, classes = sizes
    rows = per * 64
    band = per * 8
    (
        summed,
        stats_in,
        norm_rows,
        head_all,
        facts,
        slope,
        spread,
        stats,
        grad_head,
        sum_value,
        sum_slope,
        sum_cross,
    ) = refs
    mean, rstd = moments(stats_in, row_total)
    gain = norm_rows[4:5]
    bias = norm_rows[5:6]
    sum_value[...] = jnp.zeros((band, C3), full)
    sum_slope[...] = jnp.zeros((band, C3), full)
    sum_cross[...] = jnp.zeros((band, C3), full)

    def walk(index, carry):
        for part in range(band // CHUNK):
            at = pl.ds(pl.multiple_of(index * band + part * CHUNK, 16), CHUNK)
            here = slice(part * CHUNK, part * CHUNK + CHUNK)
            unit = (summed[at] - mean) * rstd
            value, gradient = gelu_pair(unit * gain + bias)
            slope[at] = gradient
            sum_value[here] += value
            sum_slope[here] += gradient
            sum_cross[here] += gradient * unit
        return carry

    lax.fori_loop(0, 8, walk, 0)

    def by_image(ref):
        return jnp.sum(ref[...].reshape(per, 8, C3), axis=1)

    pooled = (by_image(sum_value) / 64.0).astype(half)
    logits = dot(pooled, head_all[...])
    lanes = iota((per, 16), 1)
    inside = lanes < classes
    own = facts[:, 0:1].astype(jnp.int32)
    other = facts[:, 1:2].astype(jnp.int32)
    share = facts[:, 2:3]
    target = jnp.where(lanes == own, share, 0.0) + jnp.where(lanes == other, 1.0 - share, 0.0)
    top = jnp.max(jnp.where(inside, logits, -3e38), axis=1, keepdims=True)
    powers = jnp.where(inside, jnp.exp(jnp.where(inside, logits - top, 0.0)), 0.0)
    lse = top + jnp.log(jnp.sum(powers, axis=1, keepdims=True))
    losses = lse - jnp.sum(target * logits, axis=1, keepdims=True)
    loss = jnp.sum(losses, axis=0, keepdims=True)
    soft = jnp.where(inside, jnp.exp(jnp.where(inside, logits - lse, 0.0)), 0.0)
    grad_logits = ((soft - target) / image_total).astype(half)
    grad_head[...] = dot(pooled, grad_logits, TN)
    pull = dot(grad_logits, head_all[...], NT) / 64.0
    spread[...] = jnp.broadcast_to(pull[:, None, :], (per, 8, C3)).reshape(band, C3)
    bias_sum = jnp.sum(pull * by_image(sum_slope), axis=0, keepdims=True)
    gain_sum = jnp.sum(pull * by_image(sum_cross), axis=0, keepdims=True)
    spread_stats(stats, [bias_sum, gain_sum, jnp.broadcast_to(loss, (1, 128))])


def grad_moments(stats, row_total):
    line = jnp.sum(stats[...], axis=0)
    return (line[:, 0:C3] / row_total, line[:, C3 : 2 * C3] / row_total)


def input_grad(gradient, weights, out, band):
    rows = gradient.shape[0]
    inner = rows - band
    spans = (
        (1, slice(0, rows), slice(0, rows)),
        (0, slice(0, inner), slice(band, rows)),
        (2, slice(band, rows), slice(0, inner)),
    )
    for line, to, of in spans:
        for col in range(3):
            tap = 3 * line + col
            part = dot(
                gradient[of, col * C3 : (col + 1) * C3], weights[:, tap * C3 : (tap + 1) * C3]
            )
            if line == 1 and col == 0:
                out[to] = part
            else:
                out[to] += part


def half_filters(ids, split):
    tall = C3 // (2 * split)
    place = iota((1, 2 * WIDE), 1)
    side = jnp.where(place < WIDE, 0, 1)
    place = place - side * WIDE
    target = (ids[0] ^ (place // tall)) * (2 * tall) + (ids[2] ^ side) * tall + place % tall
    target = jnp.where(place < C3 // 2, target, -1)
    return hot(iota((C3, 2 * WIDE), 0) == target)


def norm_back(arriving, unit, factor, low, high):
    return factor * (arriving - low - unit * high)


def send_halves(middle, pick, helds, halves, sems, part):
    here = quarter_rows(helds[0].shape[0], part)
    both = dot(middle, pick).astype(half)
    copies = []
    for side in range(2):
        helds[side][here] = both[:, side * WIDE : (side + 1) * WIDE]
        copies.append(
            fetch(helds[side].at[here], halves[side].at[here], sems.at[2 * part + side])
        )
    return copies


def back_kernel(sizes, layer, *refs):
    per, row_total, split = sizes
    rows = per * 64
    band = per * 8
    last = layer == 1
    ids = refs[0]
    if last:
        incoming, source, stats_here, stats_grad, norm_rows, spread = refs[1:7]
        offset = 7
    else:
        incoming = refs[1]
        offset = 2
    before, slope_before, stats_before = refs[offset : offset + 3]
    pieces = refs[offset + 3 : offset + 13]
    result, stats = refs[offset + 13 : offset + 15]
    offset += 15
    if last:
        own_half, far_half, grad_out, kept, own_held, far_held, pick, half_sems = refs[
            offset : offset + 8
        ]
        offset += 8
    else:
        arrived = refs[offset]
        offset += 1
    held, origin, weights, gradient, total = refs[offset : offset + 5]
    weight_sems, in_sems, out_sems = refs[offset + 5 : offset + 8]
    inputs = []
    for part in range(QUARTERS):
        if last:
            inputs.append(
                (
                    fetch_quarter(incoming, held, in_sems.at[2 * part], part),
                    fetch_quarter(source, origin, in_sems.at[2 * part + 1], part),
                )
            )
        else:
            inputs.append((fetch_quarter(incoming, arrived, in_sems.at[2 * part], part),))
    copies = start_weights(ids, pieces, weights, weight_sems)
    if last:
        mean, rstd = moments(stats_here, row_total)
        low, high = grad_moments(stats_grad, row_total)
        factor = rstd * norm_rows[4:5]
        parts = band // CHUNK
        pick[...] = half_filters(ids, split)

    def prepare(index, carry):
        at = pl.ds(pl.multiple_of(index * CHUNK, 16), CHUNK)
        if last:
            here = pl.ds(pl.multiple_of(lax.rem(index, parts) * CHUNK, 16), CHUNK)
            unit = (origin[at] - mean) * rstd
            value = norm_back(held[at] * spread[here], unit, factor, low, high)
            kept[at] = value
            gradient[at, C3 : 2 * C3] = value.astype(half)
        else:
            gradient[at, C3 : 2 * C3] = arrived[at]
            value = arrived[at].astype(full)
        gradient[at, 0:C3] = shifted(value, -1).astype(half)
        gradient[at, 2 * C3 : TRIPLE] = shifted(value, 1).astype(half)
        return carry

    for part in range(QUARTERS):
        for copy in inputs[part]:
            copy.wait()
        walk_quarter(rows, part, prepare, 0)
    outputs = []
    if last:
        outputs.append(fetch(kept, grad_out, half_sems.at[2 * QUARTERS]))
        for part in range(QUARTERS):
            outputs += send_halves(
                gradient[quarter_rows(rows, part), C3 : 2 * C3],
                pick[...],
                (own_held, far_held),
                (own_half, far_half),
                half_sems,
                part,
            )
    inputs = []
    for part in range(QUARTERS):
        inputs.append(
            (
                fetch_quarter(before, origin, in_sems.at[2 * part], part),
                fetch_quarter(slope_before, held, in_sems.at[2 * part + 1], part),
            )
        )
    for copy in copies:
        copy.wait()
    input_grad(gradient, weights, total, band)
    mean, rstd = moments(stats_before, row_total)

    def finish(index, carry):
        at = pl.ds(pl.multiple_of(index * CHUNK, 16), CHUNK)
        value = total[at] * held[at]
        total[at] = value
        unit = (origin[at] - mean) * rstd
        return (
            carry[0] + jnp.sum(value.reshape(CHUNK // 8, 8, C3), axis=0),
            carry[1] + jnp.sum((value * unit).reshape(CHUNK // 8, 8, C3), axis=0),
        )

    zero = jnp.zeros((8, C3), full)
    sums = (zero, zero)
    for part in range(QUARTERS):
        for copy in inputs[part]:
            copy.wait()
        sums = walk_quarter(rows, part, finish, sums)
        outputs.append(fetch_quarter(total, result, out_sems.at[part], part))
    spread_stats(stats, [jnp.sum(item, axis=0, keepdims=True) for item in sums])
    for copy in outputs:
        copy.wait()


def norm_back_kernel(sizes, *refs):
    row_total, split = sizes
    ids, incoming, source, stats_here, stats_grad, norm_rows = refs[0:6]
    grad_half, own_half, far_half = refs[6:9]
    held, origin, middle, own_held, far_held, pick, in_sems, out_sems = refs[9:]
    rows = held.shape[0]
    inputs = []
    for part in range(QUARTERS):
        inputs.append(
            (
                fetch_quarter(incoming, held, in_sems.at[2 * part], part),
                fetch_quarter(source, origin, in_sems.at[2 * part + 1], part),
            )
        )
    mean, rstd = moments(stats_here, row_total)
    low, high = grad_moments(stats_grad, row_total)
    factor = rstd * norm_rows[2:3]
    pick[...] = half_filters(ids, split)

    def prepare(index, carry):
        at = pl.ds(pl.multiple_of(index * CHUNK, 16), CHUNK)
        unit = (origin[at] - mean) * rstd
        middle[at] = norm_back(held[at], unit, factor, low, high).astype(half)
        return carry

    outputs = []
    for part in range(QUARTERS):
        for copy in inputs[part]:
            copy.wait()
        walk_quarter(rows, part, prepare, 0)
        here = quarter_rows(rows, part)
        outputs.append(fetch(middle.at[here], grad_half.at[here], out_sems.at[8 + part]))
        outputs += send_halves(
            middle[here], pick[...], (own_held, far_held), (own_half, far_half), out_sems, part
        )
    for copy in outputs:
        copy.wait()


def weight_grad_kernel(sizes, *refs):
    chunks, split, band = sizes
    gradients = refs[0:2]
    fields = refs[2:4]
    count = sum(len(part_sizes(split, lines)) for lines in chunks)
    outs = refs[4 : 4 + count]
    (gradient, field, plain, held, in_sems, grad_sems, sems) = refs[4 + count :]
    inputs = []
    for line in range(8):
        for side in range(2):
            of = pl.ds(line * band, band)
            inputs.append(
                fetch(fields[side].at[of], plain.at[side, of], in_sems.at[2 * line + side])
            )
    arriving = []
    for line in range(8):
        for side in range(2):
            of = pl.ds(line * band, band)
            to = pl.ds((2 * line + side) * band, band)
            arriving.append(
                fetch(gradients[side].at[of], gradient.at[to], grad_sems.at[2 * line + side])
            )

    def prepare(index, carry):
        for side in range(2):
            for part in range(band // CHUNK):
                to = pl.ds(
                    pl.multiple_of((2 * index + side) * band + part * CHUNK, 16), CHUNK
                )
                of = pl.ds(pl.multiple_of(index * band + part * CHUNK, 16), CHUNK)
                value = plain[side, of]
                wide = value.astype(full)
                field[to, 0:C3] = shifted(wide, 1).astype(half)
                field[to, C3 : 2 * C3] = value
                field[to, 2 * C3 : TRIPLE] = shifted(wide, -1).astype(half)
        return carry

    for part in range(QUARTERS):
        for copy in inputs[4 * part : 4 * part + 4]:
            copy.wait()
        lax.fori_loop(2 * part, 2 * part + 2, prepare, 0)
    for copy in arriving:
        copy.wait()
    rows = field.shape[0]
    inner = rows - 2 * band
    spans = {
        0: (slice(2 * band, rows), slice(0, inner)),
        1: (slice(0, rows), slice(0, rows)),
        2: (slice(0, inner), slice(2 * band, rows)),
    }
    tall = held.shape[2]
    copies = []
    start = 0
    number = 0
    for lines in chunks:
        for place, line in enumerate(lines):
            left, right = spans[line]
            part = dot(gradient[left, 0 : C3 // 2], field[right], TN).astype(half)
            for turn in range(split):
                for block in range(15):
                    held[turn, start + place * 15 + block] = part[
                        turn * tall : (turn + 1) * tall, block * 128 : (block + 1) * 128
                    ]
        for turn, first, size in part_sizes(split, lines):
            copies.append(
                fetch(
                    held.at[turn, start + first : start + first + size],
                    outs[number],
                    sems.at[number],
                )
            )
            number += 1
        start += 15 * len(lines)
    for copy in copies:
        copy.wait()


def part_sizes(split, lines):
    blocks = 15 * len(lines)
    sizes = [(turn, 0, blocks) for turn in range(split - 1)]
    return sizes + [(split - 1, 0, blocks // 2), (split - 1, blocks // 2, blocks - blocks // 2)]


def trunk_kernel(sizes, *refs):
    per, row_total, split = sizes
    rows = per * 64
    band = per * 8
    (
        ids,
        incoming,
        grad_summed,
        base,
        stats_one,
        stats_six,
        norm_rows,
        proj_t,
        act_three,
        mid_two,
        mid_one,
        stem_out,
        patches,
        proj_a,
        proj_b,
        grad_head,
        mine,
        other,
        trunk,
        grad_two,
        act_two,
        grad_one,
        act_one,
        grad_stem,
        proj_b_pad,
        split_part,
        shared_part,
        sems,
    ) = refs
    mean, rstd = moments(stats_one, row_total)
    low, high = grad_moments(stats_six, row_total)
    factor = rstd * norm_rows[0:1]
    proj_b_pad[...] = jnp.zeros(proj_b_pad.shape, half)
    proj_b_pad[:, 0:C2] = proj_b[...].astype(half)
    proj_a_half = proj_a[...].astype(half)

    def prepare(index, carry):
        at = pl.ds(pl.multiple_of(index * CHUNK, 16), CHUNK)
        unit = (base[at] - mean) * rstd
        value = grad_summed[at] + factor * (incoming[at] - low - unit * high)
        trunk[at] = value.astype(half)
        return carry

    lax.fori_loop(0, rows // CHUNK, prepare, 0)
    tall_chunk = 2 * band

    def step(index, carry):
        at = pl.ds(pl.multiple_of(index * tall_chunk, 16), tall_chunk)
        three = dot(trunk[at], proj_t[...])
        two = (three * gelu_pair(mid_two[at])[1]).astype(half)
        grad_two[at] = two
        value, slope = gelu_pair(mid_one[at])
        act_two[at] = value.astype(half)
        one = (dot(two, proj_b_pad[...], NT) * slope).astype(half)
        grad_one[at] = one
        value, slope = gelu_pair(stem_out[at])
        act_one[at] = value.astype(half)
        grad_stem[at] = (dot(one, proj_a_half, NT) * slope).astype(half)
        return carry

    lax.fori_loop(0, rows // tall_chunk, step, 0)
    place = hot(iota((16, WIDE), 0) + C2 == iota((16, WIDE), 1))
    split_part[...] = (
        dot(trunk[...], act_three[...], TN) + dot(grad_head[...].astype(half), place)
    ).astype(half)
    shared = dot(act_two[...], grad_two[...], TN)
    shared = shared + dot(dot(grad_one[...], act_one[...], TN).astype(half), place)
    stem = dot(patches[...], grad_stem[...], TN).astype(half)
    tall = split_part.shape[0] // (2 * split)
    spot = iota((C1, 32), 0)
    twice = hot((spot % tall == iota((C1, 32), 1)) & (spot % tall < 27))
    place = hot(iota((16, WIDE), 0) + (C2 + 16) == iota((16, WIDE), 1))
    shared = shared + dot(dot(twice, stem).astype(half), place)
    shared_part[...] = shared.astype(half)
    copies = []
    for turn in range(split):
        for side, target in ((0, mine), (1, other)):
            place = pl.multiple_of((ids[2] ^ side) * tall, 16)
            spot = pl.multiple_of((ids[0] ^ turn) * (2 * tall) + (ids[2] ^ side) * tall, 16)
            number = 2 * (2 * turn + side)
            copy = pltpu.make_async_copy(
                split_part.at[pl.ds(spot, tall)], target.at[turn, 0:tall], sems.at[number]
            )
            copy.start()
            copies.append(copy)
            copy = pltpu.make_async_copy(
                shared_part.at[pl.ds(place, tall)],
                target.at[turn, tall : 2 * tall],
                sems.at[number + 1],
            )
            copy.start()
            copies.append(copy)
    for copy in copies:
        copy.wait()


def clip_scale(squares):
    total = jnp.sum(jnp.sum(squares[...], axis=0), axis=1, keepdims=True)
    size = jnp.sqrt(total[:, 0:1] / 128.0)
    return (size, jnp.minimum(1.0, clip_limit / size))


def conv_update_kernel(sizes, *refs):
    pieces_count, places, step_rate = sizes
    ids = refs[0]
    squares, weight, first, second = refs[1:5]
    pieces = refs[5 : 5 + pieces_count]
    (first_new, second_new, weight_new, held, sems) = refs[5 + pieces_count :]
    layer = pl.program_id(0)
    line = pl.program_id(1)

    def copies(wanted):
        made = []
        for number, (owner, start, size, side) in enumerate(places):
            if owner not in wanted:
                continue
            tall = pieces[number].shape[1]
            row = pl.multiple_of((ids[2] ^ side) * tall, 16)
            made.append(
                pltpu.make_async_copy(
                    pieces[number],
                    held.at[owner, start : start + size, pl.ds(row, tall), :],
                    sems.at[number],
                )
            )
        return made

    @pl.when((layer == 0) & (line == 0))
    def _():
        for copy in copies((0, 1)):
            copy.start()

    for owner in range(2):

        @pl.when((layer == owner) & (line == 0))
        def _():
            for copy in copies((owner,)):
                copy.wait()

    size, scale = clip_scale(squares)
    for part in range(9):
        lanes = slice(part * 128, part * 128 + 128)
        block = line * 9 + part
        gradient = held[layer, block].astype(full) * scale
        results = adamw(
            weight[0, :, lanes], gradient, first[0, :, lanes], second[0, :, lanes], step_rate
        )
        first_new[0, :, lanes] = results[0]
        second_new[0, :, lanes] = results[1]
        weight_new[0, :, lanes] = results[2]


def small_update_kernel(rates, *refs):
    ids, squares, mine, other, grad_norm_p = refs[0:5]
    states = refs[5:23]
    outs = refs[23:41]
    size_out = refs[41]
    size, scale = clip_scale(squares)
    size_out[...] = jnp.broadcast_to(size, size_out.shape)
    first_core = ids[2] == 0
    tall = mine.shape[0] // 2
    here = mine[...].astype(full)
    there = other[...].astype(full)
    even = jnp.where(first_core, here, there)
    odd = jnp.where(first_core, there, here)
    split_part = jnp.concatenate([even[0:tall], odd[0:tall]], axis=0).astype(half)
    shared = jnp.concatenate([even[tall:], odd[tall:]], axis=0).astype(half)
    grad_c = split_part[:, 0:C2].astype(full)
    classes = states[12].shape[0]
    pick = hot(iota((classes, WIDE), 0) + C2 == iota((classes, WIDE), 1))
    grad_head = dot(pick, split_part, NT)
    grad_b = shared[:, 0:C2].astype(full)
    pick = hot(iota((C0, WIDE), 0) + C2 == iota((C0, WIDE), 1))
    grad_a = dot(pick, shared, NT)
    pick = hot(iota((C0, WIDE), 0) + (C2 + 16) == iota((C0, WIDE), 1))
    grad_stem = dot(pick, shared[0:32], NT)[:, 0:27]
    gradients = (grad_stem, grad_a, grad_b, grad_c, grad_head, grad_norm_p[...])
    for index in range(6):
        weight, first, second = states[3 * index : 3 * index + 3]
        results = adamw(
            weight[...], gradients[index] * scale, first[...], second[...], rates[index]
        )
        for item in range(3):
            outs[3 * index + item][...] = results[item]


def xor_pairs(size, turn):
    return [(index, index ^ turn) for index in range(size)]


def shards(
    images,
    labels,
    corners,
    partners,
    stem_w,
    stem_w_m,
    stem_w_v,
    proj_a,
    proj_a_m,
    proj_a_v,
    proj_b,
    proj_b_m,
    proj_b_v,
    proj_c,
    proj_c_m,
    proj_c_v,
    conv_w,
    conv_w_m,
    conv_w_v,
    head_w,
    head_w_m,
    head_w_v,
    norm_p,
    norm_p_m,
    norm_p_v,
):
    split = lax.axis_size("dp")
    groups = lax.axis_size("filt")
    chips = groups // 2
    devices = split * groups
    count = images.shape[0]
    per = count // split
    rows = per * 64
    band = per * 8
    image_total = float(count * groups)
    row_total = image_total * 64.0
    tall = conv_w.shape[1] // 2
    spot_d = lax.axis_index("dp")
    spot_f = lax.axis_index("filt")
    ids = jnp.stack([spot_d, spot_f, spot_f % 2, spot_f // 2]).astype(jnp.int32)

    def over_dp(value, turn):
        return lax.ppermute(value, "dp", xor_pairs(split, turn))

    def over_filt(value, turn):
        return lax.ppermute(value, "filt", xor_pairs(groups, turn))

    def exchange(stats):
        return lax.all_to_all(stats, ("dp", "filt"), 0, 0)

    (own_images,) = call(
        image_kernel,
        [VMEM] * 4,
        [(shape((count, 3 * PLANE), half), VMEM)],
        [pltpu.VMEM((8, count), full)],
        3,
    )(
        images.transpose(1, 0, 2),
        labels.reshape(1, count),
        corners.T,
        partners.reshape(1, count),
    )
    (own_pack,) = call(
        pack_kernel,
        [VMEM] * 3,
        [(shape((2 * tall, WIDE), half), VMEM)],
        [],
        2,
        1,
    )(proj_c.T, head_w.T, norm_p, own_images)
    packs = [own_pack] + [over_dp(own_pack, turn) for turn in range(1, split)]
    far_images = [own_images] + [over_filt(own_images, 2 * turn) for turn in range(1, chips)]
    def start_gather(layer, after):
        own = cast_half(ids, conv_w, layer, after)
        return [own, over_dp(own, 1), over_dp(own, 2)]

    def middle_gather(pieces, after):
        rows = pieces[0].shape[0]
        return cut_rows(pieces[:0:-1], [(0, 48), (48, rows - 48)], after)

    def end_gather(pieces, far):
        pieces = [*pieces, over_dp(far[0], 1), over_dp(far[1], 2)]
        return pieces + [over_filt(piece, 1) for piece in pieces]

    pieces = start_gather(0, packs)
    far = middle_gather(pieces, [])
    all_images = stack(
        far_images,
        [(turn, 0, count) for turn in range(chips)],
        (chips, count, 3 * PLANE),
        pieces[:1],
    )

    line = shape((devices, 1, 2 * C3))
    (
        patches,
        stem_out,
        mid_one,
        mid_two,
        act_three,
        base,
        stats,
        norm_rows,
        head_all,
        proj_t,
        facts,
    ) = call(
        functools.partial(front_kernel, (per, count, groups, devices, split)),
        [SMEM] + [VMEM] * 2 + [ANY] * split + [VMEM] * 3,
        [
            (shape((rows, 32), half), VMEM),
            (shape((rows, C0)), VMEM),
            (shape((rows, C1)), VMEM),
            (shape((rows, WIDE)), VMEM),
            (shape((rows, WIDE), half), VMEM),
            (shape((rows, C3)), VMEM),
            (line, VMEM),
            (shape((8, C3)), VMEM),
            (shape((C3, 16), half), VMEM),
            (shape((C3, WIDE), half), VMEM),
            (shape((per, 128)), VMEM),
        ],
        [
            pltpu.VMEM((C3, WIDE), half),
            pltpu.VMEM((per, 32, 128), full),
            pltpu.VMEM((rows, 32), full),
            pltpu.VMEM((C0, 32), full),
            pltpu.VMEM((C1, WIDE), half),
            pltpu.VMEM((8, C3), full),
            pltpu.SemaphoreType.DMA((split,)),
        ],
        10,
        1,
    )(ids, all_images, over_filt(all_images, 1), *packs, stem_w.T, proj_a, proj_b, far[0])
    kernels = [end_gather(pieces, far)]
    stats_one = exchange(stats)
    pieces = start_gather(1, [stats_one])

    table = pltpu.VMEM((rows, C3), full)
    conv_outs = [
        (shape((rows, C3)), ANY),
        (shape((rows, C3), half), ANY),
        (shape((rows, C3)), ANY),
        (line, VMEM),
    ]
    conv_scratch = [
        table,
        pltpu.VMEM((C3, 9 * C3), half),
        pltpu.VMEM((rows, TRIPLE), half),
        table,
        table,
        pltpu.SemaphoreType.DMA((10,)),
        pltpu.SemaphoreType.DMA((QUARTERS,)),
        pltpu.SemaphoreType.DMA((QUARTERS + 2,)),
    ]
    conv_one, field_one, slope_one, stats = call(
        functools.partial(conv_kernel, (per, row_total, split), 0),
        [SMEM, ANY, VMEM, VMEM] + [ANY] * 10,
        conv_outs,
        conv_scratch,
        18,
    )(ids, base, stats_one, norm_rows, *kernels[0])
    kernels.append(end_gather(pieces, middle_gather(pieces, [stats])))
    stats_two = exchange(stats)
    far_field_one = over_filt(field_one, 1)
    summed, field_two, slope_two, stats = call(
        functools.partial(conv_kernel, (per, row_total, split), 1),
        [SMEM, ANY, VMEM, VMEM, ANY] + [ANY] * 10,
        conv_outs,
        conv_scratch,
        18,
    )(ids, conv_one, stats_two, norm_rows, base, *kernels[1])
    stats_three = exchange(stats)
    far_field_two = over_filt(field_two, 1)
    slope_three, spread, stats, grad_head = call(
        functools.partial(head_kernel, (per, row_total, image_total, head_w.shape[1])),
        [VMEM] * 5,
        [
            (shape((rows, C3)), VMEM),
            (shape((band, C3)), VMEM),
            (shape((devices, 1, 2 * C3 + 128)), VMEM),
            (shape((C3, 16)), VMEM),
        ],
        [pltpu.VMEM((band, C3), full)] * 3,
        7,
    )(summed, stats_three, norm_rows, head_all, facts)
    stats_four = exchange(stats)
    loss = jnp.sum(stats_four[:, 0, 2 * C3])

    wide_half = pltpu.VMEM((rows, WIDE), half)
    picks = pltpu.VMEM((C3, 2 * WIDE), half)
    half_outs = [(shape((rows, WIDE), half), ANY)] * 2

    def back(layer, heads, tails, after):
        last = layer == 1
        return call(
            functools.partial(back_kernel, (per, row_total, split), layer),
            ([SMEM, ANY, ANY] + [VMEM] * 4 if last else [SMEM, ANY])
            + [ANY, ANY, VMEM]
            + [ANY] * 10,
            [(shape((rows, C3)), ANY), (line, VMEM)]
            + (half_outs + [(shape((rows, C3)), ANY)] if last else []),
            (
                [table, wide_half, wide_half, picks, pltpu.SemaphoreType.DMA((2 * QUARTERS + 1,))]
                if last
                else [pltpu.VMEM((rows, C3), half)]
            )
            + [
                table,
                table,
                pltpu.VMEM((C3, 9 * C3), half),
                pltpu.VMEM((rows, TRIPLE), half),
                table,
                pltpu.SemaphoreType.DMA((10,)),
                pltpu.SemaphoreType.DMA((2 * QUARTERS,)),
                pltpu.SemaphoreType.DMA((QUARTERS,)),
            ],
            22,
            len(after),
        )(ids, *heads, *tails, *kernels[layer], *after)

    grad_conv_one, stats, own_half, far_half, grad_summed = back(
        1,
        [slope_three, summed, stats_three, stats_four, norm_rows, spread],
        [conv_one, slope_two, stats_two],
        [],
    )
    stats_five = exchange(stats)

    def weight_grad(own_half, far_half, field, far_field, chunks, after):
        sizes = [part_sizes(split, lines) for lines in chunks]
        outs = [
            (shape((size, tall, 128), half), ANY) for parts in sizes for _, _, size in parts
        ]
        flat = call(
            functools.partial(weight_grad_kernel, (chunks, split, band)),
            [ANY] * 4,
            outs,
            [
                pltpu.VMEM((2 * rows, WIDE), half),
                pltpu.VMEM((2 * rows, TRIPLE), half),
                pltpu.VMEM((2, rows, C3), half),
                pltpu.VMEM((split, 45, tall, 128), half),
                pltpu.SemaphoreType.DMA((16,)),
                pltpu.SemaphoreType.DMA((16,)),
                pltpu.SemaphoreType.DMA((len(outs),)),
            ],
            13,
            len(after),
        )(own_half, over_filt(far_half, 1), field, far_field, *after)
        result = []
        for parts in sizes:
            result.append(flat[: len(parts)])
            flat = flat[len(parts) :]
        return result

    def square_sum(value):
        wide = value.astype(full)
        return jnp.sum(wide * wide)

    def add(values):
        return sum(value.astype(full) for value in values).astype(half)

    def start_dp(parts, after):
        own, near, next_near, far_low, far_high = parts
        blocks = near.shape[0]
        cut = far_low.shape[0]
        from_near = over_dp(far_low, 1)
        from_next = over_dp(far_high, 2)
        near, next_near = merge(
            [near, next_near, from_near, from_next],
            [
                (blocks, [(0, 0, 0, blocks), (3, 0, cut, blocks - cut)]),
                (blocks, [(1, 0, 0, blocks), (2, 0, 0, cut)]),
            ],
            after,
            3,
        )
        return [own, near, next_near]

    def end_dp(parts, sizes, after):
        own, near, next_near = parts
        plan = []
        start = 0
        for size in sizes:
            plan.append((size, [(source, start, 0, size) for source in range(3)]))
            start += size
        return merge([own, over_dp(near, 1), over_dp(next_near, 2)], plan, after, 2)

    def over_all_chips(value, after=()):
        result = value
        reach = 1
        while reach < chips:
            digit = ids[3] // reach % 4
            outer = (digit == 0) | (digit == 3)
            moves = ({0: 1, 3: 2}, {1: 2, 2: 1}, {1: 0, 2: 3})
            routes = []
            for move in moves:
                pairs = []
                for index in range(groups):
                    here = index // 2 // reach % 4
                    if here in move:
                        pairs.append((index, index + (move[here] - here) * 2 * reach))
                routes.append(pairs)
            arrived = lax.ppermute(result, "filt", routes[0])
            if after:
                size = result.shape[0]
                plan = [(size, [(0, 0, 0, size), (1, 0, 0, size)])]
                (result,) = merge([result, arrived], plan, after, 2)
            else:
                result = add([result, arrived])
            result = add([result, lax.ppermute(result, "filt", routes[1])])
            squares = jnp.where(outer, 0.0, square_sum(result))
            arrived = lax.ppermute(result, "filt", routes[2])
            result = jnp.where(outer, arrived, result)
            reach *= 4
        return (result, squares)

    chunks_two = ((0, 1, 2),)
    chunks_one = ((0, 1, 2),)
    grad_one_half, own_half_one, far_half_one = call(
        functools.partial(norm_back_kernel, (row_total, split)),
        [SMEM, ANY, ANY, VMEM, VMEM, VMEM],
        [(shape((rows, C3), half), ANY)] + half_outs,
        [
            table,
            table,
            pltpu.VMEM((rows, C3), half),
            wide_half,
            wide_half,
            picks,
            pltpu.SemaphoreType.DMA((2 * QUARTERS,)),
            pltpu.SemaphoreType.DMA((3 * QUARTERS,)),
        ],
        6,
    )(ids, grad_conv_one, conv_one, stats_two, stats_five, norm_rows)
    pairs_two = weight_grad(
        own_half, far_half, field_two, far_field_two, chunks_two, [grad_one_half]
    )
    pairs_one = weight_grad(
        own_half_one, far_half_one, field_one, far_field_one, chunks_one, [pairs_two[0][0]]
    )
    begun_two = start_dp(pairs_two[0], [pairs_one[0][0]])
    grad_base, stats = back(
        0,
        [grad_one_half],
        [base, slope_one, stats_one],
        [pairs_one[0][0], begun_two[1]],
    )
    stats_six = exchange(stats)
    (part_two,) = end_dp(begun_two, [begun_two[0].shape[0]], [stats_six])
    begun_one = start_dp(pairs_one[0], [stats_six])
    small = shape((split, 2 * tall, WIDE), half)
    small_mine, small_other = call(
        functools.partial(trunk_kernel, (per, row_total, split)),
        [SMEM] + [VMEM] * 15,
        [(small, ANY), (small, ANY)],
        [
            pltpu.VMEM((rows, C3), half),
            pltpu.VMEM((rows, WIDE), half),
            pltpu.VMEM((rows, C1), half),
            pltpu.VMEM((rows, C1), half),
            pltpu.VMEM((rows, C0), half),
            pltpu.VMEM((rows, C0), half),
            pltpu.VMEM((C1, WIDE), half),
            pltpu.VMEM((C3, WIDE), half),
            pltpu.VMEM((C1, WIDE), half),
            pltpu.SemaphoreType.DMA((4 * split,)),
        ],
        13,
    )(
        ids,
        grad_base,
        grad_summed,
        base,
        stats_one,
        stats_six,
        norm_rows,
        proj_t,
        act_three,
        mid_two,
        mid_one,
        stem_out,
        patches,
        proj_a,
        proj_b,
        grad_head,
    )
    blocks = begun_one[0].shape[0]
    parts_one = end_dp(begun_one, [blocks // 2, blocks - blocks // 2], [small_mine])
    reduced_two, squares_two = zip(over_all_chips(part_two, [small_mine]))
    reduced_one, squares_one = zip(*[over_all_chips(part) for part in parts_one])
    crossed = over_filt(small_other, 1)
    pair = [add([small_mine[turn], crossed[turn]]) for turn in range(split)]
    small_sum = add([pair[0]] + [over_dp(pair[turn], turn) for turn in range(1, split)])
    small_sum = add(
        [small_sum] + [over_filt(small_sum, 2 * turn) for turn in range(1, chips)]
    )
    small_far = over_filt(small_sum, 1)

    norm_sums = []
    for stats in (stats_six, stats_five, stats_four):
        sums = jnp.sum(stats[:, 0, :], axis=0)
        norm_sums += [sums[C3 : 2 * C3], sums[0:C3]]
    grad_norm_all = jnp.stack(norm_sums)
    grad_norm_p = lax.dynamic_slice_in_dim(grad_norm_all, spot_d * 2 * tall, 2 * tall, axis=1)
    squares = (
        sum(squares_one + squares_two) / (chips // 2)
        + square_sum(small_sum[0:tall, 0 : C2 + 16]) / chips
        + square_sum(small_sum[tall:, 0 : C2 + 16]) / (chips * split)
        + square_sum(small_sum[tall:, C2 + 16 :]) / (2 * chips * split)
        + jnp.sum(grad_norm_all * grad_norm_all) / devices
    )
    squares = exchange(jnp.broadcast_to(squares, (devices, 1, 128)))

    pieces = []
    places = []
    for owner, reduced in ((0, reduced_one), (1, reduced_two)):
        start = 0
        for part in reduced:
            size = part.shape[0]
            pieces += [part, over_filt(part, 1)]
            places += [(owner, start, size, side) for side in range(2)]
            start += size
    whole_spec = pl.BlockSpec((1, 2 * tall, 1152), lambda layer, line: (layer, 0, line))
    conv_shape = shape(conv_w.shape)
    conv_new = pl.pallas_call(
        functools.partial(
            conv_update_kernel, (len(pieces), places, 0.7 / math.sqrt(9.0 * C3))
        ),
        grid=(2, 5),
        in_specs=[SMEM, VMEM, whole_spec, whole_spec, whole_spec] + [ANY] * len(pieces),
        out_specs=[whole_spec] * 3,
        out_shape=[conv_shape] * 3,
        scratch_shapes=[
            pltpu.VMEM((2, 45, 2 * tall, 128), half),
            pltpu.SemaphoreType.DMA((len(pieces),)),
        ],
        compiler_params=pltpu.CompilerParams(vmem_limit_bytes=60 * MIB),
        cost_estimate=pl.CostEstimate(
            flops=20 * conv_w.size, bytes_accessed=26 * conv_w.size, transcendentals=0
        ),
    )(ids, squares, conv_w, conv_w_m, conv_w_v, *pieces)
    states = (
        (stem_w.T, stem_w_m.T, stem_w_v.T),
        (proj_a, proj_a_m, proj_a_v),
        (proj_b, proj_b_m, proj_b_v),
        (proj_c.T, proj_c_m.T, proj_c_v.T),
        (head_w.T, head_w_m.T, head_w_v.T),
        (norm_p, norm_p_m, norm_p_v),
    )
    rates = (
        0.7 / math.sqrt(27.0),
        0.7 / math.sqrt(C0),
        0.7 / math.sqrt(C1),
        0.7 / math.sqrt(C2),
        0.7 / math.sqrt(C3 / 8.0),
        0.8,
    )
    flat = [item for group in states for item in group]
    small_new = call(
        functools.partial(small_update_kernel, rates),
        [SMEM] + [VMEM] * 22,
        [(shape(item.shape), VMEM) for item in flat] + [(shape((1, 128)), VMEM)],
        [],
        3,
    )(ids, squares, small_sum, small_far, grad_norm_p, *flat)
    size = small_new[18][0, 0]
    turned = [
        item.T if index // 3 in (0, 3, 4) else item for index, item in enumerate(small_new[:18])
    ]
    return (
        *turned[0:12],
        *conv_new,
        *turned[12:18],
        loss,
        size,
    )


def solution(mesh):
    placed = (
        P("filt", None, None),
        P("filt"),
        P("filt", None),
        P("filt"),
        *([P()] * 9),
        *([P(None, "dp")] * 3),
        *([P(None, "dp", None)] * 3),
        *([P("dp", None)] * 3),
        *([P(None, "dp")] * 3),
    )
    return jax.shard_map(
        shards,
        mesh=mesh,
        in_specs=placed,
        out_specs=(
            *([P()] * 9),
            *([P(None, "dp")] * 3),
            *([P(None, "dp", None)] * 3),
            *([P("dp", None)] * 3),
            *([P(None, "dp")] * 3),
            P(),
            P(),
        ),
        check_vma=False,
    )
```

```python
import functools
import math

import jax
import jax.numpy as jnp
from jax import lax
from jax.experimental import pallas as pl
from jax.experimental.pallas import tpu as pltpu
from jax.sharding import PartitionSpec as P

C0 = 16
C1 = 160
C2 = 320
C3 = 640
WIDE = 384
TRIPLE = 3 * C3
SIDE = 32
CUT = 16
STEP = 10
PLANE = 640
META = 576
CHUNK = 48
QUARTERS = 4

beta_one = 0.9
beta_two = 0.999
adam_eps = 1e-08
weight_decay = 0.0005
clip_limit = 0.05
norm_eps = 1e-05
gelu_one = math.sqrt(2.0 / math.pi)
gelu_three = 0.044715 * gelu_one

half = jnp.bfloat16
full = jnp.float32
NT = (((1,), (1,)), ((), ()))
NN = (((1,), (0,)), ((), ()))
TN = (((0,), (0,)), ((), ()))
VMEM = pl.BlockSpec(memory_space=pltpu.VMEM)
SMEM = pl.BlockSpec(memory_space=pltpu.SMEM)
ANY = pl.BlockSpec(memory_space=pl.ANY)
MIB = 2**20


def shape(dims, kind=full):
    return jax.ShapeDtypeStruct(dims, kind)


def dot(left, right, dims=NN):
    return lax.dot_general(left, right, dims, preferred_element_type=full)


def iota(dims, axis):
    return lax.broadcasted_iota(jnp.int32, dims, axis)


def hot(condition):
    return condition.astype(full).astype(half)


def call(kernel, ins, outs, scratch, micros, after=0):
    used = len(ins)

    def body(*refs):
        kernel(*refs[:used], *refs[used + after :])

    return pl.pallas_call(
        body,
        out_shape=[item[0] for item in outs],
        in_specs=ins + [ANY] * after,
        out_specs=[item[1] for item in outs],
        scratch_shapes=scratch,
        cost_estimate=pl.CostEstimate(
            flops=int(micros * 35 * 10**7), bytes_accessed=1, transcendentals=0
        ),
        compiler_params=pltpu.CompilerParams(vmem_limit_bytes=63 * MIB),
    )


def gelu_pair(values):
    square = values * values
    bent = jnp.tanh(values * (gelu_one + gelu_three * square))
    gate = 0.5 + 0.5 * bent
    slope = gate + (0.5 * values) * (1.0 - bent * bent) * (gelu_one + (3.0 * gelu_three) * square)
    return (values * gate, slope)


def adamw(weight, gradient, first, second, step_rate):
    first_new = beta_one * first + (1.0 - beta_one) * gradient
    second_new = beta_two * second + (1.0 - beta_two) * (gradient * gradient)
    second_hat = second_new * (1.0 / (1.0 - beta_two**STEP))
    root = second_hat * lax.rsqrt(second_hat) + adam_eps
    weight_new = weight * (1.0 - step_rate * weight_decay) - (
        step_rate / (1.0 - beta_one**STEP)
    ) * (first_new / root)
    return (first_new, second_new, weight_new)


def fetch(source, target, sem):
    copy = pltpu.make_async_copy(source, target, sem)
    copy.start()
    return copy


def lane_pixel(lanes):
    tap = lanes // 64
    cell = lanes % 64
    row = 4 * (cell // 8) + tap // 3 - 1
    col = 4 * (cell % 8) + tap % 3 - 1
    return (tap, row, col)


def image_kernel(planes, labels, corners, partners, out, numbers):
    count = planes.shape[1]
    tap, row, col = lane_pixel(iota((1, PLANE), 1))
    pixel = jnp.where((row >= 0) & (col >= 0) & (tap < 9), row * SIDE + col, -1)
    pick = hot(iota((SIDE * SIDE, PLANE), 0) == pixel)
    numbers[...] = jnp.zeros(numbers.shape, full)
    numbers[0:1] = labels[...].astype(full)
    numbers[1:3] = corners[...].astype(full)
    numbers[3:4] = (partners[...] // count).astype(full)
    numbers[4:5] = (partners[...] % count).astype(full)
    place = hot(iota((8, PLANE), 0) + META == iota((8, PLANE), 1))
    for colour in range(3):
        taken = dot(planes[colour], pick)
        if colour == 0:
            taken = taken + dot(numbers[...].astype(half), place, TN)
        out[:, colour * PLANE : (colour + 1) * PLANE] = taken.astype(half)


def pack_lanes(proj_c, head, norm):
    place = hot(iota((C2, WIDE), 0) == iota((C2, WIDE), 1))
    total = dot(proj_c[...].astype(half), place)
    classes = head.shape[0]
    place = hot(iota((classes, WIDE), 0) + C2 == iota((classes, WIDE), 1))
    total = total + dot(head[...].astype(half), place, TN)
    rest = norm[...]
    for part in range(3):
        piece = rest.astype(half)
        rest = rest - piece.astype(full)
        place = hot(iota((6, WIDE), 0) + (C2 + 16 + 8 * part) == iota((6, WIDE), 1))
        total = total + dot(piece, place, TN)
    return total


def cast_kernel(layer, *refs):
    ids, weights = refs[0:2]
    out, wide, narrow, in_sems, out_sems = refs[-5:]
    rows = out.shape[0]
    cols = wide.shape[1]
    parts = rows // 16
    inputs = []
    for part in range(parts):
        spot = pl.multiple_of(ids[2] * rows + part * 16, 16)
        inputs.append(
            fetch(
                weights.at[layer, pl.ds(spot, 16)],
                wide.at[part * 16 : part * 16 + 16],
                in_sems.at[part],
            )
        )
    if layer == 0:
        total = pack_lanes(*refs[2:5])
        mine = jnp.where(ids[2] == 0, total[0:rows], total[rows : 2 * rows])
        narrow[:, cols : cols + WIDE] = mine.astype(half)
    outputs = []
    for part in range(parts):
        here = slice(part * 16, part * 16 + 16)
        inputs[part].wait()
        narrow[here, 0:cols] = wide[here].astype(half)
        outputs.append(fetch(narrow.at[here], out.at[here], out_sems.at[part]))
    for copy in outputs:
        copy.wait()


def cast_half(ids, conv_w, layer, packed, after):
    rows = conv_w.shape[1] // 2
    cols = conv_w.shape[2]
    total = cols + WIDE if layer == 0 else cols
    (result,) = call(
        functools.partial(cast_kernel, layer),
        [SMEM, ANY] + [VMEM] * len(packed),
        [(shape((rows, total), half), ANY)],
        [
            pltpu.VMEM((rows, cols), full),
            pltpu.VMEM((rows, total), half),
            pltpu.SemaphoreType.DMA((rows // 16,)),
            pltpu.SemaphoreType.DMA((rows // 16,)),
        ],
        3,
        len(after),
    )(ids, conv_w, *packed, *after)
    return result


def hold_kernel(*refs):
    pass


def hold(value, after):
    return pl.pallas_call(
        hold_kernel,
        out_shape=shape(value.shape, value.dtype),
        in_specs=[ANY] * 2,
        out_specs=ANY,
        input_output_aliases={0: 0},
        compiler_params=pltpu.CompilerParams(has_side_effects=True),
        cost_estimate=pl.CostEstimate(flops=1, bytes_accessed=1, transcendentals=0),
    )(value, after)


def merge_spans(plan):
    spans = []
    for out, (size, terms) in enumerate(plan):
        edges = {0, size}
        for _, _, start, length in terms:
            edges |= {start, start + length}
        edges = sorted(edges)
        for low, high in zip(edges[:-1], edges[1:]):
            used = [
                (source, first - start)
                for source, first, start, length in terms
                if start <= low and high <= start + length
            ]
            for begin in range(low, high, 8):
                spans.append((out, begin, min(8, high - begin), used))
    return spans


def merge_kernel(plan, count, *refs):
    values = refs[:count]
    results = refs[count : count + len(plan)]
    held = refs[count + len(plan) : 2 * count + len(plan)]
    kept = refs[2 * count + len(plan) : 2 * (count + len(plan))]
    in_sems, out_sems = refs[2 * (count + len(plan)) :]
    arrivals = []
    number = 0
    for _, begin, size, used in merge_spans(plan):
        copies = []
        for source, shift in used:
            here = slice(begin + shift, begin + shift + size)
            copies.append(
                fetch(values[source].at[here], held[source].at[here], in_sems.at[number])
            )
            number += 1
        arrivals.append(copies)
    departures = []
    for (out, begin, size, used), copies in zip(merge_spans(plan), arrivals):
        for copy in copies:
            copy.wait()
        total = None
        for source, shift in used:
            value = held[source][begin + shift : begin + shift + size].astype(full)
            total = value if total is None else total + value
        here = slice(begin, begin + size)
        kept[out][here] = total.astype(half)
        departures.append(
            fetch(kept[out].at[here], results[out].at[here], out_sems.at[len(departures)])
        )
    for copy in departures:
        copy.wait()


def merge(values, plan, after, micros):
    dims = values[0].shape[1:]
    spans = merge_spans(plan)
    return call(
        functools.partial(merge_kernel, plan, len(values)),
        [ANY] * len(values),
        [(shape((size,) + dims, half), ANY) for size, _ in plan],
        [pltpu.VMEM(value.shape, half) for value in values]
        + [pltpu.VMEM((size,) + dims, half) for size, _ in plan]
        + [
            pltpu.SemaphoreType.DMA((sum(len(used) for _, _, _, used in spans),)),
            pltpu.SemaphoreType.DMA((len(spans),)),
        ],
        micros,
        len(after),
    )(*values, *after)


def pick_kernel(reach, ids, value, arrived, out, sem):
    digit = ids[3] // reach % 4
    outer = (digit == 0) | (digit == 3)

    @pl.when(outer)
    def _():
        fetch(arrived, out, sem).wait()

    @pl.when(jnp.logical_not(outer))
    def _():
        fetch(value, out, sem).wait()


def cut_kernel(places, *refs):
    count = len(places)
    outs = refs[count : 2 * count]
    sems = refs[2 * count]
    copies = []
    for index, (start, size) in enumerate(places):
        copies.append(
            fetch(refs[index].at[start : start + size], outs[index], sems.at[index])
        )
    for copy in copies:
        copy.wait()


def cut_rows(values, places, after):
    cols = values[0].shape[1]
    return call(
        functools.partial(cut_kernel, places),
        [ANY] * len(values),
        [(shape((size, cols), half), VMEM) for _, size in places],
        [pltpu.SemaphoreType.DMA((len(values),))],
        1,
        len(after),
    )(*values, *after)


def stack_kernel(places, *refs):
    count = len(places)
    out, sems = refs[count:]
    copies = []
    for index, (slot, start, size) in enumerate(places):
        copy = pltpu.make_async_copy(
            refs[index], out.at[slot, start : start + size], sems.at[index]
        )
        copy.start()
        copies.append(copy)
    for copy in copies:
        copy.wait()


def stack(pieces, places, dims, after):
    (result,) = call(
        functools.partial(stack_kernel, places),
        [ANY] * len(pieces),
        [(shape(dims, half), VMEM)],
        [pltpu.SemaphoreType.DMA((len(pieces),))],
        3,
        len(after),
    )(*pieces, *after)
    return result


def front_kernel(sizes, *refs):
    per, count, groups, devices, split = sizes
    rows = per * 64
    band = per * 8
    ids = refs[0]
    images, far_images, stem_w, proj_a, proj_b = refs[1:6]
    (
        patches,
        stem_out,
        mid_one,
        mid_two,
        act_three,
        facts,
        tiles,
        loose,
        stem_pad,
        proj_b_pad,
    ) = refs[6:]
    slot = iota((per, count), 0)
    column = iota((per, count), 1)
    own = dot(hot(column == slot + ids[0] * per), images[0])
    group_of = own[:, META + 3 : META + 4].astype(jnp.int32)
    local_of = own[:, META + 4 : META + 5].astype(jnp.int32)
    turn_of = group_of ^ ids[1]
    other = jnp.zeros((per, 3 * PLANE), full)
    for turn in range(groups):
        source = far_images[turn // 2] if turn % 2 else images[turn // 2]
        other = other + dot(hot((turn_of == turn) & (column == local_of)), source)
    top = own[:, META + 1 : META + 2]
    left = own[:, META + 2 : META + 3]
    tap, row, col = lane_pixel(iota((1, 3 * PLANE), 1) % PLANE)
    row = row.astype(full)
    col = col.astype(full)
    inside = (row >= top) & (row < top + CUT) & (col >= left) & (col < left + CUT) & (tap < 9)
    blended = jnp.where(inside, other, own)
    tall = jnp.maximum(jnp.minimum(top + CUT, float(SIDE)) - jnp.maximum(top, 0.0), 0.0)
    broad = jnp.maximum(jnp.minimum(left + CUT, float(SIDE)) - jnp.maximum(left, 0.0), 0.0)
    share = 1.0 - tall * broad / float(SIDE * SIDE)
    lanes = iota((per, 128), 1)
    facts[...] = jnp.where(
        lanes == 0,
        own[:, META : META + 1],
        jnp.where(lanes == 1, other[:, META : META + 1], share),
    )
    tiles[...] = jnp.zeros(tiles.shape, full)
    for piece in range(15):
        tiles[:, piece, :] = blended[:, piece * 128 : (piece + 1) * 128]
    tiles[:, 16:32, :] = pltpu.roll(tiles[:, 0:16, :], 64, 2)
    spot = iota((32, 32), 0)
    tap_at = ((spot % 16) % 5) * 2 + spot // 16
    colour_at = (spot % 16) // 5
    order = hot(
        (iota((32, 32), 1) == tap_at * 3 + colour_at) & (tap_at < 9) & (spot % 16 < 15)
    )
    for image in range(per):
        cells = dot(tiles[image].astype(half), order, TN)
        for line in range(8):
            loose[line * band + image * 8 : line * band + image * 8 + 8, :] = cells[
                line * 8 : line * 8 + 8
            ]
    patches[...] = loose[...].astype(half)
    stem_pad[...] = jnp.zeros(stem_pad.shape, full)
    stem_pad[:, 0:27] = stem_w[...]
    proj_b_pad[...] = jnp.zeros(proj_b_pad.shape, half)
    proj_b_pad[:, 0:C2] = proj_b[...].astype(half)
    stem_half = stem_pad[...].astype(half)
    proj_a_half = proj_a[...].astype(half)
    tall_chunk = 2 * band

    def step(index, carry):
        at = pl.ds(pl.multiple_of(index * tall_chunk, 16), tall_chunk)
        stem = dot(patches[at], stem_half, NT)
        stem_out[at] = stem
        one = dot(gelu_pair(stem)[0].astype(half), proj_a_half)
        mid_one[at] = one
        two = dot(gelu_pair(one)[0].astype(half), proj_b_pad[...])
        mid_two[at] = two
        act_three[at] = gelu_pair(two)[0].astype(half)
        return carry

    lax.fori_loop(0, rows // tall_chunk, step, 0)


def base_kernel(*refs):
    ids, act_three = refs[0:2]
    pieces = refs[2:12]
    base, stats, norm_rows, head_all, proj_t, gathered, held, totals, sems, out_sems = refs[12:]
    rows = act_three.shape[0]
    lanes = pl.ds(pieces[0].shape[1] - WIDE, WIDE)
    for copy in start_weights(ids, pieces, gathered, sems, lanes):
        copy.wait()
    column = iota((1, WIDE), 1)
    packed = gathered[...]
    proj_t[...] = jnp.where(column < C2, packed.astype(full), 0.0).astype(half)
    place = hot(iota((WIDE, 16), 0) == iota((WIDE, 16), 1) + C2)
    head_all[...] = dot(packed, place).astype(half)
    column = iota((8, WIDE), 1)
    name = iota((8, WIDE), 0)
    pieces = [
        dot(hot((column == name + (C2 + 16 + 8 * part)) & (name < 6)), packed, NT)
        for part in range(3)
    ]
    norm_rows[...] = pieces[0] + (pieces[1] + pieces[2])
    totals[...] = jnp.zeros(totals.shape, full)
    outputs = []
    for part in range(QUARTERS):
        at = quarter_rows(rows, part)
        result = dot(act_three[at], proj_t[...], NT)
        held[at] = result
        outputs.append(fetch(held.at[at], base.at[at], out_sems.at[part]))
        totals[0:1] += jnp.sum(result, axis=0, keepdims=True)
        totals[1:2] += jnp.sum(result * result, axis=0, keepdims=True)
    spread_stats(stats, [totals[0:1], totals[1:2]])
    for copy in outputs:
        copy.wait()


def spread_stats(out, parts):
    line = jnp.concatenate(parts, axis=1)
    out[...] = jnp.broadcast_to(line[None], out.shape)


def moments(stats, row_total):
    line = jnp.sum(stats[...], axis=0)
    mean = line[:, 0:C3] / row_total
    rstd = lax.rsqrt(line[:, C3 : 2 * C3] / row_total - mean * mean + norm_eps)
    return (mean, rstd)


def quarter_rows(rows, part):
    step = rows // QUARTERS
    return pl.ds(part * step, step)


def fetch_quarter(source, target, sem, part):
    here = quarter_rows(source.shape[0], part)
    return fetch(source.at[here], target.at[here], sem)


def walk_quarter(rows, part, body, carry):
    step = rows // QUARTERS // CHUNK
    return lax.fori_loop(part * step, (part + 1) * step, body, carry)


def start_weights(ids, pieces, weights, sems, lanes=pl.ds(0, 9 * C3)):
    rows = pieces[0].shape[0]
    low = pieces[3].shape[0]
    copies = []
    for side in range(2):
        for place in range(5):
            piece = pieces[5 * side + place]
            turn = min(place, 3)
            spot = (ids[0] ^ turn) * (2 * rows) + (ids[2] ^ side) * rows
            if place == 4:
                spot = spot + low
            spot = pl.multiple_of(spot, 16)
            copies.append(
                fetch(
                    piece.at[:, lanes],
                    weights.at[pl.ds(spot, piece.shape[0])],
                    sems.at[5 * side + place],
                )
            )
    return copies


def shifted(values, by):
    block = values.reshape(CHUNK // 8, 8, C3)
    place = iota((1, 8, 1), 1)
    if by == 1:
        moved = jnp.where(place == 0, 0.0, pltpu.roll(block, 1, 1))
    else:
        moved = jnp.where(place == 7, 0.0, pltpu.roll(block, 7, 1))
    return moved.reshape(CHUNK, C3)


def conv_kernel(sizes, layer, *refs):
    per, row_total, split = sizes
    rows = per * 64
    band = per * 8
    ids, source, stats_in, norm_rows = refs[0:4]
    offset = 4
    if layer == 1:
        base = refs[4]
        offset = 5
    pieces = refs[offset : offset + 10]
    offset += 10
    (result, field_out, slope_out, stats, held, weights, field, slope, total) = refs[
        offset : offset + 9
    ]
    weight_sems, in_sems, out_sems = refs[offset + 9 : offset + 12]
    inputs = [fetch_quarter(source, held, in_sems.at[part], part) for part in range(QUARTERS)]
    copies = start_weights(ids, pieces, weights, weight_sems)
    mean, rstd = moments(stats_in, row_total)
    factor = rstd * norm_rows[2 * layer : 2 * layer + 1]
    shift = norm_rows[2 * layer + 1 : 2 * layer + 2] - mean * factor

    def prepare(index, carry):
        at = pl.ds(pl.multiple_of(index * CHUNK, 16), CHUNK)
        value, gradient = gelu_pair(held[at] * factor + shift)
        slope[at] = gradient
        field[at, 0:C3] = shifted(value, 1).astype(half)
        field[at, C3 : 2 * C3] = value.astype(half)
        field[at, 2 * C3 : TRIPLE] = shifted(value, -1).astype(half)
        return carry

    for part in range(QUARTERS):
        inputs[part].wait()
        walk_quarter(rows, part, prepare, 0)
    outputs = [
        fetch(field.at[:, C3 : 2 * C3], field_out, out_sems.at[QUARTERS]),
        fetch(slope, slope_out, out_sems.at[QUARTERS + 1]),
    ]
    if layer == 1:
        inputs = [fetch_quarter(base, held, in_sems.at[part], part) for part in range(QUARTERS)]
    for copy in copies:
        copy.wait()
    inner = rows - band
    total[...] = dot(field[...], weights[:, TRIPLE : 2 * TRIPLE], NT)
    total[band:rows] += dot(field[0:inner], weights[:, 0:TRIPLE], NT)
    total[0:inner] += dot(field[band:rows], weights[:, 2 * TRIPLE : 3 * TRIPLE], NT)

    def count(index, carry):
        at = pl.ds(pl.multiple_of(index * CHUNK, 16), CHUNK)
        value = total[at]
        if layer == 1:
            value = value + held[at]
            total[at] = value
        return (
            carry[0] + jnp.sum(value.reshape(CHUNK // 8, 8, C3), axis=0),
            carry[1] + jnp.sum((value * value).reshape(CHUNK // 8, 8, C3), axis=0),
        )

    zero = jnp.zeros((8, C3), full)
    sums = (zero, zero)
    for part in range(QUARTERS):
        if layer == 1:
            inputs[part].wait()
        else:
            outputs.append(fetch_quarter(total, result, out_sems.at[part], part))
        sums = walk_quarter(rows, part, count, sums)
        if layer == 1:
            outputs.append(fetch_quarter(total, result, out_sems.at[part], part))
    spread_stats(stats, [jnp.sum(item, axis=0, keepdims=True) for item in sums])
    for copy in outputs:
        copy.wait()


def head_kernel(sizes, *refs):
    per, row_total, image_total, classes = sizes
    rows = per * 64
    band = per * 8
    (
        summed,
        stats_in,
        norm_rows,
        head_all,
        facts,
        slope,
        spread,
        stats,
        grad_head,
        sum_value,
        sum_slope,
        sum_cross,
    ) = refs
    mean, rstd = moments(stats_in, row_total)
    gain = norm_rows[4:5]
    bias = norm_rows[5:6]
    sum_value[...] = jnp.zeros((band, C3), full)
    sum_slope[...] = jnp.zeros((band, C3), full)
    sum_cross[...] = jnp.zeros((band, C3), full)

    def walk(index, carry):
        for part in range(band // CHUNK):
            at = pl.ds(pl.multiple_of(index * band + part * CHUNK, 16), CHUNK)
            here = slice(part * CHUNK, part * CHUNK + CHUNK)
            unit = (summed[at] - mean) * rstd
            value, gradient = gelu_pair(unit * gain + bias)
            slope[at] = gradient
            sum_value[here] += value
            sum_slope[here] += gradient
            sum_cross[here] += gradient * unit
        return carry

    lax.fori_loop(0, 8, walk, 0)

    def by_image(ref):
        return jnp.sum(ref[...].reshape(per, 8, C3), axis=1)

    pooled = (by_image(sum_value) / 64.0).astype(half)
    logits = dot(pooled, head_all[...])
    lanes = iota((per, 16), 1)
    inside = lanes < classes
    own = facts[:, 0:1].astype(jnp.int32)
    other = facts[:, 1:2].astype(jnp.int32)
    share = facts[:, 2:3]
    target = jnp.where(lanes == own, share, 0.0) + jnp.where(lanes == other, 1.0 - share, 0.0)
    top = jnp.max(jnp.where(inside, logits, -3e38), axis=1, keepdims=True)
    powers = jnp.where(inside, jnp.exp(jnp.where(inside, logits - top, 0.0)), 0.0)
    lse = top + jnp.log(jnp.sum(powers, axis=1, keepdims=True))
    losses = lse - jnp.sum(target * logits, axis=1, keepdims=True)
    loss = jnp.sum(losses, axis=0, keepdims=True)
    soft = jnp.where(inside, jnp.exp(jnp.where(inside, logits - lse, 0.0)), 0.0)
    grad_logits = ((soft - target) / image_total).astype(half)
    grad_head[...] = dot(pooled, grad_logits, TN)
    pull = dot(grad_logits, head_all[...], NT) / 64.0
    spread[...] = jnp.broadcast_to(pull[:, None, :], (per, 8, C3)).reshape(band, C3)
    bias_sum = jnp.sum(pull * by_image(sum_slope), axis=0, keepdims=True)
    gain_sum = jnp.sum(pull * by_image(sum_cross), axis=0, keepdims=True)
    spread_stats(stats, [bias_sum, gain_sum, jnp.broadcast_to(loss, (1, 128))])


def grad_moments(stats, row_total):
    line = jnp.sum(stats[...], axis=0)
    return (line[:, 0:C3] / row_total, line[:, C3 : 2 * C3] / row_total)


def input_grad(gradient, weights, out, band):
    rows = gradient.shape[0]
    inner = rows - band
    spans = (
        (1, slice(0, rows), slice(0, rows)),
        (0, slice(0, inner), slice(band, rows)),
        (2, slice(band, rows), slice(0, inner)),
    )
    for line, to, of in spans:
        for col in range(3):
            tap = 3 * line + col
            part = dot(
                gradient[of, col * C3 : (col + 1) * C3], weights[:, tap * C3 : (tap + 1) * C3]
            )
            if line == 1 and col == 0:
                out[to] = part
            else:
                out[to] += part


def half_filters(ids, split):
    tall = C3 // (2 * split)
    place = iota((1, 2 * WIDE), 1)
    side = jnp.where(place < WIDE, 0, 1)
    place = place - side * WIDE
    target = (ids[0] ^ (place // tall)) * (2 * tall) + (ids[2] ^ side) * tall + place % tall
    target = jnp.where(place < C3 // 2, target, -1)
    return hot(iota((C3, 2 * WIDE), 0) == target)


def norm_back(arriving, unit, factor, low, high):
    return factor * (arriving - low - unit * high)


def send_halves(middle, pick, helds, halves, sems, part):
    here = quarter_rows(helds[0].shape[0], part)
    both = dot(middle, pick).astype(half)
    copies = []
    for side in range(2):
        helds[side][here] = both[:, side * WIDE : (side + 1) * WIDE]
        copies.append(
            fetch(helds[side].at[here], halves[side].at[here], sems.at[2 * part + side])
        )
    return copies


def back_kernel(sizes, layer, *refs):
    per, row_total, split = sizes
    rows = per * 64
    band = per * 8
    last = layer == 1
    ids = refs[0]
    if last:
        incoming, source, stats_here, stats_grad, norm_rows, spread = refs[1:7]
        offset = 7
    else:
        incoming = refs[1]
        offset = 2
    before, slope_before, stats_before = refs[offset : offset + 3]
    pieces = refs[offset + 3 : offset + 13]
    result, stats = refs[offset + 13 : offset + 15]
    offset += 15
    if last:
        own_half, far_half, grad_out, kept, own_held, far_held, pick, half_sems = refs[
            offset : offset + 8
        ]
        offset += 8
    else:
        arrived = refs[offset]
        offset += 1
    held, origin, weights, gradient, total = refs[offset : offset + 5]
    weight_sems, in_sems, out_sems = refs[offset + 5 : offset + 8]
    inputs = []
    for part in range(QUARTERS):
        if last:
            inputs.append(
                (
                    fetch_quarter(incoming, held, in_sems.at[2 * part], part),
                    fetch_quarter(source, origin, in_sems.at[2 * part + 1], part),
                )
            )
        else:
            inputs.append((fetch_quarter(incoming, arrived, in_sems.at[2 * part], part),))
    copies = start_weights(ids, pieces, weights, weight_sems)
    if last:
        mean, rstd = moments(stats_here, row_total)
        low, high = grad_moments(stats_grad, row_total)
        factor = rstd * norm_rows[4:5]
        parts = band // CHUNK
        pick[...] = half_filters(ids, split)

    def prepare(index, carry):
        at = pl.ds(pl.multiple_of(index * CHUNK, 16), CHUNK)
        if last:
            here = pl.ds(pl.multiple_of(lax.rem(index, parts) * CHUNK, 16), CHUNK)
            unit = (origin[at] - mean) * rstd
            value = norm_back(held[at] * spread[here], unit, factor, low, high)
            kept[at] = value
            gradient[at, C3 : 2 * C3] = value.astype(half)
        else:
            gradient[at, C3 : 2 * C3] = arrived[at]
            value = arrived[at].astype(full)
        gradient[at, 0:C3] = shifted(value, -1).astype(half)
        gradient[at, 2 * C3 : TRIPLE] = shifted(value, 1).astype(half)
        return carry

    for part in range(QUARTERS):
        for copy in inputs[part]:
            copy.wait()
        walk_quarter(rows, part, prepare, 0)
    outputs = []
    if last:
        outputs.append(fetch(kept, grad_out, half_sems.at[2 * QUARTERS]))
        for part in range(QUARTERS):
            outputs += send_halves(
                gradient[quarter_rows(rows, part), C3 : 2 * C3],
                pick[...],
                (own_held, far_held),
                (own_half, far_half),
                half_sems,
                part,
            )
    inputs = []
    for part in range(QUARTERS):
        inputs.append(
            (
                fetch_quarter(before, origin, in_sems.at[2 * part], part),
                fetch_quarter(slope_before, held, in_sems.at[2 * part + 1], part),
            )
        )
    for copy in copies:
        copy.wait()
    input_grad(gradient, weights, total, band)
    mean, rstd = moments(stats_before, row_total)

    def finish(index, carry):
        at = pl.ds(pl.multiple_of(index * CHUNK, 16), CHUNK)
        value = total[at] * held[at]
        total[at] = value
        unit = (origin[at] - mean) * rstd
        return (
            carry[0] + jnp.sum(value.reshape(CHUNK // 8, 8, C3), axis=0),
            carry[1] + jnp.sum((value * unit).reshape(CHUNK // 8, 8, C3), axis=0),
        )

    zero = jnp.zeros((8, C3), full)
    sums = (zero, zero)
    for part in range(QUARTERS):
        for copy in inputs[part]:
            copy.wait()
        sums = walk_quarter(rows, part, finish, sums)
        outputs.append(fetch_quarter(total, result, out_sems.at[part], part))
    spread_stats(stats, [jnp.sum(item, axis=0, keepdims=True) for item in sums])
    for copy in outputs:
        copy.wait()


def norm_back_kernel(sizes, *refs):
    row_total, split = sizes
    ids, incoming, source, stats_here, stats_grad, norm_rows = refs[0:6]
    grad_half, own_half, far_half = refs[6:9]
    held, origin, middle, own_held, far_held, pick, in_sems, out_sems = refs[9:]
    rows = held.shape[0]
    inputs = []
    for part in range(QUARTERS):
        inputs.append(
            (
                fetch_quarter(incoming, held, in_sems.at[2 * part], part),
                fetch_quarter(source, origin, in_sems.at[2 * part + 1], part),
            )
        )
    mean, rstd = moments(stats_here, row_total)
    low, high = grad_moments(stats_grad, row_total)
    factor = rstd * norm_rows[2:3]
    pick[...] = half_filters(ids, split)

    def prepare(index, carry):
        at = pl.ds(pl.multiple_of(index * CHUNK, 16), CHUNK)
        unit = (origin[at] - mean) * rstd
        middle[at] = norm_back(held[at], unit, factor, low, high).astype(half)
        return carry

    outputs = []
    for part in range(QUARTERS):
        for copy in inputs[part]:
            copy.wait()
        walk_quarter(rows, part, prepare, 0)
        here = quarter_rows(rows, part)
        outputs.append(fetch(middle.at[here], grad_half.at[here], out_sems.at[8 + part]))
        outputs += send_halves(
            middle[here], pick[...], (own_held, far_held), (own_half, far_half), out_sems, part
        )
    for copy in outputs:
        copy.wait()


def weight_grad_kernel(sizes, *refs):
    chunks, split, band = sizes
    gradients = refs[0:2]
    fields = refs[2:4]
    count = sum(len(part_sizes(split, lines)) for lines in chunks)
    outs = refs[4 : 4 + count]
    (gradient, field, plain, held, in_sems, grad_sems, sems) = refs[4 + count :]
    inputs = []
    for line in range(8):
        for side in range(2):
            of = pl.ds(line * band, band)
            inputs.append(
                fetch(fields[side].at[of], plain.at[side, of], in_sems.at[2 * line + side])
            )
    arriving = []
    for line in range(8):
        for side in range(2):
            of = pl.ds(line * band, band)
            to = pl.ds((2 * line + side) * band, band)
            arriving.append(
                fetch(gradients[side].at[of], gradient.at[to], grad_sems.at[2 * line + side])
            )

    def prepare(index, carry):
        for side in range(2):
            for part in range(band // CHUNK):
                to = pl.ds(
                    pl.multiple_of((2 * index + side) * band + part * CHUNK, 16), CHUNK
                )
                of = pl.ds(pl.multiple_of(index * band + part * CHUNK, 16), CHUNK)
                value = plain[side, of]
                wide = value.astype(full)
                field[to, 0:C3] = shifted(wide, 1).astype(half)
                field[to, C3 : 2 * C3] = value
                field[to, 2 * C3 : TRIPLE] = shifted(wide, -1).astype(half)
        return carry

    for part in range(QUARTERS):
        for copy in inputs[4 * part : 4 * part + 4]:
            copy.wait()
        lax.fori_loop(2 * part, 2 * part + 2, prepare, 0)
    for copy in arriving:
        copy.wait()
    rows = field.shape[0]
    inner = rows - 2 * band
    spans = {
        0: (slice(2 * band, rows), slice(0, inner)),
        1: (slice(0, rows), slice(0, rows)),
        2: (slice(0, inner), slice(2 * band, rows)),
    }
    tall = held.shape[2]
    copies = []
    start = 0
    number = 0
    for lines in chunks:
        for place, line in enumerate(lines):
            left, right = spans[line]
            part = dot(gradient[left, 0 : C3 // 2], field[right], TN).astype(half)
            for turn in range(split):
                for block in range(15):
                    held[turn, start + place * 15 + block] = part[
                        turn * tall : (turn + 1) * tall, block * 128 : (block + 1) * 128
                    ]
        for turn, first, size in part_sizes(split, lines):
            copies.append(
                fetch(
                    held.at[turn, start + first : start + first + size],
                    outs[number],
                    sems.at[number],
                )
            )
            number += 1
        start += 15 * len(lines)
    for copy in copies:
        copy.wait()


def part_sizes(split, lines):
    blocks = 15 * len(lines)
    sizes = [(turn, 0, blocks) for turn in range(split - 1)]
    return sizes + [(split - 1, 0, blocks // 2), (split - 1, blocks // 2, blocks - blocks // 2)]


def trunk_kernel(sizes, *refs):
    per, row_total, split = sizes
    rows = per * 64
    band = per * 8
    (
        ids,
        incoming,
        grad_summed,
        base,
        stats_one,
        stats_six,
        norm_rows,
        proj_t,
        act_three,
        mid_two,
        mid_one,
        stem_out,
        patches,
        proj_a,
        proj_b,
        grad_head,
        mine,
        other,
        trunk,
        grad_two,
        act_two,
        grad_one,
        act_one,
        grad_stem,
        proj_b_pad,
        split_part,
        shared_part,
        sems,
    ) = refs
    mean, rstd = moments(stats_one, row_total)
    low, high = grad_moments(stats_six, row_total)
    factor = rstd * norm_rows[0:1]
    proj_b_pad[...] = jnp.zeros(proj_b_pad.shape, half)
    proj_b_pad[:, 0:C2] = proj_b[...].astype(half)
    proj_a_half = proj_a[...].astype(half)

    def prepare(index, carry):
        at = pl.ds(pl.multiple_of(index * CHUNK, 16), CHUNK)
        unit = (base[at] - mean) * rstd
        value = grad_summed[at] + factor * (incoming[at] - low - unit * high)
        trunk[at] = value.astype(half)
        return carry

    lax.fori_loop(0, rows // CHUNK, prepare, 0)
    tall_chunk = 2 * band

    def step(index, carry):
        at = pl.ds(pl.multiple_of(index * tall_chunk, 16), tall_chunk)
        three = dot(trunk[at], proj_t[...])
        two = (three * gelu_pair(mid_two[at])[1]).astype(half)
        grad_two[at] = two
        value, slope = gelu_pair(mid_one[at])
        act_two[at] = value.astype(half)
        one = (dot(two, proj_b_pad[...], NT) * slope).astype(half)
        grad_one[at] = one
        value, slope = gelu_pair(stem_out[at])
        act_one[at] = value.astype(half)
        grad_stem[at] = (dot(one, proj_a_half, NT) * slope).astype(half)
        return carry

    lax.fori_loop(0, rows // tall_chunk, step, 0)
    place = hot(iota((16, WIDE), 0) + C2 == iota((16, WIDE), 1))
    split_part[...] = (
        dot(trunk[...], act_three[...], TN) + dot(grad_head[...].astype(half), place)
    ).astype(half)
    shared = dot(act_two[...], grad_two[...], TN)
    shared = shared + dot(dot(grad_one[...], act_one[...], TN).astype(half), place)
    stem = dot(patches[...], grad_stem[...], TN).astype(half)
    tall = split_part.shape[0] // (2 * split)
    spot = iota((C1, 32), 0)
    twice = hot((spot % tall == iota((C1, 32), 1)) & (spot % tall < 27))
    place = hot(iota((16, WIDE), 0) + (C2 + 16) == iota((16, WIDE), 1))
    shared = shared + dot(dot(twice, stem).astype(half), place)
    shared_part[...] = shared.astype(half)
    copies = []
    for turn in range(split):
        for side, target in ((0, mine), (1, other)):
            place = pl.multiple_of((ids[2] ^ side) * tall, 16)
            spot = pl.multiple_of((ids[0] ^ turn) * (2 * tall) + (ids[2] ^ side) * tall, 16)
            number = 2 * (2 * turn + side)
            copy = pltpu.make_async_copy(
                split_part.at[pl.ds(spot, tall)], target.at[turn, 0:tall], sems.at[number]
            )
            copy.start()
            copies.append(copy)
            copy = pltpu.make_async_copy(
                shared_part.at[pl.ds(place, tall)],
                target.at[turn, tall : 2 * tall],
                sems.at[number + 1],
            )
            copy.start()
            copies.append(copy)
    for copy in copies:
        copy.wait()


def norm_kernel(sizes, *refs):
    devices, chips, split = sizes
    ids, one, two, small, stats_six, stats_five, stats_four, line, local, loss, norm_out = refs
    digit = ids[3] // (chips // 4) % 4
    inner = (digit == 1) | (digit == 2)

    def walk(block, total):
        first = one[block].astype(full)
        second = two[block].astype(full)
        return total + (first * first + second * second)

    squares = lax.fori_loop(0, one.shape[0], walk, jnp.zeros(one.shape[1:], full))
    squares = jnp.sum(jnp.sum(squares, axis=0, keepdims=True), axis=1, keepdims=True)
    total = jnp.where(inner, squares / (chips // 2), 0.0)
    tall = small.shape[0] // 2
    value = small[...].astype(full)
    row = iota(value.shape, 0)
    lane = iota(value.shape, 1)
    share = jnp.where(
        row < tall,
        1.0 / chips,
        jnp.where(lane < C2 + 16, 1.0 / (chips * split), 1.0 / (2 * chips * split)),
    )
    value = jnp.where(inner, 2.0 * value * value * share, 0.0)
    total = total + jnp.sum(jnp.sum(value, axis=0, keepdims=True), axis=1, keepdims=True)
    norm_out[...] = jnp.zeros(norm_out.shape, full)
    for place, stats in enumerate((stats_six, stats_five, stats_four)):
        sums = jnp.sum(stats[...], axis=0)
        norm_out[2 * place : 2 * place + 1] = sums[:, C3 : 2 * C3]
        norm_out[2 * place + 1 : 2 * place + 2] = sums[:, 0:C3]
        if place == 2:
            loss[...] = sums[:, 2 * C3 : 2 * C3 + 128]
    value = norm_out[...]
    local[...] = pltpu.roll(value, C3 - ids[0] * (C3 // split), 1)[0:6, 0 : C3 // split]
    value = value * value / devices
    total = total + jnp.sum(jnp.sum(value, axis=0, keepdims=True), axis=1, keepdims=True)
    line[...] = jnp.broadcast_to(total[None], line.shape)


def clip_scale(squares):
    total = jnp.sum(jnp.sum(squares[...], axis=0), axis=1, keepdims=True)
    size = jnp.sqrt(total[:, 0:1] / 128.0)
    return (size, jnp.minimum(1.0, clip_limit / size))


def conv_update_kernel(sizes, *refs):
    pieces_count, places, step_rate = sizes
    ids = refs[0]
    squares, weight, first, second = refs[1:5]
    pieces = refs[5 : 5 + pieces_count]
    (first_new, second_new, weight_new, held, sems) = refs[5 + pieces_count :]
    layer = pl.program_id(0)
    line = pl.program_id(1)

    def copies(wanted):
        made = []
        for number, (owner, start, size, side) in enumerate(places):
            if owner not in wanted:
                continue
            tall = pieces[number].shape[1]
            row = pl.multiple_of((ids[2] ^ side) * tall, 16)
            made.append(
                pltpu.make_async_copy(
                    pieces[number],
                    held.at[owner, start : start + size, pl.ds(row, tall), :],
                    sems.at[number],
                )
            )
        return made

    @pl.when((layer == 0) & (line == 0))
    def _():
        for copy in copies((0, 1)):
            copy.start()

    for owner in range(2):

        @pl.when((layer == owner) & (line == 0))
        def _():
            for copy in copies((owner,)):
                copy.wait()

    size, scale = clip_scale(squares)
    for part in range(9):
        lanes = slice(part * 128, part * 128 + 128)
        block = line * 9 + part
        gradient = held[layer, block].astype(full) * scale
        results = adamw(
            weight[0, :, lanes], gradient, first[0, :, lanes], second[0, :, lanes], step_rate
        )
        first_new[0, :, lanes] = results[0]
        second_new[0, :, lanes] = results[1]
        weight_new[0, :, lanes] = results[2]


def small_update_kernel(rates, *refs):
    ids, squares, mine, other, grad_norm_p = refs[0:5]
    states = refs[5:23]
    outs = refs[23:41]
    size_out = refs[41]
    size, scale = clip_scale(squares)
    size_out[...] = jnp.broadcast_to(size, size_out.shape)
    first_core = ids[2] == 0
    tall = mine.shape[0] // 2
    here = mine[...].astype(full)
    there = other[...].astype(full)
    even = jnp.where(first_core, here, there)
    odd = jnp.where(first_core, there, here)
    split_part = jnp.concatenate([even[0:tall], odd[0:tall]], axis=0).astype(half)
    shared = jnp.concatenate([even[tall:], odd[tall:]], axis=0).astype(half)
    grad_c = split_part[:, 0:C2].astype(full)
    classes = states[12].shape[0]
    pick = hot(iota((classes, WIDE), 0) + C2 == iota((classes, WIDE), 1))
    grad_head = dot(pick, split_part, NT)
    grad_b = shared[:, 0:C2].astype(full)
    pick = hot(iota((C0, WIDE), 0) + C2 == iota((C0, WIDE), 1))
    grad_a = dot(pick, shared, NT)
    pick = hot(iota((C0, WIDE), 0) + (C2 + 16) == iota((C0, WIDE), 1))
    grad_stem = dot(pick, shared[0:32], NT)[:, 0:27]
    gradients = (grad_stem, grad_a, grad_b, grad_c, grad_head, grad_norm_p[...])
    for index in range(6):
        weight, first, second = states[3 * index : 3 * index + 3]
        results = adamw(
            weight[...], gradients[index] * scale, first[...], second[...], rates[index]
        )
        for item in range(3):
            outs[3 * index + item][...] = results[item]


def xor_pairs(size, turn):
    return [(index, index ^ turn) for index in range(size)]


def shards(
    images,
    labels,
    corners,
    partners,
    stem_w,
    stem_w_m,
    stem_w_v,
    proj_a,
    proj_a_m,
    proj_a_v,
    proj_b,
    proj_b_m,
    proj_b_v,
    proj_c,
    proj_c_m,
    proj_c_v,
    conv_w,
    conv_w_m,
    conv_w_v,
    head_w,
    head_w_m,
    head_w_v,
    norm_p,
    norm_p_m,
    norm_p_v,
):
    split = lax.axis_size("dp")
    groups = lax.axis_size("filt")
    chips = groups // 2
    devices = split * groups
    count = images.shape[0]
    per = count // split
    rows = per * 64
    band = per * 8
    image_total = float(count * groups)
    row_total = image_total * 64.0
    tall = conv_w.shape[1] // 2
    spot_d = lax.axis_index("dp")
    spot_f = lax.axis_index("filt")
    ids = jnp.stack([spot_d, spot_f, spot_f % 2, spot_f // 2]).astype(jnp.int32)

    def over_dp(value, turn):
        return lax.ppermute(value, "dp", xor_pairs(split, turn))

    def over_filt(value, turn):
        return lax.ppermute(value, "filt", xor_pairs(groups, turn))

    def exchange(stats):
        return lax.all_to_all(stats, ("dp", "filt"), 0, 0)

    (own_images,) = call(
        image_kernel,
        [VMEM] * 4,
        [(shape((count, 3 * PLANE), half), VMEM)],
        [pltpu.VMEM((8, count), full)],
        3,
    )(
        images.transpose(1, 0, 2),
        labels.reshape(1, count),
        corners.T,
        partners.reshape(1, count),
    )
    far_images = [own_images] + [over_filt(own_images, 2 * turn) for turn in range(1, chips)]

    def start_gather(own):
        return [own, over_dp(own, 1), over_dp(own, 2)]

    def middle_gather(pieces, after):
        rows = pieces[0].shape[0]
        return cut_rows(pieces[:0:-1], [(0, 48), (48, rows - 48)], after)

    def end_gather(pieces, far, after=()):
        far = [over_dp(far[0], 1), over_dp(far[1], 2)]
        if after:
            far = cut_rows(far, [(0, piece.shape[0]) for piece in far], after)
        pieces = [*pieces, *far]
        return pieces + [over_filt(piece, 1) for piece in pieces]

    own_one = cast_half(ids, conv_w, 0, [proj_c.T, head_w.T, norm_p], [own_images])
    own_two = cast_half(ids, conv_w, 1, [], [own_one])
    pieces = start_gather(own_one)
    far = middle_gather(pieces, [])
    all_images = stack(
        far_images,
        [(turn, 0, count) for turn in range(chips)],
        (chips, count, 3 * PLANE),
        [own_two],
    )

    line = shape((devices, 1, 2 * C3))
    patches, stem_out, mid_one, mid_two, act_three, facts = call(
        functools.partial(front_kernel, (per, count, groups, devices, split)),
        [SMEM] + [VMEM] * 5,
        [
            (shape((rows, 32), half), VMEM),
            (shape((rows, C0)), VMEM),
            (shape((rows, C1)), VMEM),
            (shape((rows, WIDE)), VMEM),
            (shape((rows, WIDE), half), VMEM),
            (shape((per, 128)), VMEM),
        ],
        [
            pltpu.VMEM((per, 32, 128), full),
            pltpu.VMEM((rows, 32), full),
            pltpu.VMEM((C0, 32), full),
            pltpu.VMEM((C1, WIDE), half),
        ],
        10,
        1,
    )(ids, all_images, over_filt(all_images, 1), stem_w.T, proj_a, proj_b, far[0])
    kernels = [end_gather(pieces, far, [facts])]
    base, stats, norm_rows, head_all, proj_t = call(
        base_kernel,
        [SMEM, VMEM] + [ANY] * 10,
        [
            (shape((rows, C3)), ANY),
            (line, VMEM),
            (shape((8, C3)), VMEM),
            (shape((C3, 16), half), VMEM),
            (shape((C3, WIDE), half), VMEM),
        ],
        [
            pltpu.VMEM((C3, WIDE), half),
            pltpu.VMEM((rows, C3), full),
            pltpu.VMEM((8, C3), full),
            pltpu.SemaphoreType.DMA((10,)),
            pltpu.SemaphoreType.DMA((QUARTERS,)),
        ],
        4,
    )(ids, act_three, *kernels[0])
    stats_one = exchange(stats)
    pieces = start_gather(hold(own_two, stats_one))

    table = pltpu.VMEM((rows, C3), full)
    conv_outs = [
        (shape((rows, C3)), ANY),
        (shape((rows, C3), half), ANY),
        (shape((rows, C3)), ANY),
        (line, VMEM),
    ]
    conv_scratch = [
        table,
        pltpu.VMEM((C3, 9 * C3), half),
        pltpu.VMEM((rows, TRIPLE), half),
        table,
        table,
        pltpu.SemaphoreType.DMA((10,)),
        pltpu.SemaphoreType.DMA((QUARTERS,)),
        pltpu.SemaphoreType.DMA((QUARTERS + 2,)),
    ]
    conv_one, field_one, slope_one, stats = call(
        functools.partial(conv_kernel, (per, row_total, split), 0),
        [SMEM, ANY, VMEM, VMEM] + [ANY] * 10,
        conv_outs,
        conv_scratch,
        18,
    )(ids, base, stats_one, norm_rows, *kernels[0])
    far = middle_gather(pieces, [stats])
    stats_two = exchange(stats)
    kernels.append(end_gather(pieces, far, [stats_two]))
    far_field_one = over_filt(field_one, 1)
    summed, field_two, slope_two, stats = call(
        functools.partial(conv_kernel, (per, row_total, split), 1),
        [SMEM, ANY, VMEM, VMEM, ANY] + [ANY] * 10,
        conv_outs,
        conv_scratch,
        18,
    )(ids, conv_one, stats_two, norm_rows, base, *kernels[1])
    stats_three = exchange(stats)
    far_field_two = over_filt(field_two, 1)
    slope_three, spread, stats, grad_head = call(
        functools.partial(head_kernel, (per, row_total, image_total, head_w.shape[1])),
        [VMEM] * 5,
        [
            (shape((rows, C3)), VMEM),
            (shape((band, C3)), VMEM),
            (shape((devices, 1, 2 * C3 + 128)), VMEM),
            (shape((C3, 16)), VMEM),
        ],
        [pltpu.VMEM((band, C3), full)] * 3,
        7,
    )(summed, stats_three, norm_rows, head_all, facts)
    stats_four = exchange(stats)

    wide_half = pltpu.VMEM((rows, WIDE), half)
    picks = pltpu.VMEM((C3, 2 * WIDE), half)
    half_outs = [(shape((rows, WIDE), half), ANY)] * 2

    def back(layer, heads, tails, after):
        last = layer == 1
        return call(
            functools.partial(back_kernel, (per, row_total, split), layer),
            ([SMEM, ANY, ANY] + [VMEM] * 4 if last else [SMEM, ANY])
            + [ANY, ANY, VMEM]
            + [ANY] * 10,
            [(shape((rows, C3)), ANY), (line, VMEM)]
            + (half_outs + [(shape((rows, C3)), ANY)] if last else []),
            (
                [table, wide_half, wide_half, picks, pltpu.SemaphoreType.DMA((2 * QUARTERS + 1,))]
                if last
                else [pltpu.VMEM((rows, C3), half)]
            )
            + [
                table,
                table,
                pltpu.VMEM((C3, 9 * C3), half),
                pltpu.VMEM((rows, TRIPLE), half),
                table,
                pltpu.SemaphoreType.DMA((10,)),
                pltpu.SemaphoreType.DMA((2 * QUARTERS,)),
                pltpu.SemaphoreType.DMA((QUARTERS,)),
            ],
            22,
            len(after),
        )(ids, *heads, *tails, *kernels[layer], *after)

    grad_conv_one, stats, own_half, far_half, grad_summed = back(
        1,
        [slope_three, summed, stats_three, stats_four, norm_rows, spread],
        [conv_one, slope_two, stats_two],
        [],
    )
    stats_five = exchange(stats)

    def weight_grad(own_half, far_half, field, far_field, chunks, after):
        sizes = [part_sizes(split, lines) for lines in chunks]
        outs = [
            (shape((size, tall, 128), half), ANY) for parts in sizes for _, _, size in parts
        ]
        flat = call(
            functools.partial(weight_grad_kernel, (chunks, split, band)),
            [ANY] * 4,
            outs,
            [
                pltpu.VMEM((2 * rows, WIDE), half),
                pltpu.VMEM((2 * rows, TRIPLE), half),
                pltpu.VMEM((2, rows, C3), half),
                pltpu.VMEM((split, 45, tall, 128), half),
                pltpu.SemaphoreType.DMA((16,)),
                pltpu.SemaphoreType.DMA((16,)),
                pltpu.SemaphoreType.DMA((len(outs),)),
            ],
            13,
            len(after),
        )(own_half, over_filt(far_half, 1), field, far_field, *after)
        result = []
        for parts in sizes:
            result.append(flat[: len(parts)])
            flat = flat[len(parts) :]
        return result

    def add(values):
        return sum(value.astype(full) for value in values).astype(half)

    def start_dp(parts, after):
        own, near, next_near, far_low, far_high = parts
        blocks = near.shape[0]
        cut = far_low.shape[0]
        from_near = over_dp(far_low, 1)
        from_next = over_dp(far_high, 2)
        near, next_near = merge(
            [near, next_near, from_near, from_next],
            [
                (blocks, [(0, 0, 0, blocks), (3, 0, cut, blocks - cut)]),
                (blocks, [(1, 0, 0, blocks), (2, 0, 0, cut)]),
            ],
            after,
            3,
        )
        return [own, near, next_near]

    def end_dp(parts, sizes, after):
        own, near, next_near = parts
        plan = []
        start = 0
        for size in sizes:
            plan.append((size, [(source, start, 0, size) for source in range(3)]))
            start += size
        return merge([own, over_dp(near, 1), over_dp(next_near, 2)], plan, after, 0.1)

    def gated_add(left, right, after):
        if not after:
            return add([left, right])
        size = left.shape[0]
        return merge([left, right], [(size, [(0, 0, 0, size), (1, 0, 0, size)])], after, 0.1)[0]

    def chip_routes(reach):
        routes = []
        for move in ({0: 1, 3: 2}, {1: 2, 2: 1}, {1: 0, 2: 3}):
            pairs = []
            for index in range(groups):
                here = index // 2 // reach % 4
                if here in move:
                    pairs.append((index, index + (move[here] - here) * 2 * reach))
            routes.append(pairs)
        return routes

    def to_middles(value, reach, after):
        arrived = lax.ppermute(value, "filt", chip_routes(reach)[0])
        return gated_add(value, arrived, after)

    def between_middles(value, reach, after):
        return gated_add(value, lax.ppermute(value, "filt", chip_routes(reach)[1]), after)

    def from_middles(value, reach, after=()):
        arrived = lax.ppermute(value, "filt", chip_routes(reach)[2])
        (result,) = call(
            functools.partial(pick_kernel, reach),
            [SMEM, ANY, ANY],
            [(shape(value.shape, half), VMEM)],
            [pltpu.SemaphoreType.DMA],
            0.1,
            len(after),
        )(ids, value, arrived, *after)
        return result

    def over_more_chips(value, reach):
        while reach < chips:
            value = from_middles(value, reach // 4)
            value = to_middles(value, reach, [])
            value = between_middles(value, reach, [])
            reach *= 4
        return value

    chunks_two = ((0, 1, 2),)
    chunks_one = ((0, 1, 2),)
    pairs_two = weight_grad(
        own_half, far_half, field_two, far_field_two, chunks_two, []
    )
    grad_one_half, own_half_one, far_half_one = call(
        functools.partial(norm_back_kernel, (row_total, split)),
        [SMEM, ANY, ANY, VMEM, VMEM, VMEM],
        [(shape((rows, C3), half), ANY)] + half_outs,
        [
            table,
            table,
            pltpu.VMEM((rows, C3), half),
            wide_half,
            wide_half,
            picks,
            pltpu.SemaphoreType.DMA((2 * QUARTERS,)),
            pltpu.SemaphoreType.DMA((3 * QUARTERS,)),
        ],
        6,
        1,
    )(ids, grad_conv_one, conv_one, stats_two, stats_five, norm_rows, pairs_two[0][0])
    pairs_one = weight_grad(
        own_half_one, far_half_one, field_one, far_field_one, chunks_one, [pairs_two[0][0]]
    )
    begun_two = start_dp(pairs_two[0], [pairs_one[0][0]])
    grad_base, stats = back(
        0,
        [grad_one_half],
        [base, slope_one, stats_one],
        [pairs_one[0][0], begun_two[1]],
    )
    stats_six = exchange(stats)
    begun_one = start_dp(pairs_one[0], [stats_six])
    blocks = begun_one[0].shape[0]
    (part_two,) = end_dp(begun_two, [blocks], [stats_six])
    small = shape((split, 2 * tall, WIDE), half)
    small_mine, small_other = call(
        functools.partial(trunk_kernel, (per, row_total, split)),
        [SMEM] + [VMEM] * 15,
        [(small, ANY), (small, ANY)],
        [
            pltpu.VMEM((rows, C3), half),
            pltpu.VMEM((rows, WIDE), half),
            pltpu.VMEM((rows, C1), half),
            pltpu.VMEM((rows, C1), half),
            pltpu.VMEM((rows, C0), half),
            pltpu.VMEM((rows, C0), half),
            pltpu.VMEM((C1, WIDE), half),
            pltpu.VMEM((C3, WIDE), half),
            pltpu.VMEM((C1, WIDE), half),
            pltpu.SemaphoreType.DMA((4 * split,)),
        ],
        0.1,
        2,
    )(
        ids,
        grad_base,
        grad_summed,
        base,
        stats_one,
        stats_six,
        norm_rows,
        proj_t,
        act_three,
        mid_two,
        mid_one,
        stem_out,
        patches,
        proj_a,
        proj_b,
        grad_head,
        begun_one[1],
        part_two,
    )
    crossed = over_filt(small_other, 1)
    pair = [add([small_mine[turn], crossed[turn]]) for turn in range(split)]
    small_sum = add([pair[0]] + [over_dp(pair[turn], turn) for turn in range(1, split)])
    (part_one,) = end_dp(begun_one, [blocks], [small_mine])
    half_two = to_middles(part_two, 1, [part_one])
    half_one = to_middles(part_one, 1, [half_two, small_sum])
    whole_two = between_middles(half_two, 1, [half_one])
    whole_two = over_more_chips(whole_two, 4)
    last = chips // 4
    small_sum = between_middles(to_middles(small_sum, 1, []), 1, [])
    small_sum = over_more_chips(small_sum, 4)
    small_whole = from_middles(small_sum, last)

    reduced_two = from_middles(whole_two, last)
    whole_one = between_middles(half_one, 1, [reduced_two, small_sum])
    whole_one = over_more_chips(whole_one, 4)
    squares, grad_norm_p, loss = call(
        functools.partial(norm_kernel, (devices, chips, split)),
        [SMEM] + [VMEM] * 6,
        [
            (shape((devices, 1, 128)), VMEM),
            (shape((6, C3 // split)), VMEM),
            (shape((1, 128)), VMEM),
        ],
        [pltpu.VMEM((8, C3), full)],
        3,
        1,
    )(ids, whole_one, whole_two, small_sum, stats_six, stats_five, stats_four, small_whole)
    squares = exchange(squares)
    reduced_one = from_middles(whole_one, last, [squares])

    pieces = []
    places = []
    for owner, value in enumerate((reduced_one, reduced_two)):
        pieces += [value, over_filt(value, 1)]
        places += [(owner, 0, blocks, side) for side in range(2)]
    whole_spec = pl.BlockSpec((1, 2 * tall, 1152), lambda layer, line: (layer, 0, line))
    conv_shape = shape(conv_w.shape)
    conv_new = pl.pallas_call(
        functools.partial(
            conv_update_kernel, (len(pieces), places, 0.7 / math.sqrt(9.0 * C3))
        ),
        grid=(2, 5),
        in_specs=[SMEM, VMEM, whole_spec, whole_spec, whole_spec] + [ANY] * len(pieces),
        out_specs=[whole_spec] * 3,
        out_shape=[conv_shape] * 3,
        scratch_shapes=[
            pltpu.VMEM((2, 45, 2 * tall, 128), half),
            pltpu.SemaphoreType.DMA((len(pieces),)),
        ],
        compiler_params=pltpu.CompilerParams(vmem_limit_bytes=63 * MIB),
        cost_estimate=pl.CostEstimate(
            flops=20 * conv_w.size, bytes_accessed=26 * conv_w.size, transcendentals=0
        ),
    )(ids, squares, conv_w, conv_w_m, conv_w_v, *pieces)
    states = (
        (stem_w.T, stem_w_m.T, stem_w_v.T),
        (proj_a, proj_a_m, proj_a_v),
        (proj_b, proj_b_m, proj_b_v),
        (proj_c.T, proj_c_m.T, proj_c_v.T),
        (head_w.T, head_w_m.T, head_w_v.T),
        (norm_p, norm_p_m, norm_p_v),
    )
    rates = (
        0.7 / math.sqrt(27.0),
        0.7 / math.sqrt(C0),
        0.7 / math.sqrt(C1),
        0.7 / math.sqrt(C2),
        0.7 / math.sqrt(C3 / 8.0),
        0.8,
    )
    flat = [item for group in states for item in group]
    small_new = call(
        functools.partial(small_update_kernel, rates),
        [SMEM] + [VMEM] * 22,
        [(shape(item.shape), VMEM) for item in flat] + [(shape((1, 128)), VMEM)],
        [],
        3,
    )(ids, squares, small_whole, over_filt(small_whole, 1), grad_norm_p, *flat)
    size = small_new[18][0, 0]
    turned = [
        item.T if index // 3 in (0, 3, 4) else item for index, item in enumerate(small_new[:18])
    ]
    return (
        *turned[0:12],
        *conv_new,
        *turned[12:18],
        loss[0, 0],
        size,
    )


def solution(mesh):
    placed = (
        P("filt", None, None),
        P("filt"),
        P("filt", None),
        P("filt"),
        *([P()] * 9),
        *([P(None, "dp")] * 3),
        *([P(None, "dp", None)] * 3),
        *([P("dp", None)] * 3),
        *([P(None, "dp")] * 3),
    )
    return jax.shard_map(
        shards,
        mesh=mesh,
        in_specs=placed,
        out_specs=(
            *([P()] * 9),
            *([P(None, "dp")] * 3),
            *([P(None, "dp", None)] * 3),
            *([P("dp", None)] * 3),
            *([P(None, "dp")] * 3),
            P(),
            P(),
        ),
        check_vma=False,
    )
```

```python
import functools
import math

import jax
import jax.numpy as jnp
from jax import lax
from jax.experimental import pallas as pl
from jax.experimental.pallas import tpu as pltpu
from jax.sharding import PartitionSpec as P

C0 = 16
C1 = 160
C2 = 320
C3 = 640
WIDE = 384
TRIPLE = 3 * C3
SIDE = 32
CUT = 16
STEP = 10
PLANE = 640
META = 576
CHUNK = 48
QUARTERS = 4

beta_one = 0.9
beta_two = 0.999
adam_eps = 1e-08
weight_decay = 0.0005
clip_limit = 0.05
norm_eps = 1e-05
gelu_one = math.sqrt(2.0 / math.pi)
gelu_three = 0.044715 * gelu_one

half = jnp.bfloat16
full = jnp.float32
NT = (((1,), (1,)), ((), ()))
NN = (((1,), (0,)), ((), ()))
TN = (((0,), (0,)), ((), ()))
VMEM = pl.BlockSpec(memory_space=pltpu.VMEM)
SMEM = pl.BlockSpec(memory_space=pltpu.SMEM)
ANY = pl.BlockSpec(memory_space=pl.ANY)
MIB = 2**20


def shape(dims, kind=full):
    return jax.ShapeDtypeStruct(dims, kind)


def dot(left, right, dims=NN):
    return lax.dot_general(left, right, dims, preferred_element_type=full)


def iota(dims, axis):
    return lax.broadcasted_iota(jnp.int32, dims, axis)


def hot(condition):
    return condition.astype(full).astype(half)


def call(kernel, ins, outs, scratch, micros, after=0):
    used = len(ins)

    def body(*refs):
        kernel(*refs[:used], *refs[used + after :])

    return pl.pallas_call(
        body,
        out_shape=[item[0] for item in outs],
        in_specs=ins + [ANY] * after,
        out_specs=[item[1] for item in outs],
        scratch_shapes=scratch,
        cost_estimate=pl.CostEstimate(
            flops=int(micros * 35 * 10**7), bytes_accessed=1, transcendentals=0
        ),
        compiler_params=pltpu.CompilerParams(vmem_limit_bytes=63 * MIB),
    )


def gelu_pair(values):
    square = values * values
    bent = jnp.tanh(values * (gelu_one + gelu_three * square))
    gate = 0.5 + 0.5 * bent
    slope = gate + (0.5 * values) * (1.0 - bent * bent) * (gelu_one + (3.0 * gelu_three) * square)
    return (values * gate, slope)


def adamw(weight, gradient, first, second, step_rate):
    first_new = beta_one * first + (1.0 - beta_one) * gradient
    second_new = beta_two * second + (1.0 - beta_two) * (gradient * gradient)
    second_hat = second_new * (1.0 / (1.0 - beta_two**STEP))
    root = second_hat * lax.rsqrt(second_hat) + adam_eps
    weight_new = weight * (1.0 - step_rate * weight_decay) - (
        step_rate / (1.0 - beta_one**STEP)
    ) * (first_new / root)
    return (first_new, second_new, weight_new)


def fetch(source, target, sem):
    copy = pltpu.make_async_copy(source, target, sem)
    copy.start()
    return copy


def lane_pixel(lanes):
    tap = lanes // 64
    cell = lanes % 64
    row = 4 * (cell // 8) + tap // 3 - 1
    col = 4 * (cell % 8) + tap % 3 - 1
    return (tap, row, col)


def image_kernel(planes, labels, corners, partners, out, numbers):
    count = planes.shape[1]
    tap, row, col = lane_pixel(iota((1, PLANE), 1))
    pixel = jnp.where((row >= 0) & (col >= 0) & (tap < 9), row * SIDE + col, -1)
    pick = hot(iota((SIDE * SIDE, PLANE), 0) == pixel)
    numbers[...] = jnp.zeros(numbers.shape, full)
    numbers[0:1] = labels[...].astype(full)
    numbers[1:3] = corners[...].astype(full)
    numbers[3:4] = (partners[...] // count).astype(full)
    numbers[4:5] = (partners[...] % count).astype(full)
    place = hot(iota((8, PLANE), 0) + META == iota((8, PLANE), 1))
    for colour in range(3):
        taken = dot(planes[colour], pick)
        if colour == 0:
            taken = taken + dot(numbers[...].astype(half), place, TN)
        out[:, colour * PLANE : (colour + 1) * PLANE] = taken.astype(half)


def pack_lanes(proj_c, head, norm):
    place = hot(iota((C2, WIDE), 0) == iota((C2, WIDE), 1))
    total = dot(proj_c[...].astype(half), place)
    classes = head.shape[0]
    place = hot(iota((classes, WIDE), 0) + C2 == iota((classes, WIDE), 1))
    total = total + dot(head[...].astype(half), place, TN)
    rest = norm[...]
    for part in range(3):
        piece = rest.astype(half)
        rest = rest - piece.astype(full)
        place = hot(iota((6, WIDE), 0) + (C2 + 16 + 8 * part) == iota((6, WIDE), 1))
        total = total + dot(piece, place, TN)
    return total


def cast_kernel(layer, *refs):
    ids, weights = refs[0:2]
    out, wide, narrow, in_sems, out_sems = refs[-5:]
    rows = out.shape[0]
    cols = wide.shape[1]
    parts = rows // 16
    inputs = []
    for part in range(parts):
        spot = pl.multiple_of(ids[2] * rows + part * 16, 16)
        inputs.append(
            fetch(
                weights.at[layer, pl.ds(spot, 16)],
                wide.at[part * 16 : part * 16 + 16],
                in_sems.at[part],
            )
        )
    if layer == 0:
        total = pack_lanes(*refs[2:5])
        mine = jnp.where(ids[2] == 0, total[0:rows], total[rows : 2 * rows])
        narrow[:, cols : cols + WIDE] = mine.astype(half)
    outputs = []
    for part in range(parts):
        here = slice(part * 16, part * 16 + 16)
        inputs[part].wait()
        narrow[here, 0:cols] = wide[here].astype(half)
        outputs.append(fetch(narrow.at[here], out.at[here], out_sems.at[part]))
    for copy in outputs:
        copy.wait()


def cast_half(ids, conv_w, layer, packed, after):
    rows = conv_w.shape[1] // 2
    cols = conv_w.shape[2]
    total = cols + WIDE if layer == 0 else cols
    (result,) = call(
        functools.partial(cast_kernel, layer),
        [SMEM, ANY] + [VMEM] * len(packed),
        [(shape((rows, total), half), ANY)],
        [
            pltpu.VMEM((rows, cols), full),
            pltpu.VMEM((rows, total), half),
            pltpu.SemaphoreType.DMA((rows // 16,)),
            pltpu.SemaphoreType.DMA((rows // 16,)),
        ],
        3,
        len(after),
    )(ids, conv_w, *packed, *after)
    return result


def hold_kernel(*refs):
    pass


def hold(value, after):
    return pl.pallas_call(
        hold_kernel,
        out_shape=shape(value.shape, value.dtype),
        in_specs=[ANY] * 2,
        out_specs=ANY,
        input_output_aliases={0: 0},
        compiler_params=pltpu.CompilerParams(has_side_effects=True),
        cost_estimate=pl.CostEstimate(flops=1, bytes_accessed=1, transcendentals=0),
    )(value, after)


def merge_spans(plan):
    spans = []
    for out, (size, terms) in enumerate(plan):
        edges = {0, size}
        for _, _, start, length in terms:
            edges |= {start, start + length}
        edges = sorted(edges)
        for low, high in zip(edges[:-1], edges[1:]):
            used = [
                (source, first - start)
                for source, first, start, length in terms
                if start <= low and high <= start + length
            ]
            for begin in range(low, high, 8):
                spans.append((out, begin, min(8, high - begin), used))
    return spans


def merge_kernel(plan, count, *refs):
    values = refs[:count]
    results = refs[count : count + len(plan)]
    held = refs[count + len(plan) : 2 * count + len(plan)]
    kept = refs[2 * count + len(plan) : 2 * (count + len(plan))]
    in_sems, out_sems = refs[2 * (count + len(plan)) :]
    arrivals = []
    number = 0
    for _, begin, size, used in merge_spans(plan):
        copies = []
        for source, shift in used:
            here = slice(begin + shift, begin + shift + size)
            copies.append(
                fetch(values[source].at[here], held[source].at[here], in_sems.at[number])
            )
            number += 1
        arrivals.append(copies)
    departures = []
    for (out, begin, size, used), copies in zip(merge_spans(plan), arrivals):
        for copy in copies:
            copy.wait()
        total = None
        for source, shift in used:
            value = held[source][begin + shift : begin + shift + size].astype(full)
            total = value if total is None else total + value
        here = slice(begin, begin + size)
        kept[out][here] = total.astype(half)
        departures.append(
            fetch(kept[out].at[here], results[out].at[here], out_sems.at[len(departures)])
        )
    for copy in departures:
        copy.wait()


def merge(values, plan, after, micros):
    dims = values[0].shape[1:]
    spans = merge_spans(plan)
    return call(
        functools.partial(merge_kernel, plan, len(values)),
        [ANY] * len(values),
        [(shape((size,) + dims, half), ANY) for size, _ in plan],
        [pltpu.VMEM(value.shape, half) for value in values]
        + [pltpu.VMEM((size,) + dims, half) for size, _ in plan]
        + [
            pltpu.SemaphoreType.DMA((sum(len(used) for _, _, _, used in spans),)),
            pltpu.SemaphoreType.DMA((len(spans),)),
        ],
        micros,
        len(after),
    )(*values, *after)


def pick_kernel(reach, ids, value, arrived, out, sem):
    digit = ids[3] // reach % 4
    outer = (digit == 0) | (digit == 3)

    @pl.when(outer)
    def _():
        fetch(arrived, out, sem).wait()

    @pl.when(jnp.logical_not(outer))
    def _():
        fetch(value, out, sem).wait()


def cut_kernel(places, *refs):
    count = len(places)
    outs = refs[count : 2 * count]
    sems = refs[2 * count]
    copies = []
    for index, (start, size) in enumerate(places):
        copies.append(
            fetch(refs[index].at[start : start + size], outs[index], sems.at[index])
        )
    for copy in copies:
        copy.wait()


def cut_rows(values, places, after):
    cols = values[0].shape[1]
    return call(
        functools.partial(cut_kernel, places),
        [ANY] * len(values),
        [(shape((size, cols), half), VMEM) for _, size in places],
        [pltpu.SemaphoreType.DMA((len(values),))],
        1,
        len(after),
    )(*values, *after)


def stack_kernel(places, *refs):
    count = len(places)
    out, sems = refs[count:]
    copies = []
    for index, (slot, start, size) in enumerate(places):
        copy = pltpu.make_async_copy(
            refs[index], out.at[slot, start : start + size], sems.at[index]
        )
        copy.start()
        copies.append(copy)
    for copy in copies:
        copy.wait()


def stack(pieces, places, dims, after):
    (result,) = call(
        functools.partial(stack_kernel, places),
        [ANY] * len(pieces),
        [(shape(dims, half), VMEM)],
        [pltpu.SemaphoreType.DMA((len(pieces),))],
        3,
        len(after),
    )(*pieces, *after)
    return result


def front_kernel(sizes, *refs):
    per, count, groups, devices, split = sizes
    rows = per * 64
    band = per * 8
    ids = refs[0]
    images, far_images, stem_w, proj_a, proj_b = refs[1:6]
    (
        patches,
        stem_out,
        mid_one,
        mid_two,
        act_three,
        facts,
        tiles,
        loose,
        stem_pad,
        proj_b_pad,
    ) = refs[6:]
    slot = iota((per, count), 0)
    column = iota((per, count), 1)
    own = dot(hot(column == slot + ids[0] * per), images[0])
    group_of = own[:, META + 3 : META + 4].astype(jnp.int32)
    local_of = own[:, META + 4 : META + 5].astype(jnp.int32)
    turn_of = group_of ^ ids[1]
    other = jnp.zeros((per, 3 * PLANE), full)
    for turn in range(groups):
        source = far_images[turn // 2] if turn % 2 else images[turn // 2]
        other = other + dot(hot((turn_of == turn) & (column == local_of)), source)
    top = own[:, META + 1 : META + 2]
    left = own[:, META + 2 : META + 3]
    tap, row, col = lane_pixel(iota((1, 3 * PLANE), 1) % PLANE)
    row = row.astype(full)
    col = col.astype(full)
    inside = (row >= top) & (row < top + CUT) & (col >= left) & (col < left + CUT) & (tap < 9)
    blended = jnp.where(inside, other, own)
    tall = jnp.maximum(jnp.minimum(top + CUT, float(SIDE)) - jnp.maximum(top, 0.0), 0.0)
    broad = jnp.maximum(jnp.minimum(left + CUT, float(SIDE)) - jnp.maximum(left, 0.0), 0.0)
    share = 1.0 - tall * broad / float(SIDE * SIDE)
    lanes = iota((per, 128), 1)
    facts[...] = jnp.where(
        lanes == 0,
        own[:, META : META + 1],
        jnp.where(lanes == 1, other[:, META : META + 1], share),
    )
    tiles[...] = jnp.zeros(tiles.shape, full)
    for piece in range(15):
        tiles[:, piece, :] = blended[:, piece * 128 : (piece + 1) * 128]
    tiles[:, 16:32, :] = pltpu.roll(tiles[:, 0:16, :], 64, 2)
    spot = iota((32, 32), 0)
    tap_at = ((spot % 16) % 5) * 2 + spot // 16
    colour_at = (spot % 16) // 5
    order = hot(
        (iota((32, 32), 1) == tap_at * 3 + colour_at) & (tap_at < 9) & (spot % 16 < 15)
    )
    for image in range(per):
        cells = dot(tiles[image].astype(half), order, TN)
        for line in range(8):
            loose[line * band + image * 8 : line * band + image * 8 + 8, :] = cells[
                line * 8 : line * 8 + 8
            ]
    patches[...] = loose[...].astype(half)
    stem_pad[...] = jnp.zeros(stem_pad.shape, full)
    stem_pad[:, 0:27] = stem_w[...]
    proj_b_pad[...] = jnp.zeros(proj_b_pad.shape, half)
    proj_b_pad[:, 0:C2] = proj_b[...].astype(half)
    stem_half = stem_pad[...].astype(half)
    proj_a_half = proj_a[...].astype(half)
    tall_chunk = 2 * band

    def step(index, carry):
        at = pl.ds(pl.multiple_of(index * tall_chunk, 16), tall_chunk)
        stem = dot(patches[at], stem_half, NT)
        stem_out[at] = stem
        one = dot(gelu_pair(stem)[0].astype(half), proj_a_half)
        mid_one[at] = one
        two = dot(gelu_pair(one)[0].astype(half), proj_b_pad[...])
        mid_two[at] = two
        act_three[at] = gelu_pair(two)[0].astype(half)
        return carry

    lax.fori_loop(0, rows // tall_chunk, step, 0)


def base_kernel(*refs):
    ids, act_three = refs[0:2]
    pieces = refs[2:12]
    base, stats, norm_rows, head_all, proj_t, gathered, held, totals, sems, out_sems = refs[12:]
    rows = act_three.shape[0]
    lanes = pl.ds(pieces[0].shape[1] - WIDE, WIDE)
    for copy in start_weights(ids, pieces, gathered, sems, lanes):
        copy.wait()
    column = iota((1, WIDE), 1)
    packed = gathered[...]
    proj_t[...] = jnp.where(column < C2, packed.astype(full), 0.0).astype(half)
    place = hot(iota((WIDE, 16), 0) == iota((WIDE, 16), 1) + C2)
    head_all[...] = dot(packed, place).astype(half)
    column = iota((8, WIDE), 1)
    name = iota((8, WIDE), 0)
    pieces = [
        dot(hot((column == name + (C2 + 16 + 8 * part)) & (name < 6)), packed, NT)
        for part in range(3)
    ]
    norm_rows[...] = pieces[0] + (pieces[1] + pieces[2])
    totals[...] = jnp.zeros(totals.shape, full)
    outputs = []
    for part in range(QUARTERS):
        at = quarter_rows(rows, part)
        result = dot(act_three[at], proj_t[...], NT)
        held[at] = result
        outputs.append(fetch(held.at[at], base.at[at], out_sems.at[part]))
        totals[0:1] += jnp.sum(result, axis=0, keepdims=True)
        totals[1:2] += jnp.sum(result * result, axis=0, keepdims=True)
    spread_stats(stats, [totals[0:1], totals[1:2]])
    for copy in outputs:
        copy.wait()


def spread_stats(out, parts):
    line = jnp.concatenate(parts, axis=1)
    out[...] = jnp.broadcast_to(line[None], out.shape)


def moments(stats, row_total):
    line = jnp.sum(stats[...], axis=0)
    mean = line[:, 0:C3] / row_total
    rstd = lax.rsqrt(line[:, C3 : 2 * C3] / row_total - mean * mean + norm_eps)
    return (mean, rstd)


def quarter_rows(rows, part):
    step = rows // QUARTERS
    return pl.ds(part * step, step)


def fetch_quarter(source, target, sem, part):
    here = quarter_rows(source.shape[0], part)
    return fetch(source.at[here], target.at[here], sem)


def walk_quarter(rows, part, body, carry):
    step = rows // QUARTERS // CHUNK
    return lax.fori_loop(part * step, (part + 1) * step, body, carry)


def start_weights(ids, pieces, weights, sems, lanes=pl.ds(0, 9 * C3)):
    rows = pieces[0].shape[0]
    low = pieces[3].shape[0]
    copies = []
    for side in range(2):
        for place in range(5):
            piece = pieces[5 * side + place]
            turn = min(place, 3)
            spot = (ids[0] ^ turn) * (2 * rows) + (ids[2] ^ side) * rows
            if place == 4:
                spot = spot + low
            spot = pl.multiple_of(spot, 16)
            copies.append(
                fetch(
                    piece.at[:, lanes],
                    weights.at[pl.ds(spot, piece.shape[0])],
                    sems.at[5 * side + place],
                )
            )
    return copies


def shifted(values, by):
    block = values.reshape(CHUNK // 8, 8, C3)
    place = iota((1, 8, 1), 1)
    if by == 1:
        moved = jnp.where(place == 0, 0.0, pltpu.roll(block, 1, 1))
    else:
        moved = jnp.where(place == 7, 0.0, pltpu.roll(block, 7, 1))
    return moved.reshape(CHUNK, C3)


def conv_kernel(sizes, layer, *refs):
    per, row_total, split = sizes
    rows = per * 64
    band = per * 8
    ids, source, stats_in, norm_rows = refs[0:4]
    offset = 4
    if layer == 1:
        base = refs[4]
        offset = 5
    pieces = refs[offset : offset + 10]
    offset += 10
    (result, field_out, slope_out, stats, held, weights, field, slope, total) = refs[
        offset : offset + 9
    ]
    weight_sems, in_sems, out_sems = refs[offset + 9 : offset + 12]
    inputs = [fetch_quarter(source, held, in_sems.at[part], part) for part in range(QUARTERS)]
    copies = start_weights(ids, pieces, weights, weight_sems)
    mean, rstd = moments(stats_in, row_total)
    factor = rstd * norm_rows[2 * layer : 2 * layer + 1]
    shift = norm_rows[2 * layer + 1 : 2 * layer + 2] - mean * factor

    def prepare(index, carry):
        at = pl.ds(pl.multiple_of(index * CHUNK, 16), CHUNK)
        value, gradient = gelu_pair(held[at] * factor + shift)
        slope[at] = gradient
        field[at, 0:C3] = shifted(value, 1).astype(half)
        field[at, C3 : 2 * C3] = value.astype(half)
        field[at, 2 * C3 : TRIPLE] = shifted(value, -1).astype(half)
        return carry

    for part in range(QUARTERS):
        inputs[part].wait()
        walk_quarter(rows, part, prepare, 0)
    outputs = [
        fetch(field.at[:, C3 : 2 * C3], field_out, out_sems.at[QUARTERS]),
        fetch(slope, slope_out, out_sems.at[QUARTERS + 1]),
    ]
    if layer == 1:
        inputs = [fetch_quarter(base, held, in_sems.at[part], part) for part in range(QUARTERS)]
    for copy in copies:
        copy.wait()
    inner = rows - band
    total[...] = dot(field[...], weights[:, TRIPLE : 2 * TRIPLE], NT)
    total[band:rows] += dot(field[0:inner], weights[:, 0:TRIPLE], NT)
    total[0:inner] += dot(field[band:rows], weights[:, 2 * TRIPLE : 3 * TRIPLE], NT)

    def count(index, carry):
        at = pl.ds(pl.multiple_of(index * CHUNK, 16), CHUNK)
        value = total[at]
        if layer == 1:
            value = value + held[at]
            total[at] = value
        return (
            carry[0] + jnp.sum(value.reshape(CHUNK // 8, 8, C3), axis=0),
            carry[1] + jnp.sum((value * value).reshape(CHUNK // 8, 8, C3), axis=0),
        )

    zero = jnp.zeros((8, C3), full)
    sums = (zero, zero)
    for part in range(QUARTERS):
        if layer == 1:
            inputs[part].wait()
        else:
            outputs.append(fetch_quarter(total, result, out_sems.at[part], part))
        sums = walk_quarter(rows, part, count, sums)
        if layer == 1:
            outputs.append(fetch_quarter(total, result, out_sems.at[part], part))
    spread_stats(stats, [jnp.sum(item, axis=0, keepdims=True) for item in sums])
    for copy in outputs:
        copy.wait()


def head_kernel(sizes, *refs):
    per, row_total, image_total, classes = sizes
    rows = per * 64
    band = per * 8
    (
        source,
        stats_in,
        norm_rows,
        head_all,
        facts,
        slope_out,
        spread,
        stats,
        grad_head,
        sum_value,
        sum_slope,
        sum_cross,
        summed,
        slope,
        in_sems,
        out_sems,
    ) = refs
    inputs = [fetch_quarter(source, summed, in_sems.at[part], part) for part in range(QUARTERS)]
    mean, rstd = moments(stats_in, row_total)
    gain = norm_rows[4:5]
    bias = norm_rows[5:6]
    sum_value[...] = jnp.zeros((band, C3), full)
    sum_slope[...] = jnp.zeros((band, C3), full)
    sum_cross[...] = jnp.zeros((band, C3), full)

    def walk(index, carry):
        for part in range(band // CHUNK):
            at = pl.ds(pl.multiple_of(index * band + part * CHUNK, 16), CHUNK)
            here = slice(part * CHUNK, part * CHUNK + CHUNK)
            unit = (summed[at] - mean) * rstd
            value, gradient = gelu_pair(unit * gain + bias)
            slope[at] = gradient
            sum_value[here] += value
            sum_slope[here] += gradient
            sum_cross[here] += gradient * unit
        return carry

    outputs = []
    for part in range(QUARTERS):
        inputs[part].wait()
        lax.fori_loop(2 * part, 2 * part + 2, walk, 0)
        outputs.append(fetch_quarter(slope, slope_out, out_sems.at[part], part))

    def by_image(ref):
        return jnp.sum(ref[...].reshape(per, 8, C3), axis=1)

    pooled = (by_image(sum_value) / 64.0).astype(half)
    logits = dot(pooled, head_all[...])
    lanes = iota((per, 16), 1)
    inside = lanes < classes
    own = facts[:, 0:1].astype(jnp.int32)
    other = facts[:, 1:2].astype(jnp.int32)
    share = facts[:, 2:3]
    target = jnp.where(lanes == own, share, 0.0) + jnp.where(lanes == other, 1.0 - share, 0.0)
    top = jnp.max(jnp.where(inside, logits, -3e38), axis=1, keepdims=True)
    powers = jnp.where(inside, jnp.exp(jnp.where(inside, logits - top, 0.0)), 0.0)
    lse = top + jnp.log(jnp.sum(powers, axis=1, keepdims=True))
    losses = lse - jnp.sum(target * logits, axis=1, keepdims=True)
    loss = jnp.sum(losses, axis=0, keepdims=True)
    soft = jnp.where(inside, jnp.exp(jnp.where(inside, logits - lse, 0.0)), 0.0)
    grad_logits = ((soft - target) / image_total).astype(half)
    grad_head[...] = dot(pooled, grad_logits, TN)
    pull = dot(grad_logits, head_all[...], NT) / 64.0
    spread[...] = jnp.broadcast_to(pull[:, None, :], (per, 8, C3)).reshape(band, C3)
    bias_sum = jnp.sum(pull * by_image(sum_slope), axis=0, keepdims=True)
    gain_sum = jnp.sum(pull * by_image(sum_cross), axis=0, keepdims=True)
    spread_stats(stats, [bias_sum, gain_sum, jnp.broadcast_to(loss, (1, 128))])
    for copy in outputs:
        copy.wait()


def grad_moments(stats, row_total):
    line = jnp.sum(stats[...], axis=0)
    return (line[:, 0:C3] / row_total, line[:, C3 : 2 * C3] / row_total)


def input_grad(gradient, weights, out, band):
    rows = gradient.shape[0]
    inner = rows - band
    spans = (
        (1, slice(0, rows), slice(0, rows)),
        (0, slice(0, inner), slice(band, rows)),
        (2, slice(band, rows), slice(0, inner)),
    )
    for line, to, of in spans:
        for col in range(3):
            tap = 3 * line + col
            part = dot(
                gradient[of, col * C3 : (col + 1) * C3], weights[:, tap * C3 : (tap + 1) * C3]
            )
            if line == 1 and col == 0:
                out[to] = part
            else:
                out[to] += part


def half_filters(ids, split):
    tall = C3 // (2 * split)
    place = iota((1, 2 * WIDE), 1)
    side = jnp.where(place < WIDE, 0, 1)
    place = place - side * WIDE
    target = (ids[0] ^ (place // tall)) * (2 * tall) + (ids[2] ^ side) * tall + place % tall
    target = jnp.where(place < C3 // 2, target, -1)
    return hot(iota((C3, 2 * WIDE), 0) == target)


def norm_back(arriving, unit, factor, low, high):
    return factor * (arriving - low - unit * high)


def send_halves(middle, pick, helds, halves, sems, part):
    here = quarter_rows(helds[0].shape[0], part)
    both = dot(middle, pick).astype(half)
    copies = []
    for side in range(2):
        helds[side][here] = both[:, side * WIDE : (side + 1) * WIDE]
        copies.append(
            fetch(helds[side].at[here], halves[side].at[here], sems.at[2 * part + side])
        )
    return copies


def back_kernel(sizes, layer, *refs):
    per, row_total, split = sizes
    rows = per * 64
    band = per * 8
    last = layer == 1
    ids = refs[0]
    if last:
        incoming, source, stats_here, stats_grad, norm_rows, spread = refs[1:7]
        offset = 7
    else:
        incoming = refs[1]
        offset = 2
    before, slope_before, stats_before = refs[offset : offset + 3]
    pieces = refs[offset + 3 : offset + 13]
    result, stats = refs[offset + 13 : offset + 15]
    offset += 15
    if last:
        own_half, far_half, grad_out, kept, own_held, far_held, pick, half_sems = refs[
            offset : offset + 8
        ]
        offset += 8
    else:
        arrived = refs[offset]
        offset += 1
    held, origin, weights, gradient, total = refs[offset : offset + 5]
    weight_sems, in_sems, out_sems = refs[offset + 5 : offset + 8]
    inputs = []
    for part in range(QUARTERS):
        if last:
            inputs.append(
                (
                    fetch_quarter(incoming, held, in_sems.at[2 * part], part),
                    fetch_quarter(source, origin, in_sems.at[2 * part + 1], part),
                )
            )
        else:
            inputs.append((fetch_quarter(incoming, arrived, in_sems.at[2 * part], part),))
    copies = start_weights(ids, pieces, weights, weight_sems)
    if last:
        mean, rstd = moments(stats_here, row_total)
        low, high = grad_moments(stats_grad, row_total)
        factor = rstd * norm_rows[4:5]
        parts = band // CHUNK
        pick[...] = half_filters(ids, split)

    def prepare(index, carry):
        at = pl.ds(pl.multiple_of(index * CHUNK, 16), CHUNK)
        if last:
            here = pl.ds(pl.multiple_of(lax.rem(index, parts) * CHUNK, 16), CHUNK)
            unit = (origin[at] - mean) * rstd
            value = norm_back(held[at] * spread[here], unit, factor, low, high)
            kept[at] = value
            gradient[at, C3 : 2 * C3] = value.astype(half)
        else:
            gradient[at, C3 : 2 * C3] = arrived[at]
            value = arrived[at].astype(full)
        gradient[at, 0:C3] = shifted(value, -1).astype(half)
        gradient[at, 2 * C3 : TRIPLE] = shifted(value, 1).astype(half)
        return carry

    for part in range(QUARTERS):
        for copy in inputs[part]:
            copy.wait()
        walk_quarter(rows, part, prepare, 0)
    outputs = []
    if last:
        outputs.append(fetch(kept, grad_out, half_sems.at[2 * QUARTERS]))
        for part in range(QUARTERS):
            outputs += send_halves(
                gradient[quarter_rows(rows, part), C3 : 2 * C3],
                pick[...],
                (own_held, far_held),
                (own_half, far_half),
                half_sems,
                part,
            )
    inputs = []
    for part in range(QUARTERS):
        inputs.append(
            (
                fetch_quarter(before, origin, in_sems.at[2 * part], part),
                fetch_quarter(slope_before, held, in_sems.at[2 * part + 1], part),
            )
        )
    for copy in copies:
        copy.wait()
    input_grad(gradient, weights, total, band)
    mean, rstd = moments(stats_before, row_total)

    def finish(index, carry):
        at = pl.ds(pl.multiple_of(index * CHUNK, 16), CHUNK)
        value = total[at] * held[at]
        total[at] = value
        unit = (origin[at] - mean) * rstd
        return (
            carry[0] + jnp.sum(value.reshape(CHUNK // 8, 8, C3), axis=0),
            carry[1] + jnp.sum((value * unit).reshape(CHUNK // 8, 8, C3), axis=0),
        )

    zero = jnp.zeros((8, C3), full)
    sums = (zero, zero)
    for part in range(QUARTERS):
        for copy in inputs[part]:
            copy.wait()
        sums = walk_quarter(rows, part, finish, sums)
        outputs.append(fetch_quarter(total, result, out_sems.at[part], part))
    spread_stats(stats, [jnp.sum(item, axis=0, keepdims=True) for item in sums])
    for copy in outputs:
        copy.wait()


def norm_back_kernel(sizes, *refs):
    row_total, split = sizes
    ids, incoming, source, stats_here, stats_grad, norm_rows = refs[0:6]
    grad_half, own_half, far_half = refs[6:9]
    held, origin, middle, own_held, far_held, pick, in_sems, out_sems = refs[9:]
    rows = held.shape[0]
    inputs = []
    for part in range(QUARTERS):
        inputs.append(
            (
                fetch_quarter(incoming, held, in_sems.at[2 * part], part),
                fetch_quarter(source, origin, in_sems.at[2 * part + 1], part),
            )
        )
    mean, rstd = moments(stats_here, row_total)
    low, high = grad_moments(stats_grad, row_total)
    factor = rstd * norm_rows[2:3]
    pick[...] = half_filters(ids, split)

    def prepare(index, carry):
        at = pl.ds(pl.multiple_of(index * CHUNK, 16), CHUNK)
        unit = (origin[at] - mean) * rstd
        middle[at] = norm_back(held[at], unit, factor, low, high).astype(half)
        return carry

    outputs = []
    for part in range(QUARTERS):
        for copy in inputs[part]:
            copy.wait()
        walk_quarter(rows, part, prepare, 0)
        here = quarter_rows(rows, part)
        outputs.append(fetch(middle.at[here], grad_half.at[here], out_sems.at[8 + part]))
        outputs += send_halves(
            middle[here], pick[...], (own_held, far_held), (own_half, far_half), out_sems, part
        )
    for copy in outputs:
        copy.wait()


def weight_grad_kernel(sizes, *refs):
    chunks, split, band = sizes
    gradients = refs[0:2]
    fields = refs[2:4]
    count = sum(len(part_sizes(split, lines)) for lines in chunks)
    outs = refs[4 : 4 + count]
    (gradient, field, plain, held, in_sems, grad_sems, sems) = refs[4 + count :]
    inputs = []
    for line in range(8):
        for side in range(2):
            of = pl.ds(line * band, band)
            inputs.append(
                fetch(fields[side].at[of], plain.at[side, of], in_sems.at[2 * line + side])
            )
    arriving = []
    for line in range(8):
        for side in range(2):
            of = pl.ds(line * band, band)
            to = pl.ds((2 * line + side) * band, band)
            arriving.append(
                fetch(gradients[side].at[of], gradient.at[to], grad_sems.at[2 * line + side])
            )

    def prepare(index, carry):
        for side in range(2):
            for part in range(band // CHUNK):
                to = pl.ds(
                    pl.multiple_of((2 * index + side) * band + part * CHUNK, 16), CHUNK
                )
                of = pl.ds(pl.multiple_of(index * band + part * CHUNK, 16), CHUNK)
                value = plain[side, of]
                wide = value.astype(full)
                field[to, 0:C3] = shifted(wide, 1).astype(half)
                field[to, C3 : 2 * C3] = value
                field[to, 2 * C3 : TRIPLE] = shifted(wide, -1).astype(half)
        return carry

    for part in range(QUARTERS):
        for copy in inputs[4 * part : 4 * part + 4]:
            copy.wait()
        lax.fori_loop(2 * part, 2 * part + 2, prepare, 0)
    for copy in arriving:
        copy.wait()
    rows = field.shape[0]
    inner = rows - 2 * band
    spans = {
        0: (slice(2 * band, rows), slice(0, inner)),
        1: (slice(0, rows), slice(0, rows)),
        2: (slice(0, inner), slice(2 * band, rows)),
    }
    tall = held.shape[2]
    copies = []
    start = 0
    number = 0
    for lines in chunks:
        for place, line in enumerate(lines):
            left, right = spans[line]
            part = dot(gradient[left, 0 : C3 // 2], field[right], TN).astype(half)
            for turn in range(split):
                for block in range(15):
                    held[turn, start + place * 15 + block] = part[
                        turn * tall : (turn + 1) * tall, block * 128 : (block + 1) * 128
                    ]
        for turn, first, size in part_sizes(split, lines):
            copies.append(
                fetch(
                    held.at[turn, start + first : start + first + size],
                    outs[number],
                    sems.at[number],
                )
            )
            number += 1
        start += 15 * len(lines)
    for copy in copies:
        copy.wait()


def part_sizes(split, lines):
    blocks = 15 * len(lines)
    sizes = [(turn, 0, blocks) for turn in range(split - 1)]
    return sizes + [(split - 1, 0, blocks // 2), (split - 1, blocks // 2, blocks - blocks // 2)]


def trunk_kernel(sizes, *refs):
    per, row_total, split = sizes
    rows = per * 64
    band = per * 8
    (
        ids,
        incoming,
        grad_summed,
        base,
        stats_one,
        stats_six,
        norm_rows,
        proj_t,
        act_three,
        mid_two,
        mid_one,
        stem_out,
        patches,
        proj_a,
        proj_b,
        grad_head,
        mine,
        other,
        trunk,
        grad_two,
        act_two,
        grad_one,
        act_one,
        grad_stem,
        proj_b_pad,
        split_part,
        shared_part,
        sems,
    ) = refs
    mean, rstd = moments(stats_one, row_total)
    low, high = grad_moments(stats_six, row_total)
    factor = rstd * norm_rows[0:1]
    proj_b_pad[...] = jnp.zeros(proj_b_pad.shape, half)
    proj_b_pad[:, 0:C2] = proj_b[...].astype(half)
    proj_a_half = proj_a[...].astype(half)

    def prepare(index, carry):
        at = pl.ds(pl.multiple_of(index * CHUNK, 16), CHUNK)
        unit = (base[at] - mean) * rstd
        value = grad_summed[at] + factor * (incoming[at] - low - unit * high)
        trunk[at] = value.astype(half)
        return carry

    lax.fori_loop(0, rows // CHUNK, prepare, 0)
    tall_chunk = 2 * band

    def step(index, carry):
        at = pl.ds(pl.multiple_of(index * tall_chunk, 16), tall_chunk)
        three = dot(trunk[at], proj_t[...])
        two = (three * gelu_pair(mid_two[at])[1]).astype(half)
        grad_two[at] = two
        value, slope = gelu_pair(mid_one[at])
        act_two[at] = value.astype(half)
        one = (dot(two, proj_b_pad[...], NT) * slope).astype(half)
        grad_one[at] = one
        value, slope = gelu_pair(stem_out[at])
        act_one[at] = value.astype(half)
        grad_stem[at] = (dot(one, proj_a_half, NT) * slope).astype(half)
        return carry

    lax.fori_loop(0, rows // tall_chunk, step, 0)
    place = hot(iota((16, WIDE), 0) + C2 == iota((16, WIDE), 1))
    split_part[...] = (
        dot(trunk[...], act_three[...], TN) + dot(grad_head[...].astype(half), place)
    ).astype(half)
    shared = dot(act_two[...], grad_two[...], TN)
    shared = shared + dot(dot(grad_one[...], act_one[...], TN).astype(half), place)
    stem = dot(patches[...], grad_stem[...], TN).astype(half)
    tall = split_part.shape[0] // (2 * split)
    spot = iota((C1, 32), 0)
    twice = hot((spot % tall == iota((C1, 32), 1)) & (spot % tall < 27))
    place = hot(iota((16, WIDE), 0) + (C2 + 16) == iota((16, WIDE), 1))
    shared = shared + dot(dot(twice, stem).astype(half), place)
    shared_part[...] = shared.astype(half)
    copies = []
    for turn in range(split):
        for side, target in ((0, mine), (1, other)):
            place = pl.multiple_of((ids[2] ^ side) * tall, 16)
            spot = pl.multiple_of((ids[0] ^ turn) * (2 * tall) + (ids[2] ^ side) * tall, 16)
            for block in range(3):
                lanes = pl.ds(block * 128, 128)
                number = 6 * (2 * turn + side) + block
                copies.append(
                    fetch(
                        split_part.at[pl.ds(spot, tall), lanes],
                        target.at[turn, block],
                        sems.at[number],
                    )
                )
                copies.append(
                    fetch(
                        shared_part.at[pl.ds(place, tall), lanes],
                        target.at[turn, 3 + block],
                        sems.at[number + 3],
                    )
                )
    for copy in copies:
        copy.wait()


def norm_kernel(sizes, *refs):
    devices, chips, split = sizes
    ids, one, two, stats_six, stats_five, stats_four, line, local, loss, norm_out = refs
    digit = ids[3] // (chips // 4) % 4
    inner = (digit == 1) | (digit == 2)

    def walk(block, total):
        first = one[block].astype(full)
        second = two[block].astype(full)
        return total + (first * first + second * second)

    blocks = two.shape[0]
    squares = lax.fori_loop(0, blocks, walk, jnp.zeros(one.shape[1:], full))
    squares = jnp.sum(jnp.sum(squares, axis=0, keepdims=True), axis=1, keepdims=True)
    total = jnp.where(inner, squares / (chips // 2), 0.0)
    value = jnp.zeros(one.shape[1:], full)
    for block in range(6):
        lane = iota(value.shape, 1) + block % 3 * 128
        share = 1.0 / chips
        if block >= 3:
            share = jnp.where(
                lane < C2 + 16, 1.0 / (chips * split), 1.0 / (2 * chips * split)
            )
        part = one[blocks + block].astype(full)
        value = value + part * part * share
    value = jnp.where(inner, 2.0 * value, 0.0)
    total = total + jnp.sum(jnp.sum(value, axis=0, keepdims=True), axis=1, keepdims=True)
    norm_out[...] = jnp.zeros(norm_out.shape, full)
    for place, stats in enumerate((stats_six, stats_five, stats_four)):
        sums = jnp.sum(stats[...], axis=0)
        norm_out[2 * place : 2 * place + 1] = sums[:, C3 : 2 * C3]
        norm_out[2 * place + 1 : 2 * place + 2] = sums[:, 0:C3]
        if place == 2:
            loss[...] = sums[:, 2 * C3 : 2 * C3 + 128]
    value = norm_out[...]
    local[...] = pltpu.roll(value, C3 - ids[0] * (C3 // split), 1)[0:6, 0 : C3 // split]
    value = value * value / devices
    total = total + jnp.sum(jnp.sum(value, axis=0, keepdims=True), axis=1, keepdims=True)
    line[...] = jnp.broadcast_to(total[None], line.shape)


def clip_scale(squares):
    total = jnp.sum(jnp.sum(squares[...], axis=0), axis=1, keepdims=True)
    size = jnp.sqrt(total[:, 0:1] / 128.0)
    return (size, jnp.minimum(1.0, clip_limit / size))


def conv_update_kernel(sizes, *refs):
    pieces_count, places, step_rate, rates = sizes
    ids = refs[0]
    squares, weight, first, second = refs[1:5]
    small_in = refs[5:24]
    pieces = refs[24 : 24 + pieces_count]
    first_new, second_new, weight_new = refs[24 + pieces_count : 27 + pieces_count]
    small_out = refs[27 + pieces_count : 46 + pieces_count]
    held, small_held, sems, small_sems = refs[46 + pieces_count :]
    layer = pl.program_id(0)
    line = pl.program_id(1)

    def copies(wanted):
        made = []
        for number, (owner, start, size, side) in enumerate(places):
            if owner not in wanted:
                continue
            tall = pieces[number].shape[1]
            row = pl.multiple_of((ids[2] ^ side) * tall, 16)
            made.append(
                pltpu.make_async_copy(
                    pieces[number].at[0:size],
                    held.at[owner, start : start + size, pl.ds(row, tall), :],
                    sems.at[number],
                )
            )
        return made

    def small_copies():
        blocks = held.shape[1]
        return [
            pltpu.make_async_copy(
                pieces[side].at[blocks : blocks + 6], small_held.at[side], small_sems.at[side]
            )
            for side in range(2)
        ]

    @pl.when((layer == 0) & (line == 0))
    def _():
        for copy in small_copies() + copies((0, 1)):
            copy.start()

    @pl.when((layer == 0) & (line == 1))
    def _():
        for copy in small_copies():
            copy.wait()
        small_update(rates, ids, squares, small_held, small_in, small_out)

    for owner in range(2):

        @pl.when((layer == owner) & (line == 0))
        def _():
            for copy in copies((owner,)):
                copy.wait()

    size, scale = clip_scale(squares)
    for part in range(9):
        lanes = slice(part * 128, part * 128 + 128)
        block = line * 9 + part
        gradient = held[layer, block].astype(full) * scale
        results = adamw(
            weight[0, :, lanes], gradient, first[0, :, lanes], second[0, :, lanes], step_rate
        )
        first_new[0, :, lanes] = results[0]
        second_new[0, :, lanes] = results[1]
        weight_new[0, :, lanes] = results[2]


def small_update(rates, ids, squares, blocks, refs, outs):
    grad_norm_p = refs[0]
    states = refs[1:19]
    size_out = outs[18]
    size, scale = clip_scale(squares)
    size_out[...] = jnp.broadcast_to(size, size_out.shape)
    first_core = ids[2] == 0
    here = blocks[0].astype(full)
    there = blocks[1].astype(full)
    cores = (jnp.where(first_core, here, there), jnp.where(first_core, there, here))
    split_part, shared = [
        jnp.concatenate(
            [
                jnp.concatenate([core[first], core[first + 1], core[first + 2]], axis=1)
                for core in cores
            ],
            axis=0,
        ).astype(half)
        for first in (0, 3)
    ]
    grad_c = split_part[:, 0:C2].astype(full)
    classes = states[12].shape[0]
    pick = hot(iota((classes, WIDE), 0) + C2 == iota((classes, WIDE), 1))
    grad_head = dot(pick, split_part, NT)
    grad_b = shared[:, 0:C2].astype(full)
    pick = hot(iota((C0, WIDE), 0) + C2 == iota((C0, WIDE), 1))
    grad_a = dot(pick, shared, NT)
    pick = hot(iota((C0, WIDE), 0) + (C2 + 16) == iota((C0, WIDE), 1))
    grad_stem = dot(pick, shared[0:32], NT)[:, 0:27]
    gradients = (grad_stem, grad_a, grad_b, grad_c, grad_head, grad_norm_p[...])
    for index in range(6):
        weight, first, second = states[3 * index : 3 * index + 3]
        results = adamw(
            weight[...], gradients[index] * scale, first[...], second[...], rates[index]
        )
        for item in range(3):
            outs[3 * index + item][...] = results[item]


def xor_pairs(size, turn):
    return [(index, index ^ turn) for index in range(size)]


def shards(
    images,
    labels,
    corners,
    partners,
    stem_w,
    stem_w_m,
    stem_w_v,
    proj_a,
    proj_a_m,
    proj_a_v,
    proj_b,
    proj_b_m,
    proj_b_v,
    proj_c,
    proj_c_m,
    proj_c_v,
    conv_w,
    conv_w_m,
    conv_w_v,
    head_w,
    head_w_m,
    head_w_v,
    norm_p,
    norm_p_m,
    norm_p_v,
):
    split = lax.axis_size("dp")
    groups = lax.axis_size("filt")
    chips = groups // 2
    devices = split * groups
    count = images.shape[0]
    per = count // split
    rows = per * 64
    band = per * 8
    image_total = float(count * groups)
    row_total = image_total * 64.0
    tall = conv_w.shape[1] // 2
    spot_d = lax.axis_index("dp")
    spot_f = lax.axis_index("filt")
    ids = jnp.stack([spot_d, spot_f, spot_f % 2, spot_f // 2]).astype(jnp.int32)

    def over_dp(value, turn):
        return lax.ppermute(value, "dp", xor_pairs(split, turn))

    def over_filt(value, turn):
        return lax.ppermute(value, "filt", xor_pairs(groups, turn))

    def exchange(stats):
        return lax.all_to_all(stats, ("dp", "filt"), 0, 0)

    (own_images,) = call(
        image_kernel,
        [VMEM] * 4,
        [(shape((count, 3 * PLANE), half), VMEM)],
        [pltpu.VMEM((8, count), full)],
        3,
    )(
        images.transpose(1, 0, 2),
        labels.reshape(1, count),
        corners.T,
        partners.reshape(1, count),
    )
    far_images = [own_images] + [over_filt(own_images, 2 * turn) for turn in range(1, chips)]

    def start_gather(own):
        return [own, over_dp(own, 1), over_dp(own, 2)]

    def middle_gather(pieces, after):
        rows = pieces[0].shape[0]
        return cut_rows(pieces[:0:-1], [(0, 48), (48, rows - 48)], after)

    def end_gather(pieces, far, after=()):
        far = [over_dp(far[0], 1), over_dp(far[1], 2)]
        if after:
            far = cut_rows(far, [(0, piece.shape[0]) for piece in far], after)
        pieces = [*pieces, *far]
        return pieces + [over_filt(piece, 1) for piece in pieces]

    own_one = cast_half(ids, conv_w, 0, [proj_c.T, head_w.T, norm_p], [own_images])
    own_two = cast_half(ids, conv_w, 1, [], [own_one])
    pieces = start_gather(own_one)
    far = middle_gather(pieces, [])
    all_images = stack(
        far_images,
        [(turn, 0, count) for turn in range(chips)],
        (chips, count, 3 * PLANE),
        [own_two],
    )

    line = shape((devices, 1, 2 * C3))
    patches, stem_out, mid_one, mid_two, act_three, facts = call(
        functools.partial(front_kernel, (per, count, groups, devices, split)),
        [SMEM] + [VMEM] * 5,
        [
            (shape((rows, 32), half), VMEM),
            (shape((rows, C0)), VMEM),
            (shape((rows, C1)), VMEM),
            (shape((rows, WIDE)), VMEM),
            (shape((rows, WIDE), half), VMEM),
            (shape((per, 128)), VMEM),
        ],
        [
            pltpu.VMEM((per, 32, 128), full),
            pltpu.VMEM((rows, 32), full),
            pltpu.VMEM((C0, 32), full),
            pltpu.VMEM((C1, WIDE), half),
        ],
        10,
        1,
    )(ids, all_images, over_filt(all_images, 1), stem_w.T, proj_a, proj_b, far[0])
    kernels = [end_gather(pieces, far, [facts])]
    base, stats, norm_rows, head_all, proj_t = call(
        base_kernel,
        [SMEM, VMEM] + [ANY] * 10,
        [
            (shape((rows, C3)), ANY),
            (line, VMEM),
            (shape((8, C3)), VMEM),
            (shape((C3, 16), half), VMEM),
            (shape((C3, WIDE), half), VMEM),
        ],
        [
            pltpu.VMEM((C3, WIDE), half),
            pltpu.VMEM((rows, C3), full),
            pltpu.VMEM((8, C3), full),
            pltpu.SemaphoreType.DMA((10,)),
            pltpu.SemaphoreType.DMA((QUARTERS,)),
        ],
        4,
    )(ids, act_three, *kernels[0])
    stats_one = exchange(stats)
    pieces = start_gather(hold(own_two, stats_one))

    table = pltpu.VMEM((rows, C3), full)
    conv_outs = [
        (shape((rows, C3)), ANY),
        (shape((rows, C3), half), ANY),
        (shape((rows, C3)), ANY),
        (line, VMEM),
    ]
    conv_scratch = [
        table,
        pltpu.VMEM((C3, 9 * C3), half),
        pltpu.VMEM((rows, TRIPLE), half),
        table,
        table,
        pltpu.SemaphoreType.DMA((10,)),
        pltpu.SemaphoreType.DMA((QUARTERS,)),
        pltpu.SemaphoreType.DMA((QUARTERS + 2,)),
    ]
    conv_one, field_one, slope_one, stats = call(
        functools.partial(conv_kernel, (per, row_total, split), 0),
        [SMEM, ANY, VMEM, VMEM] + [ANY] * 10,
        conv_outs,
        conv_scratch,
        18,
    )(ids, base, stats_one, norm_rows, *kernels[0])
    far = middle_gather(pieces, [stats])
    stats_two = exchange(stats)
    kernels.append(end_gather(pieces, far, [stats_two]))
    far_field_one = over_filt(field_one, 1)
    summed, field_two, slope_two, stats = call(
        functools.partial(conv_kernel, (per, row_total, split), 1),
        [SMEM, ANY, VMEM, VMEM, ANY] + [ANY] * 10,
        conv_outs,
        conv_scratch,
        18,
    )(ids, conv_one, stats_two, norm_rows, base, *kernels[1])
    stats_three = exchange(stats)
    far_field_two = over_filt(field_two, 1)
    slope_three, spread, stats, grad_head = call(
        functools.partial(head_kernel, (per, row_total, image_total, head_w.shape[1])),
        [ANY] + [VMEM] * 4,
        [
            (shape((rows, C3)), ANY),
            (shape((band, C3)), VMEM),
            (shape((devices, 1, 2 * C3 + 128)), VMEM),
            (shape((C3, 16)), VMEM),
        ],
        [pltpu.VMEM((band, C3), full)] * 3
        + [table, table]
        + [pltpu.SemaphoreType.DMA((QUARTERS,)), pltpu.SemaphoreType.DMA((QUARTERS,))],
        7,
    )(summed, stats_three, norm_rows, head_all, facts)
    stats_four = exchange(stats)

    wide_half = pltpu.VMEM((rows, WIDE), half)
    picks = pltpu.VMEM((C3, 2 * WIDE), half)
    half_outs = [(shape((rows, WIDE), half), ANY)] * 2

    def back(layer, heads, tails, after):
        last = layer == 1
        return call(
            functools.partial(back_kernel, (per, row_total, split), layer),
            ([SMEM, ANY, ANY] + [VMEM] * 4 if last else [SMEM, ANY])
            + [ANY, ANY, VMEM]
            + [ANY] * 10,
            [(shape((rows, C3)), ANY), (line, VMEM)]
            + (half_outs + [(shape((rows, C3)), ANY)] if last else []),
            (
                [table, wide_half, wide_half, picks, pltpu.SemaphoreType.DMA((2 * QUARTERS + 1,))]
                if last
                else [pltpu.VMEM((rows, C3), half)]
            )
            + [
                table,
                table,
                pltpu.VMEM((C3, 9 * C3), half),
                pltpu.VMEM((rows, TRIPLE), half),
                table,
                pltpu.SemaphoreType.DMA((10,)),
                pltpu.SemaphoreType.DMA((2 * QUARTERS,)),
                pltpu.SemaphoreType.DMA((QUARTERS,)),
            ],
            22,
            len(after),
        )(ids, *heads, *tails, *kernels[layer], *after)

    grad_conv_one, stats, own_half, far_half, grad_summed = back(
        1,
        [slope_three, summed, stats_three, stats_four, norm_rows, spread],
        [conv_one, slope_two, stats_two],
        [],
    )
    stats_five = exchange(stats)

    def weight_grad(own_half, far_half, field, far_field, chunks, after):
        sizes = [part_sizes(split, lines) for lines in chunks]
        outs = [
            (shape((size, tall, 128), half), ANY) for parts in sizes for _, _, size in parts
        ]
        flat = call(
            functools.partial(weight_grad_kernel, (chunks, split, band)),
            [ANY] * 4,
            outs,
            [
                pltpu.VMEM((2 * rows, WIDE), half),
                pltpu.VMEM((2 * rows, TRIPLE), half),
                pltpu.VMEM((2, rows, C3), half),
                pltpu.VMEM((split, 45, tall, 128), half),
                pltpu.SemaphoreType.DMA((16,)),
                pltpu.SemaphoreType.DMA((16,)),
                pltpu.SemaphoreType.DMA((len(outs),)),
            ],
            13,
            len(after),
        )(own_half, over_filt(far_half, 1), field, far_field, *after)
        result = []
        for parts in sizes:
            result.append(flat[: len(parts)])
            flat = flat[len(parts) :]
        return result

    def add(values):
        return sum(value.astype(full) for value in values).astype(half)

    def start_dp(parts, after):
        own, near, next_near, far_low, far_high = parts
        blocks = near.shape[0]
        cut = far_low.shape[0]
        from_near = over_dp(far_low, 1)
        from_next = over_dp(far_high, 2)
        near, next_near = merge(
            [near, next_near, from_near, from_next],
            [
                (blocks, [(0, 0, 0, blocks), (3, 0, cut, blocks - cut)]),
                (blocks, [(1, 0, 0, blocks), (2, 0, 0, cut)]),
            ],
            after,
            3,
        )
        return [own, near, next_near]

    def end_dp(parts, sizes, after):
        own, near, next_near = parts
        plan = []
        start = 0
        for size in sizes:
            plan.append((size, [(source, start, 0, size) for source in range(3)]))
            start += size
        return merge([own, over_dp(near, 1), over_dp(next_near, 2)], plan, after, 0.1)

    def gated_add(left, right, after):
        if not after:
            return add([left, right])
        size = left.shape[0]
        return merge([left, right], [(size, [(0, 0, 0, size), (1, 0, 0, size)])], after, 0.1)[0]

    def chip_routes(reach):
        routes = []
        for move in ({0: 1, 3: 2}, {1: 2, 2: 1}, {1: 0, 2: 3}):
            pairs = []
            for index in range(groups):
                here = index // 2 // reach % 4
                if here in move:
                    pairs.append((index, index + (move[here] - here) * 2 * reach))
            routes.append(pairs)
        return routes

    def to_middles(value, reach, after):
        arrived = lax.ppermute(value, "filt", chip_routes(reach)[0])
        return gated_add(value, arrived, after)

    def between_middles(value, reach, after):
        return gated_add(value, lax.ppermute(value, "filt", chip_routes(reach)[1]), after)

    def outward(value, reach):
        return lax.ppermute(value, "filt", chip_routes(reach)[2])

    def from_middles(value, reach, after=(), arrived=None):
        if arrived is None:
            arrived = outward(value, reach)
        (result,) = call(
            functools.partial(pick_kernel, reach),
            [SMEM, ANY, ANY],
            [(shape(value.shape, half), VMEM)],
            [pltpu.SemaphoreType.DMA],
            0.1,
            len(after),
        )(ids, value, arrived, *after)
        return result

    def over_more_chips(value, reach):
        while reach < chips:
            value = from_middles(value, reach // 4)
            value = to_middles(value, reach, [])
            value = between_middles(value, reach, [])
            reach *= 4
        return value

    chunks_two = ((0, 1, 2),)
    chunks_one = ((0, 1, 2),)
    pairs_two = weight_grad(
        own_half, far_half, field_two, far_field_two, chunks_two, []
    )
    grad_one_half, own_half_one, far_half_one = call(
        functools.partial(norm_back_kernel, (row_total, split)),
        [SMEM, ANY, ANY, VMEM, VMEM, VMEM],
        [(shape((rows, C3), half), ANY)] + half_outs,
        [
            table,
            table,
            pltpu.VMEM((rows, C3), half),
            wide_half,
            wide_half,
            picks,
            pltpu.SemaphoreType.DMA((2 * QUARTERS,)),
            pltpu.SemaphoreType.DMA((3 * QUARTERS,)),
        ],
        6,
        1,
    )(ids, grad_conv_one, conv_one, stats_two, stats_five, norm_rows, pairs_two[0][0])
    pairs_one = weight_grad(
        own_half_one, far_half_one, field_one, far_field_one, chunks_one, [pairs_two[0][0]]
    )
    begun_two = start_dp(pairs_two[0], [pairs_one[0][0]])
    grad_base, stats = back(
        0,
        [grad_one_half],
        [base, slope_one, stats_one],
        [pairs_one[0][0], begun_two[1]],
    )
    stats_six = exchange(stats)
    begun_one = start_dp(pairs_one[0], [stats_six])
    blocks = begun_one[0].shape[0]
    (part_two,) = end_dp(begun_two, [blocks], [stats_six])
    small = shape((split, 6, tall, 128), half)
    small_mine, small_other = call(
        functools.partial(trunk_kernel, (per, row_total, split)),
        [SMEM] + [VMEM] * 15,
        [(small, ANY), (small, ANY)],
        [
            pltpu.VMEM((rows, C3), half),
            pltpu.VMEM((rows, WIDE), half),
            pltpu.VMEM((rows, C1), half),
            pltpu.VMEM((rows, C1), half),
            pltpu.VMEM((rows, C0), half),
            pltpu.VMEM((rows, C0), half),
            pltpu.VMEM((C1, WIDE), half),
            pltpu.VMEM((C3, WIDE), half),
            pltpu.VMEM((C1, WIDE), half),
            pltpu.SemaphoreType.DMA((12 * split,)),
        ],
        0.1,
        2,
    )(
        ids,
        grad_base,
        grad_summed,
        base,
        stats_one,
        stats_six,
        norm_rows,
        proj_t,
        act_three,
        mid_two,
        mid_one,
        stem_out,
        patches,
        proj_a,
        proj_b,
        grad_head,
        begun_one[1],
        part_two,
    )
    crossed = over_filt(small_other, 1)
    pair = [add([small_mine[turn], crossed[turn]]) for turn in range(split)]
    small_sum = add([pair[0]] + [over_dp(pair[turn], turn) for turn in range(1, split)])
    (part_one,) = end_dp(begun_one, [blocks], [small_mine])
    half_two = to_middles(part_two, 1, [part_one])
    half_one = to_middles(part_one, 1, [half_two, small_sum])
    whole_two = between_middles(half_two, 1, [half_one])
    whole_two = over_more_chips(whole_two, 4)
    last = chips // 4
    small_sum = between_middles(to_middles(small_sum, 1, []), 1, [])
    small_sum = over_more_chips(small_sum, 4)

    arrived_two = outward(whole_two, last)
    terms = [half_one, lax.ppermute(half_one, "filt", chip_routes(1)[1])]
    if chips > 4:
        terms = [over_more_chips(add(terms), 4)]
    plan = [(place, 0, 0, blocks) for place in range(len(terms))]
    plan.append((len(terms), 0, blocks, 6))
    (whole_one,) = merge([*terms, small_sum], [(blocks + 6, plan)], [arrived_two], 0.1)
    reduced_two = from_middles(whole_two, last, [whole_one], arrived_two)
    far_two = over_filt(reduced_two, 1)
    squares, grad_norm_p, loss = call(
        functools.partial(norm_kernel, (devices, chips, split)),
        [SMEM] + [VMEM] * 5,
        [
            (shape((devices, 1, 128)), VMEM),
            (shape((6, C3 // split)), VMEM),
            (shape((1, 128)), VMEM),
        ],
        [pltpu.VMEM((8, C3), full)],
        3,
        1,
    )(ids, whole_one, whole_two, stats_six, stats_five, stats_four, far_two)
    squares = exchange(squares)
    reduced_one = from_middles(whole_one, last, [squares])

    pieces = []
    places = []
    far_one = over_filt(reduced_one, 1)
    for owner, both in enumerate(((reduced_one, far_one), (reduced_two, far_two))):
        pieces += both
        places += [(owner, 0, blocks, side) for side in range(2)]
    whole_spec = pl.BlockSpec((1, 2 * tall, 1152), lambda layer, line: (layer, 0, line))
    conv_shape = shape(conv_w.shape)
    states = (
        (stem_w.T, stem_w_m.T, stem_w_v.T),
        (proj_a, proj_a_m, proj_a_v),
        (proj_b, proj_b_m, proj_b_v),
        (proj_c.T, proj_c_m.T, proj_c_v.T),
        (head_w.T, head_w_m.T, head_w_v.T),
        (norm_p, norm_p_m, norm_p_v),
    )
    rates = (
        0.7 / math.sqrt(27.0),
        0.7 / math.sqrt(C0),
        0.7 / math.sqrt(C1),
        0.7 / math.sqrt(C2),
        0.7 / math.sqrt(C3 / 8.0),
        0.8,
    )
    flat = [item for group in states for item in group]
    updated = pl.pallas_call(
        functools.partial(
            conv_update_kernel, (len(pieces), places, 0.7 / math.sqrt(9.0 * C3), rates)
        ),
        grid=(2, 5),
        in_specs=[SMEM, VMEM, whole_spec, whole_spec, whole_spec]
        + [VMEM] * 19
        + [ANY] * len(pieces),
        out_specs=[whole_spec] * 3 + [VMEM] * 19,
        out_shape=[conv_shape] * 3 + [shape(item.shape) for item in flat] + [shape((1, 128))],
        scratch_shapes=[
            pltpu.VMEM((2, 45, 2 * tall, 128), half),
            pltpu.VMEM((2, 6, tall, 128), half),
            pltpu.SemaphoreType.DMA((len(pieces),)),
            pltpu.SemaphoreType.DMA((2,)),
        ],
        compiler_params=pltpu.CompilerParams(vmem_limit_bytes=63 * MIB),
        cost_estimate=pl.CostEstimate(
            flops=20 * conv_w.size, bytes_accessed=26 * conv_w.size, transcendentals=0
        ),
    )(
        ids,
        squares,
        conv_w,
        conv_w_m,
        conv_w_v,
        grad_norm_p,
        *flat,
        *pieces,
    )
    conv_new, small_new = updated[0:3], updated[3:]
    size = small_new[18][0, 0]
    turned = [
        item.T if index // 3 in (0, 3, 4) else item for index, item in enumerate(small_new[:18])
    ]
    return (
        *turned[0:12],
        *conv_new,
        *turned[12:18],
        loss[0, 0],
        size,
    )


def solution(mesh):
    placed = (
        P("filt", None, None),
        P("filt"),
        P("filt", None),
        P("filt"),
        *([P()] * 9),
        *([P(None, "dp")] * 3),
        *([P(None, "dp", None)] * 3),
        *([P("dp", None)] * 3),
        *([P(None, "dp")] * 3),
    )
    return jax.shard_map(
        shards,
        mesh=mesh,
        in_specs=placed,
        out_specs=(
            *([P()] * 9),
            *([P(None, "dp")] * 3),
            *([P(None, "dp", None)] * 3),
            *([P("dp", None)] * 3),
            *([P(None, "dp")] * 3),
            P(),
            P(),
        ),
        check_vma=False,
    )
```

```python
import functools
import math

import jax
import jax.numpy as jnp
from jax import lax
from jax.experimental import pallas as pl
from jax.experimental.pallas import tpu as pltpu
from jax.sharding import PartitionSpec as P

C0 = 16
C1 = 160
C2 = 320
C3 = 640
WIDE = 384
TRIPLE = 3 * C3
SIDE = 32
CUT = 16
STEP = 10
PLANE = 640
META = 576
CHUNK = 48
QUARTERS = 4

beta_one = 0.9
beta_two = 0.999
adam_eps = 1e-08
weight_decay = 0.0005
clip_limit = 0.05
norm_eps = 1e-05
gelu_one = math.sqrt(2.0 / math.pi)
gelu_three = 0.044715 * gelu_one

half = jnp.bfloat16
full = jnp.float32
NT = (((1,), (1,)), ((), ()))
NN = (((1,), (0,)), ((), ()))
TN = (((0,), (0,)), ((), ()))
VMEM = pl.BlockSpec(memory_space=pltpu.VMEM)
SMEM = pl.BlockSpec(memory_space=pltpu.SMEM)
ANY = pl.BlockSpec(memory_space=pl.ANY)
MIB = 2**20


def shape(dims, kind=full):
    return jax.ShapeDtypeStruct(dims, kind)


def dot(left, right, dims=NN):
    return lax.dot_general(left, right, dims, preferred_element_type=full)


def iota(dims, axis):
    return lax.broadcasted_iota(jnp.int32, dims, axis)


def hot(condition):
    return condition.astype(full).astype(half)


def call(kernel, ins, outs, scratch, micros, after=0):
    used = len(ins)

    def body(*refs):
        kernel(*refs[:used], *refs[used + after :])

    return pl.pallas_call(
        body,
        out_shape=[item[0] for item in outs],
        in_specs=ins + [ANY] * after,
        out_specs=[item[1] for item in outs],
        scratch_shapes=scratch,
        cost_estimate=pl.CostEstimate(
            flops=int(micros * 35 * 10**7), bytes_accessed=1, transcendentals=0
        ),
        compiler_params=pltpu.CompilerParams(vmem_limit_bytes=63 * MIB),
    )


def gelu_pair(values):
    square = values * values
    bent = jnp.tanh(values * (gelu_one + gelu_three * square))
    gate = 0.5 + 0.5 * bent
    slope = gate + (0.5 * values) * (1.0 - bent * bent) * (gelu_one + (3.0 * gelu_three) * square)
    return (values * gate, slope)


def adamw(weight, gradient, first, second, step_rate):
    first_new = beta_one * first + (1.0 - beta_one) * gradient
    second_new = beta_two * second + (1.0 - beta_two) * (gradient * gradient)
    second_hat = second_new * (1.0 / (1.0 - beta_two**STEP))
    root = second_hat * lax.rsqrt(second_hat) + adam_eps
    weight_new = weight * (1.0 - step_rate * weight_decay) - (
        step_rate / (1.0 - beta_one**STEP)
    ) * (first_new / root)
    return (first_new, second_new, weight_new)


def fetch(source, target, sem):
    copy = pltpu.make_async_copy(source, target, sem)
    copy.start()
    return copy


def lane_pixel(lanes):
    tap = lanes // 64
    cell = lanes % 64
    row = 4 * (cell // 8) + tap // 3 - 1
    col = 4 * (cell % 8) + tap % 3 - 1
    return (tap, row, col)


def image_kernel(planes, labels, corners, partners, out, numbers):
    count = planes.shape[1]
    tap, row, col = lane_pixel(iota((1, PLANE), 1))
    pixel = jnp.where((row >= 0) & (col >= 0) & (tap < 9), row * SIDE + col, -1)
    pick = hot(iota((SIDE * SIDE, PLANE), 0) == pixel)
    numbers[...] = jnp.zeros(numbers.shape, full)
    numbers[0:1] = labels[...].astype(full)
    numbers[1:3] = corners[...].astype(full)
    numbers[3:4] = (partners[...] // count).astype(full)
    numbers[4:5] = (partners[...] % count).astype(full)
    place = hot(iota((8, PLANE), 0) + META == iota((8, PLANE), 1))
    for colour in range(3):
        taken = dot(planes[colour], pick)
        if colour == 0:
            taken = taken + dot(numbers[...].astype(half), place, TN)
        out[:, colour * PLANE : (colour + 1) * PLANE] = taken.astype(half)


def pack_lanes(proj_c, head, norm):
    place = hot(iota((C2, WIDE), 0) == iota((C2, WIDE), 1))
    total = dot(proj_c[...].astype(half), place)
    classes = head.shape[0]
    place = hot(iota((classes, WIDE), 0) + C2 == iota((classes, WIDE), 1))
    total = total + dot(head[...].astype(half), place, TN)
    rest = norm[...]
    for part in range(3):
        piece = rest.astype(half)
        rest = rest - piece.astype(full)
        place = hot(iota((6, WIDE), 0) + (C2 + 16 + 8 * part) == iota((6, WIDE), 1))
        total = total + dot(piece, place, TN)
    return total


def cast_kernel(layer, *refs):
    ids, weights = refs[0:2]
    wide, narrow, in_sems, out_sems = refs[-4:]
    out = refs[5] if layer == 0 else refs[2]
    rows = out.shape[0]
    cols = wide.shape[1]
    parts = rows // 16
    inputs = []
    for part in range(parts):
        spot = pl.multiple_of(ids[2] * rows + part * 16, 16)
        inputs.append(
            fetch(
                weights.at[layer, pl.ds(spot, 16)],
                wide.at[part * 16 : part * 16 + 16],
                in_sems.at[part],
            )
        )
    if layer == 0:
        total = pack_lanes(*refs[2:5])
        mine = jnp.where(ids[2] == 0, total[0:rows], total[rows : 2 * rows])
        narrow[:, cols : cols + WIDE] = mine.astype(half)
        refs[6][...] = total.astype(half)
    outputs = []
    for part in range(parts):
        here = slice(part * 16, part * 16 + 16)
        inputs[part].wait()
        narrow[here, 0:cols] = wide[here].astype(half)
        outputs.append(fetch(narrow.at[here], out.at[here], out_sems.at[part]))
    for copy in outputs:
        copy.wait()


def cast_half(ids, conv_w, layer, packed, after):
    rows = conv_w.shape[1] // 2
    cols = conv_w.shape[2]
    total = cols + WIDE if layer == 0 else cols
    return call(
        functools.partial(cast_kernel, layer),
        [SMEM, ANY] + [VMEM] * len(packed),
        [(shape((rows, total), half), ANY)]
        + ([(shape((2 * rows, WIDE), half), VMEM)] if layer == 0 else []),
        [
            pltpu.VMEM((rows, cols), full),
            pltpu.VMEM((rows, total), half),
            pltpu.SemaphoreType.DMA((rows // 16,)),
            pltpu.SemaphoreType.DMA((rows // 16,)),
        ],
        3,
        len(after),
    )(ids, conv_w, *packed, *after)


def hold_kernel(*refs):
    pass


def hold(value, after):
    return pl.pallas_call(
        hold_kernel,
        out_shape=shape(value.shape, value.dtype),
        in_specs=[ANY] * 2,
        out_specs=ANY,
        input_output_aliases={0: 0},
        compiler_params=pltpu.CompilerParams(has_side_effects=True),
        cost_estimate=pl.CostEstimate(flops=1, bytes_accessed=1, transcendentals=0),
    )(value, after)


def merge_spans(plan):
    spans = []
    for out, (size, terms) in enumerate(plan):
        edges = {0, size}
        for _, _, start, length in terms:
            edges |= {start, start + length}
        edges = sorted(edges)
        for low, high in zip(edges[:-1], edges[1:]):
            used = [
                (source, first - start)
                for source, first, start, length in terms
                if start <= low and high <= start + length
            ]
            for begin in range(low, high, 8):
                spans.append((out, begin, min(8, high - begin), used))
    return spans


def merge_kernel(plan, count, *refs):
    values = refs[:count]
    results = refs[count : count + len(plan)]
    held = refs[count + len(plan) : 2 * count + len(plan)]
    kept = refs[2 * count + len(plan) : 2 * (count + len(plan))]
    in_sems, out_sems = refs[2 * (count + len(plan)) :]
    arrivals = []
    number = 0
    for _, begin, size, used in merge_spans(plan):
        copies = []
        for source, shift in used:
            here = slice(begin + shift, begin + shift + size)
            copies.append(
                fetch(values[source].at[here], held[source].at[here], in_sems.at[number])
            )
            number += 1
        arrivals.append(copies)
    departures = []
    for (out, begin, size, used), copies in zip(merge_spans(plan), arrivals):
        for copy in copies:
            copy.wait()
        total = None
        for source, shift in used:
            value = held[source][begin + shift : begin + shift + size].astype(full)
            total = value if total is None else total + value
        here = slice(begin, begin + size)
        kept[out][here] = total.astype(half)
        departures.append(
            fetch(kept[out].at[here], results[out].at[here], out_sems.at[len(departures)])
        )
    for copy in departures:
        copy.wait()


def merge(values, plan, after, micros):
    dims = values[0].shape[1:]
    spans = merge_spans(plan)
    return call(
        functools.partial(merge_kernel, plan, len(values)),
        [ANY] * len(values),
        [(shape((size,) + dims, half), ANY) for size, _ in plan],
        [pltpu.VMEM(value.shape, half) for value in values]
        + [pltpu.VMEM((size,) + dims, half) for size, _ in plan]
        + [
            pltpu.SemaphoreType.DMA((sum(len(used) for _, _, _, used in spans),)),
            pltpu.SemaphoreType.DMA((len(spans),)),
        ],
        micros,
        len(after),
    )(*values, *after)


def pick_kernel(reach, ids, value, arrived, out, sem):
    digit = ids[3] // reach % 4
    outer = (digit == 0) | (digit == 3)

    @pl.when(outer)
    def _():
        fetch(arrived, out, sem).wait()

    @pl.when(jnp.logical_not(outer))
    def _():
        fetch(value, out, sem).wait()


def cut_kernel(places, *refs):
    count = len(places)
    outs = refs[count : 2 * count]
    sems = refs[2 * count]
    copies = []
    for index, (start, size) in enumerate(places):
        copies.append(
            fetch(
                refs[index].at[start : start + size, 0 : 9 * C3], outs[index], sems.at[index]
            )
        )
    for copy in copies:
        copy.wait()


def cut_rows(values, places, after):
    cols = 9 * C3
    return call(
        functools.partial(cut_kernel, places),
        [ANY] * len(values),
        [(shape((size, cols), half), VMEM) for _, size in places],
        [pltpu.SemaphoreType.DMA((len(values),))],
        1,
        len(after),
    )(*values, *after)


def stack_kernel(places, *refs):
    count = len(places)
    out, sems = refs[count:]
    copies = []
    for index, (slot, start, size) in enumerate(places):
        copy = pltpu.make_async_copy(
            refs[index], out.at[slot, start : start + size], sems.at[index]
        )
        copy.start()
        copies.append(copy)
    for copy in copies:
        copy.wait()


def stack(pieces, places, dims, after):
    (result,) = call(
        functools.partial(stack_kernel, places),
        [ANY] * len(pieces),
        [(shape(dims, half), VMEM)],
        [pltpu.SemaphoreType.DMA((len(pieces),))],
        3,
        len(after),
    )(*pieces, *after)
    return result


def front_kernel(sizes, *refs):
    per, count, groups, devices, split = sizes
    rows = per * 64
    band = per * 8
    ids = refs[0]
    images, far_images, stem_w, proj_a, proj_b = refs[1:6]
    (
        patches,
        stem_out,
        mid_one,
        mid_two,
        act_three,
        facts,
        tiles,
        loose,
        stem_pad,
        proj_b_pad,
    ) = refs[6:]
    slot = iota((per, count), 0)
    column = iota((per, count), 1)
    own = dot(hot(column == slot + ids[0] * per), images[0])
    group_of = own[:, META + 3 : META + 4].astype(jnp.int32)
    local_of = own[:, META + 4 : META + 5].astype(jnp.int32)
    turn_of = group_of ^ ids[1]
    other = jnp.zeros((per, 3 * PLANE), full)
    for turn in range(groups):
        source = far_images[turn // 2] if turn % 2 else images[turn // 2]
        other = other + dot(hot((turn_of == turn) & (column == local_of)), source)
    top = own[:, META + 1 : META + 2]
    left = own[:, META + 2 : META + 3]
    tap, row, col = lane_pixel(iota((1, 3 * PLANE), 1) % PLANE)
    row = row.astype(full)
    col = col.astype(full)
    inside = (row >= top) & (row < top + CUT) & (col >= left) & (col < left + CUT) & (tap < 9)
    blended = jnp.where(inside, other, own)
    tall = jnp.maximum(jnp.minimum(top + CUT, float(SIDE)) - jnp.maximum(top, 0.0), 0.0)
    broad = jnp.maximum(jnp.minimum(left + CUT, float(SIDE)) - jnp.maximum(left, 0.0), 0.0)
    share = 1.0 - tall * broad / float(SIDE * SIDE)
    lanes = iota((per, 128), 1)
    facts[...] = jnp.where(
        lanes == 0,
        own[:, META : META + 1],
        jnp.where(lanes == 1, other[:, META : META + 1], share),
    )
    tiles[...] = jnp.zeros(tiles.shape, full)
    for piece in range(15):
        tiles[:, piece, :] = blended[:, piece * 128 : (piece + 1) * 128]
    tiles[:, 16:32, :] = pltpu.roll(tiles[:, 0:16, :], 64, 2)
    spot = iota((32, 32), 0)
    tap_at = ((spot % 16) % 5) * 2 + spot // 16
    colour_at = (spot % 16) // 5
    order = hot(
        (iota((32, 32), 1) == tap_at * 3 + colour_at) & (tap_at < 9) & (spot % 16 < 15)
    )
    for image in range(per):
        cells = dot(tiles[image].astype(half), order, TN)
        for line in range(8):
            loose[line * band + image * 8 : line * band + image * 8 + 8, :] = cells[
                line * 8 : line * 8 + 8
            ]
    patches[...] = loose[...].astype(half)
    stem_pad[...] = jnp.zeros(stem_pad.shape, full)
    stem_pad[:, 0:27] = stem_w[...]
    proj_b_pad[...] = jnp.zeros(proj_b_pad.shape, half)
    proj_b_pad[:, 0:C2] = proj_b[...].astype(half)
    stem_half = stem_pad[...].astype(half)
    proj_a_half = proj_a[...].astype(half)
    tall_chunk = 2 * band

    def step(index, carry):
        at = pl.ds(pl.multiple_of(index * tall_chunk, 16), tall_chunk)
        stem = dot(patches[at], stem_half, NT)
        stem_out[at] = stem
        one = dot(gelu_pair(stem)[0].astype(half), proj_a_half)
        mid_one[at] = one
        two = dot(gelu_pair(one)[0].astype(half), proj_b_pad[...])
        mid_two[at] = two
        act_three[at] = gelu_pair(two)[0].astype(half)
        return carry

    lax.fori_loop(0, rows // tall_chunk, step, 0)


def base_kernel(*refs):
    ids, act_three = refs[0:2]
    pieces = refs[2:8]
    far_pack = refs[8]
    base, stats, norm_rows, head_all, proj_t, gathered, held, totals, sems, out_sems = refs[9:]
    rows = act_three.shape[0]
    tall = pieces[0].shape[0]
    spot = pl.multiple_of((ids[0] ^ 3) * (2 * tall), 16)
    copies = [fetch(far_pack, gathered.at[pl.ds(spot, 2 * tall)], sems.at[6])]
    for side in range(2):
        for turn in range(3):
            piece = pieces[3 * side + turn]
            lanes = pl.ds(piece.shape[1] - WIDE, WIDE)
            spot = (ids[0] ^ turn) * (2 * tall) + (ids[2] ^ side) * tall
            copies.append(
                fetch(
                    piece.at[:, lanes],
                    gathered.at[pl.ds(pl.multiple_of(spot, 16), tall)],
                    sems.at[3 * side + turn],
                )
            )
    for copy in copies:
        copy.wait()
    column = iota((1, WIDE), 1)
    packed = gathered[...]
    proj_t[...] = jnp.where(column < C2, packed.astype(full), 0.0).astype(half)
    place = hot(iota((WIDE, 16), 0) == iota((WIDE, 16), 1) + C2)
    head_all[...] = dot(packed, place).astype(half)
    column = iota((8, WIDE), 1)
    name = iota((8, WIDE), 0)
    pieces = [
        dot(hot((column == name + (C2 + 16 + 8 * part)) & (name < 6)), packed, NT)
        for part in range(3)
    ]
    norm_rows[...] = pieces[0] + (pieces[1] + pieces[2])
    totals[...] = jnp.zeros(totals.shape, full)
    outputs = []
    for part in range(QUARTERS):
        at = quarter_rows(rows, part)
        result = dot(act_three[at], proj_t[...], NT)
        held[at] = result
        outputs.append(fetch(held.at[at], base.at[at], out_sems.at[part]))
        totals[0:1] += jnp.sum(result, axis=0, keepdims=True)
        totals[1:2] += jnp.sum(result * result, axis=0, keepdims=True)
    spread_stats(stats, [totals[0:1], totals[1:2]])
    for copy in outputs:
        copy.wait()


def spread_stats(out, parts):
    line = jnp.concatenate(parts, axis=1)
    out[...] = jnp.broadcast_to(line[None], out.shape)


def moments(stats, row_total):
    line = jnp.sum(stats[...], axis=0)
    mean = line[:, 0:C3] / row_total
    rstd = lax.rsqrt(line[:, C3 : 2 * C3] / row_total - mean * mean + norm_eps)
    return (mean, rstd)


def quarter_rows(rows, part):
    step = rows // QUARTERS
    return pl.ds(part * step, step)


def fetch_quarter(source, target, sem, part):
    here = quarter_rows(source.shape[0], part)
    return fetch(source.at[here], target.at[here], sem)


def walk_quarter(rows, part, body, carry):
    step = rows // QUARTERS // CHUNK
    return lax.fori_loop(part * step, (part + 1) * step, body, carry)


def start_weights(ids, pieces, weights, sems):
    rows = pieces[0].shape[0]
    low = pieces[3].shape[0]
    copies = []
    for side in range(2):
        for place in range(5):
            piece = pieces[5 * side + place]
            turn = min(place, 3)
            spot = (ids[0] ^ turn) * (2 * rows) + (ids[2] ^ side) * rows
            if place == 4:
                spot = spot + low
            spot = pl.multiple_of(spot, 16)
            copies.append(
                fetch(
                    piece.at[:, 0 : 9 * C3],
                    weights.at[pl.ds(spot, piece.shape[0])],
                    sems.at[5 * side + place],
                )
            )
    return copies


def shifted(values, by):
    block = values.reshape(CHUNK // 8, 8, C3)
    place = iota((1, 8, 1), 1)
    if by == 1:
        moved = jnp.where(place == 0, 0.0, pltpu.roll(block, 1, 1))
    else:
        moved = jnp.where(place == 7, 0.0, pltpu.roll(block, 7, 1))
    return moved.reshape(CHUNK, C3)


def conv_kernel(sizes, layer, *refs):
    per, row_total, split = sizes
    rows = per * 64
    band = per * 8
    ids, source, stats_in, norm_rows = refs[0:4]
    offset = 4
    if layer == 1:
        base = refs[4]
        offset = 5
    pieces = refs[offset : offset + 10]
    offset += 10
    (result, field_out, slope_out, stats, held, weights, field, slope, total) = refs[
        offset : offset + 9
    ]
    weight_sems, in_sems, out_sems = refs[offset + 9 : offset + 12]
    inputs = [fetch_quarter(source, held, in_sems.at[part], part) for part in range(QUARTERS)]
    copies = start_weights(ids, pieces, weights, weight_sems)
    mean, rstd = moments(stats_in, row_total)
    factor = rstd * norm_rows[2 * layer : 2 * layer + 1]
    shift = norm_rows[2 * layer + 1 : 2 * layer + 2] - mean * factor

    def prepare(index, carry):
        at = pl.ds(pl.multiple_of(index * CHUNK, 16), CHUNK)
        value, gradient = gelu_pair(held[at] * factor + shift)
        slope[at] = gradient
        field[at, 0:C3] = shifted(value, 1).astype(half)
        field[at, C3 : 2 * C3] = value.astype(half)
        field[at, 2 * C3 : TRIPLE] = shifted(value, -1).astype(half)
        return carry

    for part in range(QUARTERS):
        inputs[part].wait()
        walk_quarter(rows, part, prepare, 0)
    outputs = [
        fetch(field.at[:, C3 : 2 * C3], field_out, out_sems.at[QUARTERS]),
        fetch(slope, slope_out, out_sems.at[QUARTERS + 1]),
    ]
    if layer == 1:
        inputs = [fetch_quarter(base, held, in_sems.at[part], part) for part in range(QUARTERS)]
    for copy in copies:
        copy.wait()
    inner = rows - band
    total[...] = dot(field[...], weights[:, TRIPLE : 2 * TRIPLE], NT)
    total[band:rows] += dot(field[0:inner], weights[:, 0:TRIPLE], NT)
    total[0:inner] += dot(field[band:rows], weights[:, 2 * TRIPLE : 3 * TRIPLE], NT)

    def count(index, carry):
        at = pl.ds(pl.multiple_of(index * CHUNK, 16), CHUNK)
        value = total[at]
        if layer == 1:
            value = value + held[at]
            total[at] = value
        return (
            carry[0] + jnp.sum(value.reshape(CHUNK // 8, 8, C3), axis=0),
            carry[1] + jnp.sum((value * value).reshape(CHUNK // 8, 8, C3), axis=0),
        )

    zero = jnp.zeros((8, C3), full)
    sums = (zero, zero)
    for part in range(QUARTERS):
        if layer == 1:
            inputs[part].wait()
        else:
            outputs.append(fetch_quarter(total, result, out_sems.at[part], part))
        sums = walk_quarter(rows, part, count, sums)
        if layer == 1:
            outputs.append(fetch_quarter(total, result, out_sems.at[part], part))
    spread_stats(stats, [jnp.sum(item, axis=0, keepdims=True) for item in sums])
    for copy in outputs:
        copy.wait()


def head_kernel(sizes, *refs):
    per, row_total, image_total, classes = sizes
    rows = per * 64
    band = per * 8
    (
        source,
        stats_in,
        norm_rows,
        head_all,
        facts,
        slope_out,
        spread,
        stats,
        grad_head,
        sum_value,
        sum_slope,
        sum_cross,
        summed,
        slope,
        in_sems,
        out_sems,
    ) = refs
    inputs = [fetch_quarter(source, summed, in_sems.at[part], part) for part in range(QUARTERS)]
    mean, rstd = moments(stats_in, row_total)
    gain = norm_rows[4:5]
    bias = norm_rows[5:6]
    sum_value[...] = jnp.zeros((band, C3), full)
    sum_slope[...] = jnp.zeros((band, C3), full)
    sum_cross[...] = jnp.zeros((band, C3), full)

    def walk(index, carry):
        for part in range(band // CHUNK):
            at = pl.ds(pl.multiple_of(index * band + part * CHUNK, 16), CHUNK)
            here = slice(part * CHUNK, part * CHUNK + CHUNK)
            unit = (summed[at] - mean) * rstd
            value, gradient = gelu_pair(unit * gain + bias)
            slope[at] = gradient
            sum_value[here] += value
            sum_slope[here] += gradient
            sum_cross[here] += gradient * unit
        return carry

    outputs = []
    for part in range(QUARTERS):
        inputs[part].wait()
        lax.fori_loop(2 * part, 2 * part + 2, walk, 0)
        outputs.append(fetch_quarter(slope, slope_out, out_sems.at[part], part))

    def by_image(ref):
        return jnp.sum(ref[...].reshape(per, 8, C3), axis=1)

    pooled = (by_image(sum_value) / 64.0).astype(half)
    logits = dot(pooled, head_all[...])
    lanes = iota((per, 16), 1)
    inside = lanes < classes
    own = facts[:, 0:1].astype(jnp.int32)
    other = facts[:, 1:2].astype(jnp.int32)
    share = facts[:, 2:3]
    target = jnp.where(lanes == own, share, 0.0) + jnp.where(lanes == other, 1.0 - share, 0.0)
    top = jnp.max(jnp.where(inside, logits, -3e38), axis=1, keepdims=True)
    powers = jnp.where(inside, jnp.exp(jnp.where(inside, logits - top, 0.0)), 0.0)
    lse = top + jnp.log(jnp.sum(powers, axis=1, keepdims=True))
    losses = lse - jnp.sum(target * logits, axis=1, keepdims=True)
    loss = jnp.sum(losses, axis=0, keepdims=True)
    soft = jnp.where(inside, jnp.exp(jnp.where(inside, logits - lse, 0.0)), 0.0)
    grad_logits = ((soft - target) / image_total).astype(half)
    grad_head[...] = dot(pooled, grad_logits, TN)
    pull = dot(grad_logits, head_all[...], NT) / 64.0
    spread[...] = jnp.broadcast_to(pull[:, None, :], (per, 8, C3)).reshape(band, C3)
    bias_sum = jnp.sum(pull * by_image(sum_slope), axis=0, keepdims=True)
    gain_sum = jnp.sum(pull * by_image(sum_cross), axis=0, keepdims=True)
    spread_stats(stats, [bias_sum, gain_sum, jnp.broadcast_to(loss, (1, 128))])
    for copy in outputs:
        copy.wait()


def grad_moments(stats, row_total):
    line = jnp.sum(stats[...], axis=0)
    return (line[:, 0:C3] / row_total, line[:, C3 : 2 * C3] / row_total)


def input_grad(gradient, weights, out, band):
    rows = gradient.shape[0]
    inner = rows - band
    spans = (
        (1, slice(0, rows), slice(0, rows)),
        (0, slice(0, inner), slice(band, rows)),
        (2, slice(band, rows), slice(0, inner)),
    )
    for line, to, of in spans:
        for col in range(3):
            tap = 3 * line + col
            part = dot(
                gradient[of, col * C3 : (col + 1) * C3], weights[:, tap * C3 : (tap + 1) * C3]
            )
            if line == 1 and col == 0:
                out[to] = part
            else:
                out[to] += part


def half_filters(ids, split):
    tall = C3 // (2 * split)
    place = iota((1, 2 * WIDE), 1)
    side = jnp.where(place < WIDE, 0, 1)
    place = place - side * WIDE
    target = (ids[0] ^ (place // tall)) * (2 * tall) + (ids[2] ^ side) * tall + place % tall
    target = jnp.where(place < C3 // 2, target, -1)
    return hot(iota((C3, 2 * WIDE), 0) == target)


def norm_back(arriving, unit, factor, low, high):
    return factor * (arriving - low - unit * high)


def send_halves(middle, pick, helds, halves, sems, part):
    here = quarter_rows(helds[0].shape[0], part)
    both = dot(middle, pick).astype(half)
    copies = []
    for side in range(2):
        helds[side][here] = both[:, side * WIDE : (side + 1) * WIDE]
        copies.append(
            fetch(helds[side].at[here], halves[side].at[here], sems.at[2 * part + side])
        )
    return copies


def back_kernel(sizes, layer, *refs):
    per, row_total, split = sizes
    rows = per * 64
    band = per * 8
    last = layer == 1
    ids = refs[0]
    if last:
        incoming, source, stats_here, stats_grad, norm_rows, spread = refs[1:7]
        offset = 7
    else:
        incoming = refs[1]
        offset = 2
    before, slope_before, stats_before = refs[offset : offset + 3]
    pieces = refs[offset + 3 : offset + 13]
    result, stats = refs[offset + 13 : offset + 15]
    offset += 15
    if last:
        own_half, far_half, grad_out, kept, own_held, far_held, pick, half_sems = refs[
            offset : offset + 8
        ]
        offset += 8
    else:
        arrived = refs[offset]
        offset += 1
    held, origin, weights, gradient, total = refs[offset : offset + 5]
    weight_sems, in_sems, out_sems = refs[offset + 5 : offset + 8]
    inputs = []
    for part in range(QUARTERS):
        if last:
            inputs.append(
                (
                    fetch_quarter(incoming, held, in_sems.at[2 * part], part),
                    fetch_quarter(source, origin, in_sems.at[2 * part + 1], part),
                )
            )
        else:
            inputs.append((fetch_quarter(incoming, arrived, in_sems.at[2 * part], part),))
    copies = start_weights(ids, pieces, weights, weight_sems)
    if last:
        mean, rstd = moments(stats_here, row_total)
        low, high = grad_moments(stats_grad, row_total)
        factor = rstd * norm_rows[4:5]
        parts = band // CHUNK
        pick[...] = half_filters(ids, split)

    def prepare(index, carry):
        at = pl.ds(pl.multiple_of(index * CHUNK, 16), CHUNK)
        if last:
            here = pl.ds(pl.multiple_of(lax.rem(index, parts) * CHUNK, 16), CHUNK)
            unit = (origin[at] - mean) * rstd
            value = norm_back(held[at] * spread[here], unit, factor, low, high)
            kept[at] = value
            gradient[at, C3 : 2 * C3] = value.astype(half)
        else:
            gradient[at, C3 : 2 * C3] = arrived[at]
            value = arrived[at].astype(full)
        gradient[at, 0:C3] = shifted(value, -1).astype(half)
        gradient[at, 2 * C3 : TRIPLE] = shifted(value, 1).astype(half)
        return carry

    for part in range(QUARTERS):
        for copy in inputs[part]:
            copy.wait()
        walk_quarter(rows, part, prepare, 0)
    outputs = []
    if last:
        outputs.append(fetch(kept, grad_out, half_sems.at[2 * QUARTERS]))
        for part in range(QUARTERS):
            outputs += send_halves(
                gradient[quarter_rows(rows, part), C3 : 2 * C3],
                pick[...],
                (own_held, far_held),
                (own_half, far_half),
                half_sems,
                part,
            )
    inputs = []
    for part in range(QUARTERS):
        inputs.append(
            (
                fetch_quarter(before, origin, in_sems.at[2 * part], part),
                fetch_quarter(slope_before, held, in_sems.at[2 * part + 1], part),
            )
        )
    for copy in copies:
        copy.wait()
    input_grad(gradient, weights, total, band)
    mean, rstd = moments(stats_before, row_total)

    def finish(index, carry):
        at = pl.ds(pl.multiple_of(index * CHUNK, 16), CHUNK)
        value = total[at] * held[at]
        total[at] = value
        unit = (origin[at] - mean) * rstd
        return (
            carry[0] + jnp.sum(value.reshape(CHUNK // 8, 8, C3), axis=0),
            carry[1] + jnp.sum((value * unit).reshape(CHUNK // 8, 8, C3), axis=0),
        )

    zero = jnp.zeros((8, C3), full)
    sums = (zero, zero)
    for part in range(QUARTERS):
        for copy in inputs[part]:
            copy.wait()
        sums = walk_quarter(rows, part, finish, sums)
        outputs.append(fetch_quarter(total, result, out_sems.at[part], part))
    spread_stats(stats, [jnp.sum(item, axis=0, keepdims=True) for item in sums])
    for copy in outputs:
        copy.wait()


def norm_back_kernel(sizes, *refs):
    row_total, split = sizes
    ids, incoming, source, stats_here, stats_grad, norm_rows = refs[0:6]
    grad_half, own_half, far_half = refs[6:9]
    held, origin, middle, own_held, far_held, pick, in_sems, out_sems = refs[9:]
    rows = held.shape[0]
    inputs = []
    for part in range(QUARTERS):
        inputs.append(
            (
                fetch_quarter(incoming, held, in_sems.at[2 * part], part),
                fetch_quarter(source, origin, in_sems.at[2 * part + 1], part),
            )
        )
    mean, rstd = moments(stats_here, row_total)
    low, high = grad_moments(stats_grad, row_total)
    factor = rstd * norm_rows[2:3]
    pick[...] = half_filters(ids, split)

    def prepare(index, carry):
        at = pl.ds(pl.multiple_of(index * CHUNK, 16), CHUNK)
        unit = (origin[at] - mean) * rstd
        middle[at] = norm_back(held[at], unit, factor, low, high).astype(half)
        return carry

    outputs = []
    for part in range(QUARTERS):
        for copy in inputs[part]:
            copy.wait()
        walk_quarter(rows, part, prepare, 0)
        here = quarter_rows(rows, part)
        outputs.append(fetch(middle.at[here], grad_half.at[here], out_sems.at[8 + part]))
        outputs += send_halves(
            middle[here], pick[...], (own_held, far_held), (own_half, far_half), out_sems, part
        )
    for copy in outputs:
        copy.wait()


def weight_grad_kernel(sizes, *refs):
    chunks, split, band = sizes
    gradients = refs[0:2]
    fields = refs[2:4]
    count = sum(len(part_sizes(split, lines)) for lines in chunks)
    outs = refs[4 : 4 + count]
    (gradient, field, plain, held, in_sems, grad_sems, sems) = refs[4 + count :]
    inputs = []
    for line in range(8):
        for side in range(2):
            of = pl.ds(line * band, band)
            inputs.append(
                fetch(fields[side].at[of], plain.at[side, of], in_sems.at[2 * line + side])
            )
    arriving = []
    for line in range(8):
        for side in range(2):
            of = pl.ds(line * band, band)
            to = pl.ds((2 * line + side) * band, band)
            arriving.append(
                fetch(gradients[side].at[of], gradient.at[to], grad_sems.at[2 * line + side])
            )

    def prepare(index, carry):
        for side in range(2):
            for part in range(band // CHUNK):
                to = pl.ds(
                    pl.multiple_of((2 * index + side) * band + part * CHUNK, 16), CHUNK
                )
                of = pl.ds(pl.multiple_of(index * band + part * CHUNK, 16), CHUNK)
                value = plain[side, of]
                wide = value.astype(full)
                field[to, 0:C3] = shifted(wide, 1).astype(half)
                field[to, C3 : 2 * C3] = value
                field[to, 2 * C3 : TRIPLE] = shifted(wide, -1).astype(half)
        return carry

    for part in range(QUARTERS):
        for copy in inputs[4 * part : 4 * part + 4]:
            copy.wait()
        lax.fori_loop(2 * part, 2 * part + 2, prepare, 0)
    for copy in arriving:
        copy.wait()
    rows = field.shape[0]
    inner = rows - 2 * band
    spans = {
        0: (slice(2 * band, rows), slice(0, inner)),
        1: (slice(0, rows), slice(0, rows)),
        2: (slice(0, inner), slice(2 * band, rows)),
    }
    tall = held.shape[2]
    copies = []
    start = 0
    number = 0
    for lines in chunks:
        for place, line in enumerate(lines):
            left, right = spans[line]
            part = dot(gradient[left, 0 : C3 // 2], field[right], TN).astype(half)
            for turn in range(split):
                for block in range(15):
                    held[turn, start + place * 15 + block] = part[
                        turn * tall : (turn + 1) * tall, block * 128 : (block + 1) * 128
                    ]
        for turn, first, size in part_sizes(split, lines):
            copies.append(
                fetch(
                    held.at[turn, start + first : start + first + size],
                    outs[number],
                    sems.at[number],
                )
            )
            number += 1
        start += 15 * len(lines)
    for copy in copies:
        copy.wait()


def part_sizes(split, lines):
    blocks = 15 * len(lines)
    sizes = [(turn, 0, blocks) for turn in range(split - 1)]
    return sizes + [(split - 1, 0, blocks // 2), (split - 1, blocks // 2, blocks - blocks // 2)]


def trunk_kernel(sizes, *refs):
    per, row_total, split = sizes
    rows = per * 64
    band = per * 8
    (
        ids,
        incoming,
        grad_summed,
        base,
        stats_one,
        stats_six,
        norm_rows,
        proj_t,
        act_three,
        mid_two,
        mid_one,
        stem_out,
        patches,
        proj_a,
        proj_b,
        grad_head,
        mine,
        other,
        trunk,
        grad_two,
        act_two,
        grad_one,
        act_one,
        grad_stem,
        proj_b_pad,
        split_part,
        shared_part,
        sems,
    ) = refs
    mean, rstd = moments(stats_one, row_total)
    low, high = grad_moments(stats_six, row_total)
    factor = rstd * norm_rows[0:1]
    proj_b_pad[...] = jnp.zeros(proj_b_pad.shape, half)
    proj_b_pad[:, 0:C2] = proj_b[...].astype(half)
    proj_a_half = proj_a[...].astype(half)

    def prepare(index, carry):
        at = pl.ds(pl.multiple_of(index * CHUNK, 16), CHUNK)
        unit = (base[at] - mean) * rstd
        value = grad_summed[at] + factor * (incoming[at] - low - unit * high)
        trunk[at] = value.astype(half)
        return carry

    lax.fori_loop(0, rows // CHUNK, prepare, 0)
    tall_chunk = 2 * band

    def step(index, carry):
        at = pl.ds(pl.multiple_of(index * tall_chunk, 16), tall_chunk)
        three = dot(trunk[at], proj_t[...])
        two = (three * gelu_pair(mid_two[at])[1]).astype(half)
        grad_two[at] = two
        value, slope = gelu_pair(mid_one[at])
        act_two[at] = value.astype(half)
        one = (dot(two, proj_b_pad[...], NT) * slope).astype(half)
        grad_one[at] = one
        value, slope = gelu_pair(stem_out[at])
        act_one[at] = value.astype(half)
        grad_stem[at] = (dot(one, proj_a_half, NT) * slope).astype(half)
        return carry

    lax.fori_loop(0, rows // tall_chunk, step, 0)
    place = hot(iota((16, WIDE), 0) + C2 == iota((16, WIDE), 1))
    split_part[...] = (
        dot(trunk[...], act_three[...], TN) + dot(grad_head[...].astype(half), place)
    ).astype(half)
    shared = dot(act_two[...], grad_two[...], TN)
    shared = shared + dot(dot(grad_one[...], act_one[...], TN).astype(half), place)
    stem = dot(patches[...], grad_stem[...], TN).astype(half)
    tall = split_part.shape[0] // (2 * split)
    spot = iota((C1, 32), 0)
    twice = hot((spot % tall == iota((C1, 32), 1)) & (spot % tall < 27))
    place = hot(iota((16, WIDE), 0) + (C2 + 16) == iota((16, WIDE), 1))
    shared = shared + dot(dot(twice, stem).astype(half), place)
    shared_part[...] = shared.astype(half)
    copies = []
    for turn in range(split):
        for side, target in ((0, mine), (1, other)):
            place = pl.multiple_of((ids[2] ^ side) * tall, 16)
            spot = pl.multiple_of((ids[0] ^ turn) * (2 * tall) + (ids[2] ^ side) * tall, 16)
            for block in range(3):
                lanes = pl.ds(block * 128, 128)
                number = 6 * (2 * turn + side) + block
                copies.append(
                    fetch(
                        split_part.at[pl.ds(spot, tall), lanes],
                        target.at[turn, block],
                        sems.at[number],
                    )
                )
                copies.append(
                    fetch(
                        shared_part.at[pl.ds(place, tall), lanes],
                        target.at[turn, 3 + block],
                        sems.at[number + 3],
                    )
                )
    for copy in copies:
        copy.wait()


def norm_kernel(sizes, *refs):
    devices, chips, split = sizes
    ids, one, two, stats_six, stats_five, stats_four, line, local, loss, norm_out = refs
    digit = ids[3] // (chips // 4) % 4
    inner = (digit == 1) | (digit == 2)

    def walk(block, total):
        first = one[block].astype(full)
        second = two[block].astype(full)
        return total + (first * first + second * second)

    blocks = two.shape[0]
    squares = lax.fori_loop(0, blocks, walk, jnp.zeros(one.shape[1:], full))
    squares = jnp.sum(jnp.sum(squares, axis=0, keepdims=True), axis=1, keepdims=True)
    total = jnp.where(inner, squares / (chips // 2), 0.0)
    value = jnp.zeros(one.shape[1:], full)
    for block in range(6):
        lane = iota(value.shape, 1) + block % 3 * 128
        share = 1.0 / chips
        if block >= 3:
            share = jnp.where(
                lane < C2 + 16, 1.0 / (chips * split), 1.0 / (2 * chips * split)
            )
        part = one[blocks + block].astype(full)
        value = value + part * part * share
    value = jnp.where(inner, 2.0 * value, 0.0)
    total = total + jnp.sum(jnp.sum(value, axis=0, keepdims=True), axis=1, keepdims=True)
    norm_out[...] = jnp.zeros(norm_out.shape, full)
    for place, stats in enumerate((stats_six, stats_five, stats_four)):
        sums = jnp.sum(stats[...], axis=0)
        norm_out[2 * place : 2 * place + 1] = sums[:, C3 : 2 * C3]
        norm_out[2 * place + 1 : 2 * place + 2] = sums[:, 0:C3]
        if place == 2:
            loss[...] = sums[:, 2 * C3 : 2 * C3 + 128]
    value = norm_out[...]
    local[...] = pltpu.roll(value, C3 - ids[0] * (C3 // split), 1)[0:6, 0 : C3 // split]
    value = value * value / devices
    total = total + jnp.sum(jnp.sum(value, axis=0, keepdims=True), axis=1, keepdims=True)
    line[...] = jnp.broadcast_to(total[None], line.shape)


def clip_scale(squares):
    total = jnp.sum(jnp.sum(squares[...], axis=0), axis=1, keepdims=True)
    size = jnp.sqrt(total[:, 0:1] / 128.0)
    return (size, jnp.minimum(1.0, clip_limit / size))


def conv_update_kernel(sizes, *refs):
    pieces_count, places, step_rate, rates = sizes
    ids = refs[0]
    squares, weight, first, second = refs[1:5]
    small_in = refs[5:24]
    pieces = refs[24 : 24 + pieces_count]
    first_new, second_new, weight_new = refs[24 + pieces_count : 27 + pieces_count]
    small_out = refs[27 + pieces_count : 46 + pieces_count]
    held, small_held, sems, small_sems = refs[46 + pieces_count :]
    layer = pl.program_id(0)
    line = pl.program_id(1)

    def copies(wanted):
        made = []
        for number, (owner, start, size, side) in enumerate(places):
            if owner not in wanted:
                continue
            tall = pieces[number].shape[1]
            row = pl.multiple_of((ids[2] ^ side) * tall, 16)
            made.append(
                pltpu.make_async_copy(
                    pieces[number].at[0:size],
                    held.at[owner, start : start + size, pl.ds(row, tall), :],
                    sems.at[number],
                )
            )
        return made

    def small_copies():
        blocks = held.shape[1]
        return [
            pltpu.make_async_copy(
                pieces[side].at[blocks : blocks + 6], small_held.at[side], small_sems.at[side]
            )
            for side in range(2)
        ]

    @pl.when((layer == 0) & (line == 0))
    def _():
        for copy in small_copies() + copies((0, 1)):
            copy.start()

    @pl.when((layer == 0) & (line == 1))
    def _():
        for copy in small_copies():
            copy.wait()
        small_update(rates, ids, squares, small_held, small_in, small_out)

    for owner in range(2):

        @pl.when((layer == owner) & (line == 0))
        def _():
            for copy in copies((owner,)):
                copy.wait()

    size, scale = clip_scale(squares)
    for part in range(9):
        lanes = slice(part * 128, part * 128 + 128)
        block = line * 9 + part
        gradient = held[layer, block].astype(full) * scale
        results = adamw(
            weight[0, :, lanes], gradient, first[0, :, lanes], second[0, :, lanes], step_rate
        )
        first_new[0, :, lanes] = results[0]
        second_new[0, :, lanes] = results[1]
        weight_new[0, :, lanes] = results[2]


def small_update(rates, ids, squares, blocks, refs, outs):
    grad_norm_p = refs[0]
    states = refs[1:19]
    size_out = outs[18]
    size, scale = clip_scale(squares)
    size_out[...] = jnp.broadcast_to(size, size_out.shape)
    first_core = ids[2] == 0
    here = blocks[0].astype(full)
    there = blocks[1].astype(full)
    cores = (jnp.where(first_core, here, there), jnp.where(first_core, there, here))
    split_part, shared = [
        jnp.concatenate(
            [
                jnp.concatenate([core[first], core[first + 1], core[first + 2]], axis=1)
                for core in cores
            ],
            axis=0,
        ).astype(half)
        for first in (0, 3)
    ]
    grad_c = split_part[:, 0:C2].astype(full)
    classes = states[12].shape[0]
    pick = hot(iota((classes, WIDE), 0) + C2 == iota((classes, WIDE), 1))
    grad_head = dot(pick, split_part, NT)
    grad_b = shared[:, 0:C2].astype(full)
    pick = hot(iota((C0, WIDE), 0) + C2 == iota((C0, WIDE), 1))
    grad_a = dot(pick, shared, NT)
    pick = hot(iota((C0, WIDE), 0) + (C2 + 16) == iota((C0, WIDE), 1))
    grad_stem = dot(pick, shared[0:32], NT)[:, 0:27]
    gradients = (grad_stem, grad_a, grad_b, grad_c, grad_head, grad_norm_p[...])
    for index in range(6):
        weight, first, second = states[3 * index : 3 * index + 3]
        results = adamw(
            weight[...], gradients[index] * scale, first[...], second[...], rates[index]
        )
        for item in range(3):
            outs[3 * index + item][...] = results[item]


def xor_pairs(size, turn):
    return [(index, index ^ turn) for index in range(size)]


def shards(
    images,
    labels,
    corners,
    partners,
    stem_w,
    stem_w_m,
    stem_w_v,
    proj_a,
    proj_a_m,
    proj_a_v,
    proj_b,
    proj_b_m,
    proj_b_v,
    proj_c,
    proj_c_m,
    proj_c_v,
    conv_w,
    conv_w_m,
    conv_w_v,
    head_w,
    head_w_m,
    head_w_v,
    norm_p,
    norm_p_m,
    norm_p_v,
):
    split = lax.axis_size("dp")
    groups = lax.axis_size("filt")
    chips = groups // 2
    devices = split * groups
    count = images.shape[0]
    per = count // split
    rows = per * 64
    band = per * 8
    image_total = float(count * groups)
    row_total = image_total * 64.0
    tall = conv_w.shape[1] // 2
    spot_d = lax.axis_index("dp")
    spot_f = lax.axis_index("filt")
    ids = jnp.stack([spot_d, spot_f, spot_f % 2, spot_f // 2]).astype(jnp.int32)

    def over_dp(value, turn):
        return lax.ppermute(value, "dp", xor_pairs(split, turn))

    def over_filt(value, turn):
        return lax.ppermute(value, "filt", xor_pairs(groups, turn))

    def exchange(stats):
        return lax.all_to_all(stats, ("dp", "filt"), 0, 0)

    (own_images,) = call(
        image_kernel,
        [VMEM] * 4,
        [(shape((count, 3 * PLANE), half), VMEM)],
        [pltpu.VMEM((8, count), full)],
        3,
    )(
        images.transpose(1, 0, 2),
        labels.reshape(1, count),
        corners.T,
        partners.reshape(1, count),
    )
    far_images = [own_images] + [over_filt(own_images, 2 * turn) for turn in range(1, chips)]

    def start_gather(own):
        return [own, over_dp(own, 1), over_dp(own, 2)]

    def middle_gather(pieces, after):
        rows = pieces[0].shape[0]
        return cut_rows(pieces[:0:-1], [(0, 48), (48, rows - 48)], after)

    def cross(pieces):
        return [over_filt(piece, 1) for piece in pieces]

    def end_gather(pieces, crossed, far, after):
        far = [over_dp(far[0], 1), over_dp(far[1], 2)]
        far = cut_rows(far, [(0, piece.shape[0]) for piece in far], after)
        return [*pieces, *far, *crossed, *cross(far)]

    own_one, own_pack = cast_half(ids, conv_w, 0, [proj_c.T, head_w.T, norm_p], [own_images])
    (own_two,) = cast_half(ids, conv_w, 1, [], [own_one])
    far_pack = over_dp(own_pack, 3)
    pieces = start_gather(own_one)
    far = middle_gather(pieces, [])
    all_images = stack(
        far_images,
        [(turn, 0, count) for turn in range(chips)],
        (chips, count, 3 * PLANE),
        [own_two],
    )

    line = shape((devices, 1, 2 * C3))
    patches, stem_out, mid_one, mid_two, act_three, facts = call(
        functools.partial(front_kernel, (per, count, groups, devices, split)),
        [SMEM] + [VMEM] * 5,
        [
            (shape((rows, 32), half), VMEM),
            (shape((rows, C0)), VMEM),
            (shape((rows, C1)), VMEM),
            (shape((rows, WIDE)), VMEM),
            (shape((rows, WIDE), half), VMEM),
            (shape((per, 128)), VMEM),
        ],
        [
            pltpu.VMEM((per, 32, 128), full),
            pltpu.VMEM((rows, 32), full),
            pltpu.VMEM((C0, 32), full),
            pltpu.VMEM((C1, WIDE), half),
        ],
        10,
        1,
    )(ids, all_images, over_filt(all_images, 1), stem_w.T, proj_a, proj_b, far[0])
    crossed = cross(pieces)
    base, stats, norm_rows, head_all, proj_t = call(
        base_kernel,
        [SMEM, VMEM] + [ANY] * 7,
        [
            (shape((rows, C3)), ANY),
            (line, VMEM),
            (shape((8, C3)), VMEM),
            (shape((C3, 16), half), VMEM),
            (shape((C3, WIDE), half), VMEM),
        ],
        [
            pltpu.VMEM((C3, WIDE), half),
            pltpu.VMEM((rows, C3), full),
            pltpu.VMEM((8, C3), full),
            pltpu.SemaphoreType.DMA((10,)),
            pltpu.SemaphoreType.DMA((QUARTERS,)),
        ],
        4,
    )(ids, act_three, *pieces, *crossed, far_pack)
    kernels = [end_gather(pieces, crossed, far, [stats])]
    stats_one = exchange(stats)
    pieces = start_gather(hold(own_two, stats_one))

    table = pltpu.VMEM((rows, C3), full)
    conv_outs = [
        (shape((rows, C3)), ANY),
        (shape((rows, C3), half), ANY),
        (shape((rows, C3)), ANY),
        (line, VMEM),
    ]
    conv_scratch = [
        table,
        pltpu.VMEM((C3, 9 * C3), half),
        pltpu.VMEM((rows, TRIPLE), half),
        table,
        table,
        pltpu.SemaphoreType.DMA((10,)),
        pltpu.SemaphoreType.DMA((QUARTERS,)),
        pltpu.SemaphoreType.DMA((QUARTERS + 2,)),
    ]
    conv_one, field_one, slope_one, stats = call(
        functools.partial(conv_kernel, (per, row_total, split), 0),
        [SMEM, ANY, VMEM, VMEM] + [ANY] * 10,
        conv_outs,
        conv_scratch,
        18,
    )(ids, base, stats_one, norm_rows, *kernels[0])
    far = middle_gather(pieces, [stats])
    stats_two = exchange(stats)
    kernels.append(end_gather(pieces, cross(pieces), far, [stats_two]))
    far_field_one = over_filt(field_one, 1)
    summed, field_two, slope_two, stats = call(
        functools.partial(conv_kernel, (per, row_total, split), 1),
        [SMEM, ANY, VMEM, VMEM, ANY] + [ANY] * 10,
        conv_outs,
        conv_scratch,
        18,
    )(ids, conv_one, stats_two, norm_rows, base, *kernels[1])
    stats_three = exchange(stats)
    far_field_two = over_filt(field_two, 1)
    slope_three, spread, stats, grad_head = call(
        functools.partial(head_kernel, (per, row_total, image_total, head_w.shape[1])),
        [ANY] + [VMEM] * 4,
        [
            (shape((rows, C3)), ANY),
            (shape((band, C3)), VMEM),
            (shape((devices, 1, 2 * C3 + 128)), VMEM),
            (shape((C3, 16)), VMEM),
        ],
        [pltpu.VMEM((band, C3), full)] * 3
        + [table, table]
        + [pltpu.SemaphoreType.DMA((QUARTERS,)), pltpu.SemaphoreType.DMA((QUARTERS,))],
        7,
    )(summed, stats_three, norm_rows, head_all, facts)
    stats_four = exchange(stats)

    wide_half = pltpu.VMEM((rows, WIDE), half)
    picks = pltpu.VMEM((C3, 2 * WIDE), half)
    half_outs = [(shape((rows, WIDE), half), ANY)] * 2

    def back(layer, heads, tails, after):
        last = layer == 1
        return call(
            functools.partial(back_kernel, (per, row_total, split), layer),
            ([SMEM, ANY, ANY] + [VMEM] * 4 if last else [SMEM, ANY])
            + [ANY, ANY, VMEM]
            + [ANY] * 10,
            [(shape((rows, C3)), ANY), (line, VMEM)]
            + (half_outs + [(shape((rows, C3)), ANY)] if last else []),
            (
                [table, wide_half, wide_half, picks, pltpu.SemaphoreType.DMA((2 * QUARTERS + 1,))]
                if last
                else [pltpu.VMEM((rows, C3), half)]
            )
            + [
                table,
                table,
                pltpu.VMEM((C3, 9 * C3), half),
                pltpu.VMEM((rows, TRIPLE), half),
                table,
                pltpu.SemaphoreType.DMA((10,)),
                pltpu.SemaphoreType.DMA((2 * QUARTERS,)),
                pltpu.SemaphoreType.DMA((QUARTERS,)),
            ],
            22,
            len(after),
        )(ids, *heads, *tails, *kernels[layer], *after)

    grad_conv_one, stats, own_half, far_half, grad_summed = back(
        1,
        [slope_three, summed, stats_three, stats_four, norm_rows, spread],
        [conv_one, slope_two, stats_two],
        [],
    )
    stats_five = exchange(stats)

    def weight_grad(own_half, far_half, field, far_field, chunks, after):
        sizes = [part_sizes(split, lines) for lines in chunks]
        outs = [
            (shape((size, tall, 128), half), ANY) for parts in sizes for _, _, size in parts
        ]
        flat = call(
            functools.partial(weight_grad_kernel, (chunks, split, band)),
            [ANY] * 4,
            outs,
            [
                pltpu.VMEM((2 * rows, WIDE), half),
                pltpu.VMEM((2 * rows, TRIPLE), half),
                pltpu.VMEM((2, rows, C3), half),
                pltpu.VMEM((split, 45, tall, 128), half),
                pltpu.SemaphoreType.DMA((16,)),
                pltpu.SemaphoreType.DMA((16,)),
                pltpu.SemaphoreType.DMA((len(outs),)),
            ],
            13,
            len(after),
        )(own_half, over_filt(far_half, 1), field, far_field, *after)
        result = []
        for parts in sizes:
            result.append(flat[: len(parts)])
            flat = flat[len(parts) :]
        return result

    def add(values):
        return sum(value.astype(full) for value in values).astype(half)

    def start_dp(parts, after):
        own, near, next_near, far_low, far_high = parts
        blocks = near.shape[0]
        cut = far_low.shape[0]
        from_near = over_dp(far_low, 1)
        from_next = over_dp(far_high, 2)
        near, next_near = merge(
            [near, next_near, from_near, from_next],
            [
                (blocks, [(0, 0, 0, blocks), (3, 0, cut, blocks - cut)]),
                (blocks, [(1, 0, 0, blocks), (2, 0, 0, cut)]),
            ],
            after,
            3,
        )
        return [own, near, next_near]

    def end_dp(parts, sizes, after):
        own, near, next_near = parts
        plan = []
        start = 0
        for size in sizes:
            plan.append((size, [(source, start, 0, size) for source in range(3)]))
            start += size
        return merge([own, over_dp(near, 1), over_dp(next_near, 2)], plan, after, 0.1)

    def gated_add(left, right, after):
        if not after:
            return add([left, right])
        size = left.shape[0]
        return merge([left, right], [(size, [(0, 0, 0, size), (1, 0, 0, size)])], after, 0.1)[0]

    def chip_routes(reach):
        routes = []
        for move in ({0: 1, 3: 2}, {1: 2, 2: 1}, {1: 0, 2: 3}):
            pairs = []
            for index in range(groups):
                here = index // 2 // reach % 4
                if here in move:
                    pairs.append((index, index + (move[here] - here) * 2 * reach))
            routes.append(pairs)
        return routes

    def to_middles(value, reach, after):
        arrived = lax.ppermute(value, "filt", chip_routes(reach)[0])
        return gated_add(value, arrived, after)

    def between_middles(value, reach, after):
        return gated_add(value, lax.ppermute(value, "filt", chip_routes(reach)[1]), after)

    def outward(value, reach):
        return lax.ppermute(value, "filt", chip_routes(reach)[2])

    def from_middles(value, reach, after=(), arrived=None):
        if arrived is None:
            arrived = outward(value, reach)
        (result,) = call(
            functools.partial(pick_kernel, reach),
            [SMEM, ANY, ANY],
            [(shape(value.shape, half), VMEM)],
            [pltpu.SemaphoreType.DMA],
            0.1,
            len(after),
        )(ids, value, arrived, *after)
        return result

    def over_more_chips(value, reach):
        while reach < chips:
            value = from_middles(value, reach // 4)
            value = to_middles(value, reach, [])
            value = between_middles(value, reach, [])
            reach *= 4
        return value

    chunks_two = ((0, 1, 2),)
    chunks_one = ((0, 1, 2),)
    pairs_two = weight_grad(
        own_half, far_half, field_two, far_field_two, chunks_two, []
    )
    grad_one_half, own_half_one, far_half_one = call(
        functools.partial(norm_back_kernel, (row_total, split)),
        [SMEM, ANY, ANY, VMEM, VMEM, VMEM],
        [(shape((rows, C3), half), ANY)] + half_outs,
        [
            table,
            table,
            pltpu.VMEM((rows, C3), half),
            wide_half,
            wide_half,
            picks,
            pltpu.SemaphoreType.DMA((2 * QUARTERS,)),
            pltpu.SemaphoreType.DMA((3 * QUARTERS,)),
        ],
        6,
        1,
    )(ids, grad_conv_one, conv_one, stats_two, stats_five, norm_rows, pairs_two[0][0])
    pairs_one = weight_grad(
        own_half_one, far_half_one, field_one, far_field_one, chunks_one, [pairs_two[0][0]]
    )
    begun_two = start_dp(pairs_two[0], [pairs_one[0][0]])
    grad_base, stats = back(
        0,
        [grad_one_half],
        [base, slope_one, stats_one],
        [pairs_one[0][0], begun_two[1]],
    )
    stats_six = exchange(stats)
    begun_one = start_dp(pairs_one[0], [stats_six])
    blocks = begun_one[0].shape[0]
    (part_two,) = end_dp(begun_two, [blocks], [stats_six])
    small = shape((split, 6, tall, 128), half)
    small_mine, small_other = call(
        functools.partial(trunk_kernel, (per, row_total, split)),
        [SMEM] + [VMEM] * 15,
        [(small, ANY), (small, ANY)],
        [
            pltpu.VMEM((rows, C3), half),
            pltpu.VMEM((rows, WIDE), half),
            pltpu.VMEM((rows, C1), half),
            pltpu.VMEM((rows, C1), half),
            pltpu.VMEM((rows, C0), half),
            pltpu.VMEM((rows, C0), half),
            pltpu.VMEM((C1, WIDE), half),
            pltpu.VMEM((C3, WIDE), half),
            pltpu.VMEM((C1, WIDE), half),
            pltpu.SemaphoreType.DMA((12 * split,)),
        ],
        0.1,
        2,
    )(
        ids,
        grad_base,
        grad_summed,
        base,
        stats_one,
        stats_six,
        norm_rows,
        proj_t,
        act_three,
        mid_two,
        mid_one,
        stem_out,
        patches,
        proj_a,
        proj_b,
        grad_head,
        begun_one[1],
        part_two,
    )
    crossed = over_filt(small_other, 1)
    pair = [add([small_mine[turn], crossed[turn]]) for turn in range(split)]
    small_sum = add([pair[0]] + [over_dp(pair[turn], turn) for turn in range(1, split)])
    (part_one,) = end_dp(begun_one, [blocks], [small_mine])
    half_two = to_middles(part_two, 1, [part_one])
    half_one = to_middles(part_one, 1, [half_two, small_sum])
    whole_two = between_middles(half_two, 1, [half_one])
    whole_two = over_more_chips(whole_two, 4)
    last = chips // 4
    small_sum = between_middles(to_middles(small_sum, 1, []), 1, [])
    small_sum = over_more_chips(small_sum, 4)

    arrived_two = outward(whole_two, last)
    terms = [half_one, lax.ppermute(half_one, "filt", chip_routes(1)[1])]
    if chips > 4:
        terms = [over_more_chips(add(terms), 4)]
    plan = [(place, 0, 0, blocks) for place in range(len(terms))]
    plan.append((len(terms), 0, blocks, 6))
    (whole_one,) = merge([*terms, small_sum], [(blocks + 6, plan)], [arrived_two], 0.1)
    arrived_one = outward(whole_one, last)
    squares, grad_norm_p, loss = call(
        functools.partial(norm_kernel, (devices, chips, split)),
        [SMEM] + [VMEM] * 5,
        [
            (shape((devices, 1, 128)), VMEM),
            (shape((6, C3 // split)), VMEM),
            (shape((1, 128)), VMEM),
        ],
        [pltpu.VMEM((8, C3), full)],
        3,
    )(ids, whole_one, whole_two, stats_six, stats_five, stats_four)
    reduced_two = from_middles(whole_two, last, [squares], arrived_two)
    far_two = over_filt(reduced_two, 1)
    squares = exchange(squares)
    reduced_one = from_middles(whole_one, last, [squares, far_two], arrived_one)

    pieces = []
    places = []
    far_one = over_filt(reduced_one, 1)
    for owner, both in enumerate(((reduced_one, far_one), (reduced_two, far_two))):
        pieces += both
        places += [(owner, 0, blocks, side) for side in range(2)]
    whole_spec = pl.BlockSpec((1, 2 * tall, 1152), lambda layer, line: (layer, 0, line))
    conv_shape = shape(conv_w.shape)
    states = (
        (stem_w.T, stem_w_m.T, stem_w_v.T),
        (proj_a, proj_a_m, proj_a_v),
        (proj_b, proj_b_m, proj_b_v),
        (proj_c.T, proj_c_m.T, proj_c_v.T),
        (head_w.T, head_w_m.T, head_w_v.T),
        (norm_p, norm_p_m, norm_p_v),
    )
    rates = (
        0.7 / math.sqrt(27.0),
        0.7 / math.sqrt(C0),
        0.7 / math.sqrt(C1),
        0.7 / math.sqrt(C2),
        0.7 / math.sqrt(C3 / 8.0),
        0.8,
    )
    flat = [item for group in states for item in group]
    updated = pl.pallas_call(
        functools.partial(
            conv_update_kernel, (len(pieces), places, 0.7 / math.sqrt(9.0 * C3), rates)
        ),
        grid=(2, 5),
        in_specs=[SMEM, VMEM, whole_spec, whole_spec, whole_spec]
        + [VMEM] * 19
        + [ANY] * len(pieces),
        out_specs=[whole_spec] * 3 + [VMEM] * 19,
        out_shape=[conv_shape] * 3 + [shape(item.shape) for item in flat] + [shape((1, 128))],
        scratch_shapes=[
            pltpu.VMEM((2, 45, 2 * tall, 128), half),
            pltpu.VMEM((2, 6, tall, 128), half),
            pltpu.SemaphoreType.DMA((len(pieces),)),
            pltpu.SemaphoreType.DMA((2,)),
        ],
        compiler_params=pltpu.CompilerParams(vmem_limit_bytes=63 * MIB),
        cost_estimate=pl.CostEstimate(
            flops=20 * conv_w.size, bytes_accessed=26 * conv_w.size, transcendentals=0
        ),
    )(
        ids,
        squares,
        conv_w,
        conv_w_m,
        conv_w_v,
        grad_norm_p,
        *flat,
        *pieces,
    )
    conv_new, small_new = updated[0:3], updated[3:]
    size = small_new[18][0, 0]
    turned = [
        item.T if index // 3 in (0, 3, 4) else item for index, item in enumerate(small_new[:18])
    ]
    return (
        *turned[0:12],
        *conv_new,
        *turned[12:18],
        loss[0, 0],
        size,
    )


def solution(mesh):
    placed = (
        P("filt", None, None),
        P("filt"),
        P("filt", None),
        P("filt"),
        *([P()] * 9),
        *([P(None, "dp")] * 3),
        *([P(None, "dp", None)] * 3),
        *([P("dp", None)] * 3),
        *([P(None, "dp")] * 3),
    )
    return jax.shard_map(
        shards,
        mesh=mesh,
        in_specs=placed,
        out_specs=(
            *([P()] * 9),
            *([P(None, "dp")] * 3),
            *([P(None, "dp", None)] * 3),
            *([P("dp", None)] * 3),
            *([P(None, "dp")] * 3),
            P(),
            P(),
        ),
        check_vma=False,
    )
```

```python
import functools
import math

import jax
import jax.numpy as jnp
from jax import lax
from jax.experimental import pallas as pl
from jax.experimental.pallas import tpu as pltpu
from jax.sharding import PartitionSpec as P

C0 = 16
C1 = 160
C2 = 320
C3 = 640
WIDE = 384
TRIPLE = 3 * C3
SIDE = 32
CUT = 16
STEP = 10
PLANE = 640
META = 576
CHUNK = 48
QUARTERS = 4

beta_one = 0.9
beta_two = 0.999
adam_eps = 1e-08
weight_decay = 0.0005
clip_limit = 0.05
norm_eps = 1e-05
gelu_one = math.sqrt(2.0 / math.pi)
gelu_three = 0.044715 * gelu_one

half = jnp.bfloat16
full = jnp.float32
NT = (((1,), (1,)), ((), ()))
NN = (((1,), (0,)), ((), ()))
TN = (((0,), (0,)), ((), ()))
VMEM = pl.BlockSpec(memory_space=pltpu.VMEM)
SMEM = pl.BlockSpec(memory_space=pltpu.SMEM)
ANY = pl.BlockSpec(memory_space=pl.ANY)
MIB = 2**20


def shape(dims, kind=full):
    return jax.ShapeDtypeStruct(dims, kind)


def dot(left, right, dims=NN):
    return lax.dot_general(left, right, dims, preferred_element_type=full)


def iota(dims, axis):
    return lax.broadcasted_iota(jnp.int32, dims, axis)


def hot(condition):
    return condition.astype(full).astype(half)


def call(kernel, ins, outs, scratch, micros, after=0):
    used = len(ins)

    def body(*refs):
        kernel(*refs[:used], *refs[used + after :])

    return pl.pallas_call(
        body,
        out_shape=[item[0] for item in outs],
        in_specs=ins + [ANY] * after,
        out_specs=[item[1] for item in outs],
        scratch_shapes=scratch,
        cost_estimate=pl.CostEstimate(
            flops=int(micros * 35 * 10**7), bytes_accessed=1, transcendentals=0
        ),
        compiler_params=pltpu.CompilerParams(vmem_limit_bytes=63 * MIB),
    )


def gelu_pair(values):
    square = values * values
    bent = jnp.tanh(values * (gelu_one + gelu_three * square))
    gate = 0.5 + 0.5 * bent
    slope = gate + (0.5 * values) * (1.0 - bent * bent) * (gelu_one + (3.0 * gelu_three) * square)
    return (values * gate, slope)


def adamw(weight, gradient, first, second, step_rate):
    first_new = beta_one * first + (1.0 - beta_one) * gradient
    second_new = beta_two * second + (1.0 - beta_two) * (gradient * gradient)
    second_hat = second_new * (1.0 / (1.0 - beta_two**STEP))
    root = second_hat * lax.rsqrt(second_hat) + adam_eps
    weight_new = weight * (1.0 - step_rate * weight_decay) - (
        step_rate / (1.0 - beta_one**STEP)
    ) * (first_new / root)
    return (first_new, second_new, weight_new)


def fetch(source, target, sem):
    copy = pltpu.make_async_copy(source, target, sem)
    copy.start()
    return copy


def lane_pixel(lanes):
    tap = lanes // 64
    cell = lanes % 64
    row = 4 * (cell // 8) + tap // 3 - 1
    col = 4 * (cell % 8) + tap % 3 - 1
    return (tap, row, col)


def image_kernel(planes, labels, corners, partners, out, numbers):
    count = planes.shape[1]
    tap, row, col = lane_pixel(iota((1, PLANE), 1))
    pixel = jnp.where((row >= 0) & (col >= 0) & (tap < 9), row * SIDE + col, -1)
    pick = hot(iota((SIDE * SIDE, PLANE), 0) == pixel)
    numbers[...] = jnp.zeros(numbers.shape, full)
    numbers[0:1] = labels[...].astype(full)
    numbers[1:3] = corners[...].astype(full)
    numbers[3:4] = (partners[...] // count).astype(full)
    numbers[4:5] = (partners[...] % count).astype(full)
    place = hot(iota((8, PLANE), 0) + META == iota((8, PLANE), 1))
    for colour in range(3):
        taken = dot(planes[colour], pick)
        if colour == 0:
            taken = taken + dot(numbers[...].astype(half), place, TN)
        out[:, colour * PLANE : (colour + 1) * PLANE] = taken.astype(half)


def pack_lanes(proj_c, head, norm):
    place = hot(iota((C2, WIDE), 0) == iota((C2, WIDE), 1))
    total = dot(proj_c[...].astype(half), place)
    classes = head.shape[0]
    place = hot(iota((classes, WIDE), 0) + C2 == iota((classes, WIDE), 1))
    total = total + dot(head[...].astype(half), place, TN)
    rest = norm[...]
    for part in range(3):
        piece = rest.astype(half)
        rest = rest - piece.astype(full)
        place = hot(iota((6, WIDE), 0) + (C2 + 16 + 8 * part) == iota((6, WIDE), 1))
        total = total + dot(piece, place, TN)
    return total


def cast_kernel(layer, *refs):
    ids, weights = refs[0:2]
    wide, narrow, in_sems, out_sems = refs[-4:]
    out = refs[5] if layer == 0 else refs[2]
    rows = out.shape[0]
    cols = wide.shape[1]
    parts = rows // 16
    inputs = []
    for part in range(parts):
        spot = pl.multiple_of(ids[2] * rows + part * 16, 16)
        inputs.append(
            fetch(
                weights.at[layer, pl.ds(spot, 16)],
                wide.at[part * 16 : part * 16 + 16],
                in_sems.at[part],
            )
        )
    if layer == 0:
        total = pack_lanes(*refs[2:5])
        mine = jnp.where(ids[2] == 0, total[0:rows], total[rows : 2 * rows])
        narrow[:, cols : cols + WIDE] = mine.astype(half)
        refs[6][...] = total.astype(half)
    outputs = []
    for part in range(parts):
        here = slice(part * 16, part * 16 + 16)
        inputs[part].wait()
        narrow[here, 0:cols] = wide[here].astype(half)
        outputs.append(fetch(narrow.at[here], out.at[here], out_sems.at[part]))
    for copy in outputs:
        copy.wait()


def cast_half(ids, conv_w, layer, packed, after):
    rows = conv_w.shape[1] // 2
    cols = conv_w.shape[2]
    total = cols + WIDE if layer == 0 else cols
    return call(
        functools.partial(cast_kernel, layer),
        [SMEM, ANY] + [VMEM] * len(packed),
        [(shape((rows, total), half), ANY)]
        + ([(shape((2 * rows, WIDE), half), VMEM)] if layer == 0 else []),
        [
            pltpu.VMEM((rows, cols), full),
            pltpu.VMEM((rows, total), half),
            pltpu.SemaphoreType.DMA((rows // 16,)),
            pltpu.SemaphoreType.DMA((rows // 16,)),
        ],
        0.1,
        len(after),
    )(ids, conv_w, *packed, *after)


def hold_kernel(*refs):
    pass


def hold(value, after):
    return pl.pallas_call(
        hold_kernel,
        out_shape=shape(value.shape, value.dtype),
        in_specs=[ANY] * 2,
        out_specs=ANY,
        input_output_aliases={0: 0},
        compiler_params=pltpu.CompilerParams(has_side_effects=True),
        cost_estimate=pl.CostEstimate(flops=1, bytes_accessed=1, transcendentals=0),
    )(value, after)


def merge_spans(plan):
    spans = []
    for out, (size, terms) in enumerate(plan):
        edges = {0, size}
        for _, _, start, length in terms:
            edges |= {start, start + length}
        edges = sorted(edges)
        for low, high in zip(edges[:-1], edges[1:]):
            used = [
                (source, first - start)
                for source, first, start, length in terms
                if start <= low and high <= start + length
            ]
            for begin in range(low, high, 8):
                spans.append((out, begin, min(8, high - begin), used))
    return spans


def merge_kernel(plan, count, *refs):
    values = refs[:count]
    results = refs[count : count + len(plan)]
    held = refs[count + len(plan) : 2 * count + len(plan)]
    kept = refs[2 * count + len(plan) : 2 * (count + len(plan))]
    in_sems, out_sems = refs[2 * (count + len(plan)) :]
    arrivals = []
    number = 0
    for _, begin, size, used in merge_spans(plan):
        copies = []
        for source, shift in used:
            here = slice(begin + shift, begin + shift + size)
            copies.append(
                fetch(values[source].at[here], held[source].at[here], in_sems.at[number])
            )
            number += 1
        arrivals.append(copies)
    departures = []
    for (out, begin, size, used), copies in zip(merge_spans(plan), arrivals):
        for copy in copies:
            copy.wait()
        total = None
        for source, shift in used:
            value = held[source][begin + shift : begin + shift + size].astype(full)
            total = value if total is None else total + value
        here = slice(begin, begin + size)
        kept[out][here] = total.astype(half)
        departures.append(
            fetch(kept[out].at[here], results[out].at[here], out_sems.at[len(departures)])
        )
    for copy in departures:
        copy.wait()


def merge(values, plan, after, micros):
    dims = values[0].shape[1:]
    spans = merge_spans(plan)
    return call(
        functools.partial(merge_kernel, plan, len(values)),
        [ANY] * len(values),
        [(shape((size,) + dims, half), ANY) for size, _ in plan],
        [pltpu.VMEM(value.shape, half) for value in values]
        + [pltpu.VMEM((size,) + dims, half) for size, _ in plan]
        + [
            pltpu.SemaphoreType.DMA((sum(len(used) for _, _, _, used in spans),)),
            pltpu.SemaphoreType.DMA((len(spans),)),
        ],
        micros,
        len(after),
    )(*values, *after)


def pick_kernel(reach, ids, value, arrived, out, sem):
    digit = ids[3] // reach % 4
    outer = (digit == 0) | (digit == 3)

    @pl.when(outer)
    def _():
        fetch(arrived, out, sem).wait()

    @pl.when(jnp.logical_not(outer))
    def _():
        fetch(value, out, sem).wait()


def cut_kernel(places, *refs):
    count = len(places)
    outs = refs[count : 2 * count]
    sems = refs[2 * count]
    copies = []
    for index, (start, size) in enumerate(places):
        copies.append(
            fetch(
                refs[index].at[start : start + size, 0 : 9 * C3], outs[index], sems.at[index]
            )
        )
    for copy in copies:
        copy.wait()


def cut_rows(values, places, after):
    cols = 9 * C3
    return call(
        functools.partial(cut_kernel, places),
        [ANY] * len(values),
        [(shape((size, cols), half), VMEM) for _, size in places],
        [pltpu.SemaphoreType.DMA((len(values),))],
        1,
        len(after),
    )(*values, *after)


def stack_kernel(places, *refs):
    count = len(places)
    out, sems = refs[count:]
    copies = []
    for index, (slot, start, size) in enumerate(places):
        copy = pltpu.make_async_copy(
            refs[index], out.at[slot, start : start + size], sems.at[index]
        )
        copy.start()
        copies.append(copy)
    for copy in copies:
        copy.wait()


def stack(pieces, places, dims, after):
    (result,) = call(
        functools.partial(stack_kernel, places),
        [ANY] * len(pieces),
        [(shape(dims, half), VMEM)],
        [pltpu.SemaphoreType.DMA((len(pieces),))],
        3,
        len(after),
    )(*pieces, *after)
    return result


def front_kernel(sizes, *refs):
    per, count, groups, devices, split = sizes
    rows = per * 64
    band = per * 8
    ids = refs[0]
    images, far_images, stem_w, proj_a, proj_b = refs[1:6]
    (
        patches,
        stem_out,
        mid_one,
        mid_two,
        act_three,
        facts,
        tiles,
        loose,
        stem_pad,
        proj_b_pad,
    ) = refs[6:]
    slot = iota((per, count), 0)
    column = iota((per, count), 1)
    own = dot(hot(column == slot + ids[0] * per), images[0])
    group_of = own[:, META + 3 : META + 4].astype(jnp.int32)
    local_of = own[:, META + 4 : META + 5].astype(jnp.int32)
    turn_of = group_of ^ ids[1]
    other = jnp.zeros((per, 3 * PLANE), full)
    for turn in range(groups):
        source = far_images[turn // 2] if turn % 2 else images[turn // 2]
        other = other + dot(hot((turn_of == turn) & (column == local_of)), source)
    top = own[:, META + 1 : META + 2]
    left = own[:, META + 2 : META + 3]
    tap, row, col = lane_pixel(iota((1, 3 * PLANE), 1) % PLANE)
    row = row.astype(full)
    col = col.astype(full)
    inside = (row >= top) & (row < top + CUT) & (col >= left) & (col < left + CUT) & (tap < 9)
    blended = jnp.where(inside, other, own)
    tall = jnp.maximum(jnp.minimum(top + CUT, float(SIDE)) - jnp.maximum(top, 0.0), 0.0)
    broad = jnp.maximum(jnp.minimum(left + CUT, float(SIDE)) - jnp.maximum(left, 0.0), 0.0)
    share = 1.0 - tall * broad / float(SIDE * SIDE)
    lanes = iota((per, 128), 1)
    facts[...] = jnp.where(
        lanes == 0,
        own[:, META : META + 1],
        jnp.where(lanes == 1, other[:, META : META + 1], share),
    )
    tiles[...] = jnp.zeros(tiles.shape, full)
    for piece in range(15):
        tiles[:, piece, :] = blended[:, piece * 128 : (piece + 1) * 128]
    tiles[:, 16:32, :] = pltpu.roll(tiles[:, 0:16, :], 64, 2)
    spot = iota((32, 32), 0)
    tap_at = ((spot % 16) % 5) * 2 + spot // 16
    colour_at = (spot % 16) // 5
    order = hot(
        (iota((32, 32), 1) == tap_at * 3 + colour_at) & (tap_at < 9) & (spot % 16 < 15)
    )
    for image in range(per):
        cells = dot(tiles[image].astype(half), order, TN)
        for line in range(8):
            loose[line * band + image * 8 : line * band + image * 8 + 8, :] = cells[
                line * 8 : line * 8 + 8
            ]
    patches[...] = loose[...].astype(half)
    stem_pad[...] = jnp.zeros(stem_pad.shape, full)
    stem_pad[:, 0:27] = stem_w[...]
    proj_b_pad[...] = jnp.zeros(proj_b_pad.shape, half)
    proj_b_pad[:, 0:C2] = proj_b[...].astype(half)
    stem_half = stem_pad[...].astype(half)
    proj_a_half = proj_a[...].astype(half)
    tall_chunk = 2 * band

    def step(index, carry):
        at = pl.ds(pl.multiple_of(index * tall_chunk, 16), tall_chunk)
        stem = dot(patches[at], stem_half, NT)
        stem_out[at] = stem
        one = dot(gelu_pair(stem)[0].astype(half), proj_a_half)
        mid_one[at] = one
        two = dot(gelu_pair(one)[0].astype(half), proj_b_pad[...])
        mid_two[at] = two
        act_three[at] = gelu_pair(two)[0].astype(half)
        return carry

    lax.fori_loop(0, rows // tall_chunk, step, 0)


def base_kernel(*refs):
    ids, act_three = refs[0:2]
    pieces = refs[2:8]
    far_pack = refs[8]
    base, stats, norm_rows, head_all, proj_t, gathered, held, totals, sems, out_sems = refs[9:]
    rows = act_three.shape[0]
    tall = pieces[0].shape[0]
    spot = pl.multiple_of((ids[0] ^ 3) * (2 * tall), 16)
    copies = [fetch(far_pack, gathered.at[pl.ds(spot, 2 * tall)], sems.at[6])]
    for side in range(2):
        for turn in range(3):
            piece = pieces[3 * side + turn]
            lanes = pl.ds(piece.shape[1] - WIDE, WIDE)
            spot = (ids[0] ^ turn) * (2 * tall) + (ids[2] ^ side) * tall
            copies.append(
                fetch(
                    piece.at[:, lanes],
                    gathered.at[pl.ds(pl.multiple_of(spot, 16), tall)],
                    sems.at[3 * side + turn],
                )
            )
    for copy in copies:
        copy.wait()
    column = iota((1, WIDE), 1)
    packed = gathered[...]
    proj_t[...] = jnp.where(column < C2, packed.astype(full), 0.0).astype(half)
    place = hot(iota((WIDE, 16), 0) == iota((WIDE, 16), 1) + C2)
    head_all[...] = dot(packed, place).astype(half)
    column = iota((8, WIDE), 1)
    name = iota((8, WIDE), 0)
    pieces = [
        dot(hot((column == name + (C2 + 16 + 8 * part)) & (name < 6)), packed, NT)
        for part in range(3)
    ]
    norm_rows[...] = pieces[0] + (pieces[1] + pieces[2])
    totals[...] = jnp.zeros(totals.shape, full)
    outputs = []
    for part in range(QUARTERS):
        at = quarter_rows(rows, part)
        result = dot(act_three[at], proj_t[...], NT)
        held[at] = result
        outputs.append(fetch(held.at[at], base.at[at], out_sems.at[part]))
        totals[0:1] += jnp.sum(result, axis=0, keepdims=True)
        totals[1:2] += jnp.sum(result * result, axis=0, keepdims=True)
    spread_stats(stats, [totals[0:1], totals[1:2]])
    for copy in outputs:
        copy.wait()


def spread_stats(out, parts):
    line = jnp.concatenate(parts, axis=1)
    out[...] = jnp.broadcast_to(line[None], out.shape)


def moments(stats, row_total):
    line = jnp.sum(stats[...], axis=0)
    mean = line[:, 0:C3] / row_total
    rstd = lax.rsqrt(line[:, C3 : 2 * C3] / row_total - mean * mean + norm_eps)
    return (mean, rstd)


def quarter_rows(rows, part):
    step = rows // QUARTERS
    return pl.ds(part * step, step)


def fetch_quarter(source, target, sem, part):
    here = quarter_rows(source.shape[0], part)
    return fetch(source.at[here], target.at[here], sem)


def walk_quarter(rows, part, body, carry):
    step = rows // QUARTERS // CHUNK
    return lax.fori_loop(part * step, (part + 1) * step, body, carry)


def start_weights(ids, pieces, weights, sems):
    rows = pieces[0].shape[0]
    low = pieces[3].shape[0]
    copies = []
    for side in range(2):
        for place in range(5):
            piece = pieces[5 * side + place]
            turn = min(place, 3)
            spot = (ids[0] ^ turn) * (2 * rows) + (ids[2] ^ side) * rows
            if place == 4:
                spot = spot + low
            spot = pl.multiple_of(spot, 16)
            copies.append(
                fetch(
                    piece.at[:, 0 : 9 * C3],
                    weights.at[pl.ds(spot, piece.shape[0])],
                    sems.at[5 * side + place],
                )
            )
    return copies


def shifted(values, by):
    block = values.reshape(CHUNK // 8, 8, C3)
    place = iota((1, 8, 1), 1)
    if by == 1:
        moved = jnp.where(place == 0, 0.0, pltpu.roll(block, 1, 1))
    else:
        moved = jnp.where(place == 7, 0.0, pltpu.roll(block, 7, 1))
    return moved.reshape(CHUNK, C3)


def conv_kernel(sizes, layer, *refs):
    per, row_total, split = sizes
    rows = per * 64
    band = per * 8
    ids, source, stats_in, norm_rows = refs[0:4]
    offset = 4
    if layer == 1:
        base = refs[4]
        offset = 5
    pieces = refs[offset : offset + 10]
    offset += 10
    (result, field_out, slope_out, stats, held, weights, field, slope, total) = refs[
        offset : offset + 9
    ]
    weight_sems, in_sems, out_sems = refs[offset + 9 : offset + 12]
    inputs = [fetch_quarter(source, held, in_sems.at[part], part) for part in range(QUARTERS)]
    copies = start_weights(ids, pieces, weights, weight_sems)
    mean, rstd = moments(stats_in, row_total)
    factor = rstd * norm_rows[2 * layer : 2 * layer + 1]
    shift = norm_rows[2 * layer + 1 : 2 * layer + 2] - mean * factor

    def prepare(index, carry):
        at = pl.ds(pl.multiple_of(index * CHUNK, 16), CHUNK)
        value, gradient = gelu_pair(held[at] * factor + shift)
        slope[at] = gradient
        field[at, 0:C3] = shifted(value, 1).astype(half)
        field[at, C3 : 2 * C3] = value.astype(half)
        field[at, 2 * C3 : TRIPLE] = shifted(value, -1).astype(half)
        return carry

    for part in range(QUARTERS):
        inputs[part].wait()
        walk_quarter(rows, part, prepare, 0)
    outputs = [
        fetch(field.at[:, C3 : 2 * C3], field_out, out_sems.at[QUARTERS]),
        fetch(slope, slope_out, out_sems.at[QUARTERS + 1]),
    ]
    if layer == 1:
        inputs = [fetch_quarter(base, held, in_sems.at[part], part) for part in range(QUARTERS)]
    for copy in copies:
        copy.wait()
    inner = rows - band
    total[...] = dot(field[...], weights[:, TRIPLE : 2 * TRIPLE], NT)
    total[band:rows] += dot(field[0:inner], weights[:, 0:TRIPLE], NT)
    total[0:inner] += dot(field[band:rows], weights[:, 2 * TRIPLE : 3 * TRIPLE], NT)

    def count(index, carry):
        at = pl.ds(pl.multiple_of(index * CHUNK, 16), CHUNK)
        value = total[at]
        if layer == 1:
            value = value + held[at]
            total[at] = value
        return (
            carry[0] + jnp.sum(value.reshape(CHUNK // 8, 8, C3), axis=0),
            carry[1] + jnp.sum((value * value).reshape(CHUNK // 8, 8, C3), axis=0),
        )

    zero = jnp.zeros((8, C3), full)
    sums = (zero, zero)
    for part in range(QUARTERS):
        if layer == 1:
            inputs[part].wait()
        else:
            outputs.append(fetch_quarter(total, result, out_sems.at[part], part))
        sums = walk_quarter(rows, part, count, sums)
        if layer == 1:
            outputs.append(fetch_quarter(total, result, out_sems.at[part], part))
    spread_stats(stats, [jnp.sum(item, axis=0, keepdims=True) for item in sums])
    for copy in outputs:
        copy.wait()


def head_kernel(sizes, *refs):
    per, row_total, image_total, classes = sizes
    rows = per * 64
    band = per * 8
    (
        source,
        stats_in,
        norm_rows,
        head_all,
        facts,
        slope_out,
        spread,
        stats,
        grad_head,
        sum_value,
        sum_slope,
        sum_cross,
        summed,
        slope,
        in_sems,
        out_sems,
    ) = refs
    inputs = [fetch_quarter(source, summed, in_sems.at[part], part) for part in range(QUARTERS)]
    mean, rstd = moments(stats_in, row_total)
    gain = norm_rows[4:5]
    bias = norm_rows[5:6]
    sum_value[...] = jnp.zeros((band, C3), full)
    sum_slope[...] = jnp.zeros((band, C3), full)
    sum_cross[...] = jnp.zeros((band, C3), full)

    def walk(index, carry):
        for part in range(band // CHUNK):
            at = pl.ds(pl.multiple_of(index * band + part * CHUNK, 16), CHUNK)
            here = slice(part * CHUNK, part * CHUNK + CHUNK)
            unit = (summed[at] - mean) * rstd
            value, gradient = gelu_pair(unit * gain + bias)
            slope[at] = gradient
            sum_value[here] += value
            sum_slope[here] += gradient
            sum_cross[here] += gradient * unit
        return carry

    outputs = []
    for part in range(QUARTERS):
        inputs[part].wait()
        lax.fori_loop(2 * part, 2 * part + 2, walk, 0)
        outputs.append(fetch_quarter(slope, slope_out, out_sems.at[part], part))

    def by_image(ref):
        return jnp.sum(ref[...].reshape(per, 8, C3), axis=1)

    pooled = (by_image(sum_value) / 64.0).astype(half)
    logits = dot(pooled, head_all[...])
    lanes = iota((per, 16), 1)
    inside = lanes < classes
    own = facts[:, 0:1].astype(jnp.int32)
    other = facts[:, 1:2].astype(jnp.int32)
    share = facts[:, 2:3]
    target = jnp.where(lanes == own, share, 0.0) + jnp.where(lanes == other, 1.0 - share, 0.0)
    top = jnp.max(jnp.where(inside, logits, -3e38), axis=1, keepdims=True)
    powers = jnp.where(inside, jnp.exp(jnp.where(inside, logits - top, 0.0)), 0.0)
    lse = top + jnp.log(jnp.sum(powers, axis=1, keepdims=True))
    losses = lse - jnp.sum(target * logits, axis=1, keepdims=True)
    loss = jnp.sum(losses, axis=0, keepdims=True)
    soft = jnp.where(inside, jnp.exp(jnp.where(inside, logits - lse, 0.0)), 0.0)
    grad_logits = ((soft - target) / image_total).astype(half)
    grad_head[...] = dot(pooled, grad_logits, TN)
    pull = dot(grad_logits, head_all[...], NT) / 64.0
    spread[...] = jnp.broadcast_to(pull[:, None, :], (per, 8, C3)).reshape(band, C3)
    bias_sum = jnp.sum(pull * by_image(sum_slope), axis=0, keepdims=True)
    gain_sum = jnp.sum(pull * by_image(sum_cross), axis=0, keepdims=True)
    spread_stats(stats, [bias_sum, gain_sum, jnp.broadcast_to(loss, (1, 128))])
    for copy in outputs:
        copy.wait()


def grad_moments(stats, row_total):
    line = jnp.sum(stats[...], axis=0)
    return (line[:, 0:C3] / row_total, line[:, C3 : 2 * C3] / row_total)


def input_grad(gradient, weights, out, band):
    rows = gradient.shape[0]
    inner = rows - band
    spans = (
        (1, slice(0, rows), slice(0, rows)),
        (0, slice(0, inner), slice(band, rows)),
        (2, slice(band, rows), slice(0, inner)),
    )
    for line, to, of in spans:
        for col in range(3):
            tap = 3 * line + col
            part = dot(
                gradient[of, col * C3 : (col + 1) * C3], weights[:, tap * C3 : (tap + 1) * C3]
            )
            if line == 1 and col == 0:
                out[to] = part
            else:
                out[to] += part


def half_filters(ids, split):
    tall = C3 // (2 * split)
    place = iota((1, 2 * WIDE), 1)
    side = jnp.where(place < WIDE, 0, 1)
    place = place - side * WIDE
    target = (ids[0] ^ (place // tall)) * (2 * tall) + (ids[2] ^ side) * tall + place % tall
    target = jnp.where(place < C3 // 2, target, -1)
    return hot(iota((C3, 2 * WIDE), 0) == target)


def norm_back(arriving, unit, factor, low, high):
    return factor * (arriving - low - unit * high)


def send_halves(middle, pick, helds, halves, sems, part):
    here = quarter_rows(helds[0].shape[0], part)
    both = dot(middle, pick).astype(half)
    copies = []
    for side in range(2):
        helds[side][here] = both[:, side * WIDE : (side + 1) * WIDE]
        copies.append(
            fetch(helds[side].at[here], halves[side].at[here], sems.at[2 * part + side])
        )
    return copies


def back_kernel(sizes, layer, *refs):
    per, row_total, split = sizes
    rows = per * 64
    band = per * 8
    last = layer == 1
    ids = refs[0]
    if last:
        incoming, source, stats_here, stats_grad, norm_rows, spread = refs[1:7]
        offset = 7
    else:
        incoming = refs[1]
        offset = 2
    before, slope_before, stats_before = refs[offset : offset + 3]
    pieces = refs[offset + 3 : offset + 13]
    result, stats = refs[offset + 13 : offset + 15]
    offset += 15
    if last:
        own_half, far_half, grad_out, kept, own_held, far_held, pick, half_sems = refs[
            offset : offset + 8
        ]
        offset += 8
    else:
        arrived = refs[offset]
        offset += 1
    held, origin, weights, gradient, total = refs[offset : offset + 5]
    weight_sems, in_sems, out_sems = refs[offset + 5 : offset + 8]
    inputs = []
    for part in range(QUARTERS):
        if last:
            inputs.append(
                (
                    fetch_quarter(incoming, held, in_sems.at[2 * part], part),
                    fetch_quarter(source, origin, in_sems.at[2 * part + 1], part),
                )
            )
        else:
            inputs.append((fetch_quarter(incoming, arrived, in_sems.at[2 * part], part),))
    copies = start_weights(ids, pieces, weights, weight_sems)
    if last:
        mean, rstd = moments(stats_here, row_total)
        low, high = grad_moments(stats_grad, row_total)
        factor = rstd * norm_rows[4:5]
        parts = band // CHUNK
        pick[...] = half_filters(ids, split)

    def prepare(index, carry):
        at = pl.ds(pl.multiple_of(index * CHUNK, 16), CHUNK)
        if last:
            here = pl.ds(pl.multiple_of(lax.rem(index, parts) * CHUNK, 16), CHUNK)
            unit = (origin[at] - mean) * rstd
            value = norm_back(held[at] * spread[here], unit, factor, low, high)
            kept[at] = value
            gradient[at, C3 : 2 * C3] = value.astype(half)
        else:
            gradient[at, C3 : 2 * C3] = arrived[at]
            value = arrived[at].astype(full)
        gradient[at, 0:C3] = shifted(value, -1).astype(half)
        gradient[at, 2 * C3 : TRIPLE] = shifted(value, 1).astype(half)
        return carry

    for part in range(QUARTERS):
        for copy in inputs[part]:
            copy.wait()
        walk_quarter(rows, part, prepare, 0)
    outputs = []
    if last:
        outputs.append(fetch(kept, grad_out, half_sems.at[2 * QUARTERS]))
        for part in range(QUARTERS):
            outputs += send_halves(
                gradient[quarter_rows(rows, part), C3 : 2 * C3],
                pick[...],
                (own_held, far_held),
                (own_half, far_half),
                half_sems,
                part,
            )
    inputs = []
    for part in range(QUARTERS):
        inputs.append(
            (
                fetch_quarter(before, origin, in_sems.at[2 * part], part),
                fetch_quarter(slope_before, held, in_sems.at[2 * part + 1], part),
            )
        )
    for copy in copies:
        copy.wait()
    input_grad(gradient, weights, total, band)
    mean, rstd = moments(stats_before, row_total)

    def finish(index, carry):
        at = pl.ds(pl.multiple_of(index * CHUNK, 16), CHUNK)
        value = total[at] * held[at]
        total[at] = value
        unit = (origin[at] - mean) * rstd
        return (
            carry[0] + jnp.sum(value.reshape(CHUNK // 8, 8, C3), axis=0),
            carry[1] + jnp.sum((value * unit).reshape(CHUNK // 8, 8, C3), axis=0),
        )

    zero = jnp.zeros((8, C3), full)
    sums = (zero, zero)
    for part in range(QUARTERS):
        for copy in inputs[part]:
            copy.wait()
        sums = walk_quarter(rows, part, finish, sums)
        outputs.append(fetch_quarter(total, result, out_sems.at[part], part))
    spread_stats(stats, [jnp.sum(item, axis=0, keepdims=True) for item in sums])
    for copy in outputs:
        copy.wait()


def norm_back_kernel(sizes, *refs):
    row_total, split = sizes
    ids, incoming, source, stats_here, stats_grad, norm_rows = refs[0:6]
    grad_half, own_half, far_half = refs[6:9]
    held, origin, middle, own_held, far_held, pick, in_sems, out_sems = refs[9:]
    rows = held.shape[0]
    inputs = []
    for part in range(QUARTERS):
        inputs.append(
            (
                fetch_quarter(incoming, held, in_sems.at[2 * part], part),
                fetch_quarter(source, origin, in_sems.at[2 * part + 1], part),
            )
        )
    mean, rstd = moments(stats_here, row_total)
    low, high = grad_moments(stats_grad, row_total)
    factor = rstd * norm_rows[2:3]
    pick[...] = half_filters(ids, split)

    def prepare(index, carry):
        at = pl.ds(pl.multiple_of(index * CHUNK, 16), CHUNK)
        unit = (origin[at] - mean) * rstd
        middle[at] = norm_back(held[at], unit, factor, low, high).astype(half)
        return carry

    outputs = []
    for part in range(QUARTERS):
        for copy in inputs[part]:
            copy.wait()
        walk_quarter(rows, part, prepare, 0)
        here = quarter_rows(rows, part)
        outputs.append(fetch(middle.at[here], grad_half.at[here], out_sems.at[8 + part]))
        outputs += send_halves(
            middle[here], pick[...], (own_held, far_held), (own_half, far_half), out_sems, part
        )
    for copy in outputs:
        copy.wait()


def weight_grad_kernel(sizes, *refs):
    chunks, split, band = sizes
    gradients = refs[0:2]
    fields = refs[2:4]
    count = sum(len(part_sizes(split, lines)) for lines in chunks)
    outs = refs[4 : 4 + count]
    (gradient, field, plain, held, in_sems, grad_sems, sems) = refs[4 + count :]
    inputs = []
    for line in range(8):
        for side in range(2):
            of = pl.ds(line * band, band)
            inputs.append(
                fetch(fields[side].at[of], plain.at[side, of], in_sems.at[2 * line + side])
            )
    arriving = []
    for line in range(8):
        for side in range(2):
            of = pl.ds(line * band, band)
            to = pl.ds((2 * line + side) * band, band)
            arriving.append(
                fetch(gradients[side].at[of], gradient.at[to], grad_sems.at[2 * line + side])
            )

    def prepare(index, carry):
        for side in range(2):
            for part in range(band // CHUNK):
                to = pl.ds(
                    pl.multiple_of((2 * index + side) * band + part * CHUNK, 16), CHUNK
                )
                of = pl.ds(pl.multiple_of(index * band + part * CHUNK, 16), CHUNK)
                value = plain[side, of]
                wide = value.astype(full)
                field[to, 0:C3] = shifted(wide, 1).astype(half)
                field[to, C3 : 2 * C3] = value
                field[to, 2 * C3 : TRIPLE] = shifted(wide, -1).astype(half)
        return carry

    for part in range(QUARTERS):
        for copy in inputs[4 * part : 4 * part + 4]:
            copy.wait()
        lax.fori_loop(2 * part, 2 * part + 2, prepare, 0)
    for copy in arriving:
        copy.wait()
    rows = field.shape[0]
    inner = rows - 2 * band
    spans = {
        0: (slice(2 * band, rows), slice(0, inner)),
        1: (slice(0, rows), slice(0, rows)),
        2: (slice(0, inner), slice(2 * band, rows)),
    }
    tall = held.shape[2]
    copies = []
    start = 0
    number = 0
    for lines in chunks:
        for place, line in enumerate(lines):
            left, right = spans[line]
            part = dot(gradient[left, 0 : C3 // 2], field[right], TN).astype(half)
            for turn in range(split):
                for block in range(15):
                    held[turn, start + place * 15 + block] = part[
                        turn * tall : (turn + 1) * tall, block * 128 : (block + 1) * 128
                    ]
        for turn, first, size in part_sizes(split, lines):
            copies.append(
                fetch(
                    held.at[turn, start + first : start + first + size],
                    outs[number],
                    sems.at[number],
                )
            )
            number += 1
        start += 15 * len(lines)
    for copy in copies:
        copy.wait()


def part_sizes(split, lines):
    blocks = 15 * len(lines)
    sizes = [(turn, 0, blocks) for turn in range(split - 1)]
    return sizes + [(split - 1, 0, blocks // 2), (split - 1, blocks // 2, blocks - blocks // 2)]


def trunk_kernel(sizes, *refs):
    per, row_total, split = sizes
    rows = per * 64
    band = per * 8
    (
        ids,
        incoming,
        grad_summed,
        base,
        stats_one,
        stats_six,
        norm_rows,
        proj_t,
        act_three,
        mid_two,
        mid_one,
        stem_out,
        patches,
        proj_a,
        proj_b,
        grad_head,
        mine,
        other,
        trunk,
        grad_two,
        act_two,
        grad_one,
        act_one,
        grad_stem,
        proj_b_pad,
        split_part,
        shared_part,
        sems,
    ) = refs
    mean, rstd = moments(stats_one, row_total)
    low, high = grad_moments(stats_six, row_total)
    factor = rstd * norm_rows[0:1]
    proj_b_pad[...] = jnp.zeros(proj_b_pad.shape, half)
    proj_b_pad[:, 0:C2] = proj_b[...].astype(half)
    proj_a_half = proj_a[...].astype(half)

    def prepare(index, carry):
        at = pl.ds(pl.multiple_of(index * CHUNK, 16), CHUNK)
        unit = (base[at] - mean) * rstd
        value = grad_summed[at] + factor * (incoming[at] - low - unit * high)
        trunk[at] = value.astype(half)
        return carry

    lax.fori_loop(0, rows // CHUNK, prepare, 0)
    tall_chunk = 2 * band

    def step(index, carry):
        at = pl.ds(pl.multiple_of(index * tall_chunk, 16), tall_chunk)
        three = dot(trunk[at], proj_t[...])
        two = (three * gelu_pair(mid_two[at])[1]).astype(half)
        grad_two[at] = two
        value, slope = gelu_pair(mid_one[at])
        act_two[at] = value.astype(half)
        one = (dot(two, proj_b_pad[...], NT) * slope).astype(half)
        grad_one[at] = one
        value, slope = gelu_pair(stem_out[at])
        act_one[at] = value.astype(half)
        grad_stem[at] = (dot(one, proj_a_half, NT) * slope).astype(half)
        return carry

    lax.fori_loop(0, rows // tall_chunk, step, 0)
    place = hot(iota((16, WIDE), 0) + C2 == iota((16, WIDE), 1))
    split_part[...] = (
        dot(trunk[...], act_three[...], TN) + dot(grad_head[...].astype(half), place)
    ).astype(half)
    shared = dot(act_two[...], grad_two[...], TN)
    shared = shared + dot(dot(grad_one[...], act_one[...], TN).astype(half), place)
    stem = dot(patches[...], grad_stem[...], TN).astype(half)
    tall = split_part.shape[0] // (2 * split)
    spot = iota((C1, 32), 0)
    twice = hot((spot % tall == iota((C1, 32), 1)) & (spot % tall < 27))
    place = hot(iota((16, WIDE), 0) + (C2 + 16) == iota((16, WIDE), 1))
    shared = shared + dot(dot(twice, stem).astype(half), place)
    shared_part[...] = shared.astype(half)
    copies = []
    for turn in range(split):
        for side, target in ((0, mine), (1, other)):
            place = pl.multiple_of((ids[2] ^ side) * tall, 16)
            spot = pl.multiple_of((ids[0] ^ turn) * (2 * tall) + (ids[2] ^ side) * tall, 16)
            for block in range(3):
                lanes = pl.ds(block * 128, 128)
                number = 6 * (2 * turn + side) + block
                copies.append(
                    fetch(
                        split_part.at[pl.ds(spot, tall), lanes],
                        target.at[turn, block],
                        sems.at[number],
                    )
                )
                copies.append(
                    fetch(
                        shared_part.at[pl.ds(place, tall), lanes],
                        target.at[turn, 3 + block],
                        sems.at[number + 3],
                    )
                )
    for copy in copies:
        copy.wait()


def norm_kernel(sizes, *refs):
    devices, chips, split = sizes
    ids, one, two, stats_six, stats_five, stats_four, line, local, loss, norm_out = refs
    digit = ids[3] // (chips // 4) % 4
    inner = (digit == 1) | (digit == 2)

    def walk(block, total):
        first = one[block].astype(full)
        second = two[block].astype(full)
        return total + (first * first + second * second)

    blocks = two.shape[0]
    squares = lax.fori_loop(0, blocks, walk, jnp.zeros(one.shape[1:], full))
    squares = jnp.sum(jnp.sum(squares, axis=0, keepdims=True), axis=1, keepdims=True)
    total = jnp.where(inner, squares / (chips // 2), 0.0)
    value = jnp.zeros(one.shape[1:], full)
    for block in range(6):
        lane = iota(value.shape, 1) + block % 3 * 128
        share = 1.0 / chips
        if block >= 3:
            share = jnp.where(
                lane < C2 + 16, 1.0 / (chips * split), 1.0 / (2 * chips * split)
            )
        part = one[blocks + block].astype(full)
        value = value + part * part * share
    value = jnp.where(inner, 2.0 * value, 0.0)
    total = total + jnp.sum(jnp.sum(value, axis=0, keepdims=True), axis=1, keepdims=True)
    norm_out[...] = jnp.zeros(norm_out.shape, full)
    for place, stats in enumerate((stats_six, stats_five, stats_four)):
        sums = jnp.sum(stats[...], axis=0)
        norm_out[2 * place : 2 * place + 1] = sums[:, C3 : 2 * C3]
        norm_out[2 * place + 1 : 2 * place + 2] = sums[:, 0:C3]
        if place == 2:
            loss[...] = sums[:, 2 * C3 : 2 * C3 + 128]
    value = norm_out[...]
    local[...] = pltpu.roll(value, C3 - ids[0] * (C3 // split), 1)[0:6, 0 : C3 // split]
    value = value * value / devices
    total = total + jnp.sum(jnp.sum(value, axis=0, keepdims=True), axis=1, keepdims=True)
    line[...] = jnp.broadcast_to(total[None], line.shape)


def clip_scale(squares):
    total = jnp.sum(jnp.sum(squares[...], axis=0), axis=1, keepdims=True)
    size = jnp.sqrt(total[:, 0:1] / 128.0)
    return (size, jnp.minimum(1.0, clip_limit / size))


def conv_update_kernel(sizes, *refs):
    pieces_count, places, step_rate, rates = sizes
    ids = refs[0]
    squares, weight, first, second = refs[1:5]
    small_in = refs[5:24]
    pieces = refs[24 : 24 + pieces_count]
    first_new, second_new, weight_new = refs[24 + pieces_count : 27 + pieces_count]
    small_out = refs[27 + pieces_count : 46 + pieces_count]
    held, small_held, sems, small_sems = refs[46 + pieces_count :]
    layer = pl.program_id(0)
    line = pl.program_id(1)

    def copies(wanted):
        made = []
        for number, (owner, start, size, side) in enumerate(places):
            if owner not in wanted:
                continue
            tall = pieces[number].shape[1]
            row = pl.multiple_of((ids[2] ^ side) * tall, 16)
            made.append(
                pltpu.make_async_copy(
                    pieces[number].at[0:size],
                    held.at[owner, start : start + size, pl.ds(row, tall), :],
                    sems.at[number],
                )
            )
        return made

    def small_copies():
        blocks = held.shape[1]
        return [
            pltpu.make_async_copy(
                pieces[side].at[blocks : blocks + 6], small_held.at[side], small_sems.at[side]
            )
            for side in range(2)
        ]

    @pl.when((layer == 0) & (line == 0))
    def _():
        for copy in small_copies() + copies((0, 1)):
            copy.start()

    @pl.when((layer == 0) & (line == 1))
    def _():
        for copy in small_copies():
            copy.wait()
        small_update(rates, ids, squares, small_held, small_in, small_out)

    for owner in range(2):

        @pl.when((layer == owner) & (line == 0))
        def _():
            for copy in copies((owner,)):
                copy.wait()

    size, scale = clip_scale(squares)
    for part in range(9):
        lanes = slice(part * 128, part * 128 + 128)
        block = line * 9 + part
        gradient = held[layer, block].astype(full) * scale
        results = adamw(
            weight[0, :, lanes], gradient, first[0, :, lanes], second[0, :, lanes], step_rate
        )
        first_new[0, :, lanes] = results[0]
        second_new[0, :, lanes] = results[1]
        weight_new[0, :, lanes] = results[2]


def small_update(rates, ids, squares, blocks, refs, outs):
    grad_norm_p = refs[0]
    states = refs[1:19]
    size_out = outs[18]
    size, scale = clip_scale(squares)
    size_out[...] = jnp.broadcast_to(size, size_out.shape)
    first_core = ids[2] == 0
    here = blocks[0].astype(full)
    there = blocks[1].astype(full)
    cores = (jnp.where(first_core, here, there), jnp.where(first_core, there, here))
    split_part, shared = [
        jnp.concatenate(
            [
                jnp.concatenate([core[first], core[first + 1], core[first + 2]], axis=1)
                for core in cores
            ],
            axis=0,
        ).astype(half)
        for first in (0, 3)
    ]
    grad_c = split_part[:, 0:C2].astype(full)
    classes = states[12].shape[0]
    pick = hot(iota((classes, WIDE), 0) + C2 == iota((classes, WIDE), 1))
    grad_head = dot(pick, split_part, NT)
    grad_b = shared[:, 0:C2].astype(full)
    pick = hot(iota((C0, WIDE), 0) + C2 == iota((C0, WIDE), 1))
    grad_a = dot(pick, shared, NT)
    pick = hot(iota((C0, WIDE), 0) + (C2 + 16) == iota((C0, WIDE), 1))
    grad_stem = dot(pick, shared[0:32], NT)[:, 0:27]
    gradients = (grad_stem, grad_a, grad_b, grad_c, grad_head, grad_norm_p[...])
    for index in range(6):
        weight, first, second = states[3 * index : 3 * index + 3]
        results = adamw(
            weight[...], gradients[index] * scale, first[...], second[...], rates[index]
        )
        for item in range(3):
            outs[3 * index + item][...] = results[item]


def xor_pairs(size, turn):
    return [(index, index ^ turn) for index in range(size)]


def shards(
    images,
    labels,
    corners,
    partners,
    stem_w,
    stem_w_m,
    stem_w_v,
    proj_a,
    proj_a_m,
    proj_a_v,
    proj_b,
    proj_b_m,
    proj_b_v,
    proj_c,
    proj_c_m,
    proj_c_v,
    conv_w,
    conv_w_m,
    conv_w_v,
    head_w,
    head_w_m,
    head_w_v,
    norm_p,
    norm_p_m,
    norm_p_v,
):
    split = lax.axis_size("dp")
    groups = lax.axis_size("filt")
    chips = groups // 2
    devices = split * groups
    count = images.shape[0]
    per = count // split
    rows = per * 64
    band = per * 8
    image_total = float(count * groups)
    row_total = image_total * 64.0
    tall = conv_w.shape[1] // 2
    spot_d = lax.axis_index("dp")
    spot_f = lax.axis_index("filt")
    ids = jnp.stack([spot_d, spot_f, spot_f % 2, spot_f // 2]).astype(jnp.int32)

    def over_dp(value, turn):
        return lax.ppermute(value, "dp", xor_pairs(split, turn))

    def over_filt(value, turn):
        return lax.ppermute(value, "filt", xor_pairs(groups, turn))

    def exchange(stats):
        return lax.all_to_all(stats, ("dp", "filt"), 0, 0)

    (own_images,) = call(
        image_kernel,
        [VMEM] * 4,
        [(shape((count, 3 * PLANE), half), VMEM)],
        [pltpu.VMEM((8, count), full)],
        3,
    )(
        images.transpose(1, 0, 2),
        labels.reshape(1, count),
        corners.T,
        partners.reshape(1, count),
    )
    far_images = [own_images] + [over_filt(own_images, 2 * turn) for turn in range(1, chips)]

    def start_gather(own):
        return [own, over_dp(own, 1), over_dp(own, 2)]

    def middle_gather(pieces, after):
        rows = pieces[0].shape[0]
        return cut_rows(pieces[:0:-1], [(0, 48), (48, rows - 48)], after)

    def cross(pieces):
        return [over_filt(piece, 1) for piece in pieces]

    def end_gather(pieces, crossed, far, after):
        far = [over_dp(far[0], 1), over_dp(far[1], 2)]
        far = cut_rows(far, [(0, piece.shape[0]) for piece in far], after)
        return [*pieces, *far, *crossed, *cross(far)]

    own_one, own_pack = cast_half(ids, conv_w, 0, [proj_c.T, head_w.T, norm_p], [own_images])
    (own_two,) = cast_half(ids, conv_w, 1, [], [own_one])
    far_pack = over_dp(own_pack, 3)
    pieces = start_gather(own_one)
    far = middle_gather(pieces, [])
    all_images = stack(
        far_images,
        [(turn, 0, count) for turn in range(chips)],
        (chips, count, 3 * PLANE),
        [own_two],
    )

    line = shape((devices, 1, 2 * C3))
    patches, stem_out, mid_one, mid_two, act_three, facts = call(
        functools.partial(front_kernel, (per, count, groups, devices, split)),
        [SMEM] + [VMEM] * 5,
        [
            (shape((rows, 32), half), VMEM),
            (shape((rows, C0)), VMEM),
            (shape((rows, C1)), VMEM),
            (shape((rows, WIDE)), VMEM),
            (shape((rows, WIDE), half), VMEM),
            (shape((per, 128)), VMEM),
        ],
        [
            pltpu.VMEM((per, 32, 128), full),
            pltpu.VMEM((rows, 32), full),
            pltpu.VMEM((C0, 32), full),
            pltpu.VMEM((C1, WIDE), half),
        ],
        10,
        1,
    )(ids, all_images, over_filt(all_images, 1), stem_w.T, proj_a, proj_b, far[0])
    crossed = cross(pieces)
    base, stats, norm_rows, head_all, proj_t = call(
        base_kernel,
        [SMEM, VMEM] + [ANY] * 7,
        [
            (shape((rows, C3)), ANY),
            (line, VMEM),
            (shape((8, C3)), VMEM),
            (shape((C3, 16), half), VMEM),
            (shape((C3, WIDE), half), VMEM),
        ],
        [
            pltpu.VMEM((C3, WIDE), half),
            pltpu.VMEM((rows, C3), full),
            pltpu.VMEM((8, C3), full),
            pltpu.SemaphoreType.DMA((10,)),
            pltpu.SemaphoreType.DMA((QUARTERS,)),
        ],
        4,
    )(ids, act_three, *pieces, *crossed, far_pack)
    kernels = [end_gather(pieces, crossed, far, [stats])]
    stats_one = exchange(stats)
    pieces = start_gather(hold(own_two, stats_one))

    table = pltpu.VMEM((rows, C3), full)
    conv_outs = [
        (shape((rows, C3)), ANY),
        (shape((rows, C3), half), ANY),
        (shape((rows, C3)), ANY),
        (line, VMEM),
    ]
    conv_scratch = [
        table,
        pltpu.VMEM((C3, 9 * C3), half),
        pltpu.VMEM((rows, TRIPLE), half),
        table,
        table,
        pltpu.SemaphoreType.DMA((10,)),
        pltpu.SemaphoreType.DMA((QUARTERS,)),
        pltpu.SemaphoreType.DMA((QUARTERS + 2,)),
    ]
    conv_one, field_one, slope_one, stats = call(
        functools.partial(conv_kernel, (per, row_total, split), 0),
        [SMEM, ANY, VMEM, VMEM] + [ANY] * 10,
        conv_outs,
        conv_scratch,
        18,
    )(ids, base, stats_one, norm_rows, *kernels[0])
    far = middle_gather(pieces, [stats])
    stats_two = exchange(stats)
    kernels.append(end_gather(pieces, cross(pieces), far, [stats_two]))
    far_field_one = over_filt(field_one, 1)
    summed, field_two, slope_two, stats = call(
        functools.partial(conv_kernel, (per, row_total, split), 1),
        [SMEM, ANY, VMEM, VMEM, ANY] + [ANY] * 10,
        conv_outs,
        conv_scratch,
        18,
    )(ids, conv_one, stats_two, norm_rows, base, *kernels[1])
    stats_three = exchange(stats)
    far_field_two = over_filt(field_two, 1)
    slope_three, spread, stats, grad_head = call(
        functools.partial(head_kernel, (per, row_total, image_total, head_w.shape[1])),
        [ANY] + [VMEM] * 4,
        [
            (shape((rows, C3)), ANY),
            (shape((band, C3)), VMEM),
            (shape((devices, 1, 2 * C3 + 128)), VMEM),
            (shape((C3, 16)), VMEM),
        ],
        [pltpu.VMEM((band, C3), full)] * 3
        + [table, table]
        + [pltpu.SemaphoreType.DMA((QUARTERS,)), pltpu.SemaphoreType.DMA((QUARTERS,))],
        7,
    )(summed, stats_three, norm_rows, head_all, facts)
    stats_four = exchange(stats)

    wide_half = pltpu.VMEM((rows, WIDE), half)
    picks = pltpu.VMEM((C3, 2 * WIDE), half)
    half_outs = [(shape((rows, WIDE), half), ANY)] * 2

    def back(layer, heads, tails, after):
        last = layer == 1
        return call(
            functools.partial(back_kernel, (per, row_total, split), layer),
            ([SMEM, ANY, ANY] + [VMEM] * 4 if last else [SMEM, ANY])
            + [ANY, ANY, VMEM]
            + [ANY] * 10,
            [(shape((rows, C3)), ANY), (line, VMEM)]
            + (half_outs + [(shape((rows, C3)), ANY)] if last else []),
            (
                [table, wide_half, wide_half, picks, pltpu.SemaphoreType.DMA((2 * QUARTERS + 1,))]
                if last
                else [pltpu.VMEM((rows, C3), half)]
            )
            + [
                table,
                table,
                pltpu.VMEM((C3, 9 * C3), half),
                pltpu.VMEM((rows, TRIPLE), half),
                table,
                pltpu.SemaphoreType.DMA((10,)),
                pltpu.SemaphoreType.DMA((2 * QUARTERS,)),
                pltpu.SemaphoreType.DMA((QUARTERS,)),
            ],
            22,
            len(after),
        )(ids, *heads, *tails, *kernels[layer], *after)

    grad_conv_one, stats, own_half, far_half, grad_summed = back(
        1,
        [slope_three, summed, stats_three, stats_four, norm_rows, spread],
        [conv_one, slope_two, stats_two],
        [],
    )
    stats_five = exchange(stats)

    def weight_grad(own_half, far_half, field, far_field, chunks, after):
        sizes = [part_sizes(split, lines) for lines in chunks]
        outs = [
            (shape((size, tall, 128), half), ANY) for parts in sizes for _, _, size in parts
        ]
        flat = call(
            functools.partial(weight_grad_kernel, (chunks, split, band)),
            [ANY] * 4,
            outs,
            [
                pltpu.VMEM((2 * rows, WIDE), half),
                pltpu.VMEM((2 * rows, TRIPLE), half),
                pltpu.VMEM((2, rows, C3), half),
                pltpu.VMEM((split, 45, tall, 128), half),
                pltpu.SemaphoreType.DMA((16,)),
                pltpu.SemaphoreType.DMA((16,)),
                pltpu.SemaphoreType.DMA((len(outs),)),
            ],
            13,
            len(after),
        )(own_half, over_filt(far_half, 1), field, far_field, *after)
        result = []
        for parts in sizes:
            result.append(flat[: len(parts)])
            flat = flat[len(parts) :]
        return result

    def add(values):
        return sum(value.astype(full) for value in values).astype(half)

    def start_dp(parts, after):
        own, near, next_near, far_low, far_high = parts
        blocks = near.shape[0]
        cut = far_low.shape[0]
        from_near = over_dp(far_low, 1)
        from_next = over_dp(far_high, 2)
        near, next_near = merge(
            [near, next_near, from_near, from_next],
            [
                (blocks, [(0, 0, 0, blocks), (3, 0, cut, blocks - cut)]),
                (blocks, [(1, 0, 0, blocks), (2, 0, 0, cut)]),
            ],
            after,
            3,
        )
        return [own, near, next_near]

    def end_dp(parts, sizes, after):
        own, near, next_near = parts
        plan = []
        start = 0
        for size in sizes:
            plan.append((size, [(source, start, 0, size) for source in range(3)]))
            start += size
        return merge([own, over_dp(near, 1), over_dp(next_near, 2)], plan, after, 0.1)

    def gated_add(left, right, after):
        if not after:
            return add([left, right])
        size = left.shape[0]
        return merge([left, right], [(size, [(0, 0, 0, size), (1, 0, 0, size)])], after, 0.1)[0]

    def chip_routes(reach):
        routes = []
        for move in ({0: 1, 3: 2}, {1: 2, 2: 1}, {1: 0, 2: 3}):
            pairs = []
            for index in range(groups):
                here = index // 2 // reach % 4
                if here in move:
                    pairs.append((index, index + (move[here] - here) * 2 * reach))
            routes.append(pairs)
        return routes

    def to_middles(value, reach, after):
        arrived = lax.ppermute(value, "filt", chip_routes(reach)[0])
        return gated_add(value, arrived, after)

    def between_middles(value, reach, after):
        return gated_add(value, lax.ppermute(value, "filt", chip_routes(reach)[1]), after)

    def outward(value, reach):
        return lax.ppermute(value, "filt", chip_routes(reach)[2])

    def from_middles(value, reach, after=(), arrived=None):
        if arrived is None:
            arrived = outward(value, reach)
        (result,) = call(
            functools.partial(pick_kernel, reach),
            [SMEM, ANY, ANY],
            [(shape(value.shape, half), VMEM)],
            [pltpu.SemaphoreType.DMA],
            0.1,
            len(after),
        )(ids, value, arrived, *after)
        return result

    def over_more_chips(value, reach):
        while reach < chips:
            value = from_middles(value, reach // 4)
            value = to_middles(value, reach, [])
            value = between_middles(value, reach, [])
            reach *= 4
        return value

    chunks_two = ((0, 1, 2),)
    chunks_one = ((0, 1, 2),)
    pairs_two = weight_grad(
        own_half, far_half, field_two, far_field_two, chunks_two, []
    )
    grad_one_half, own_half_one, far_half_one = call(
        functools.partial(norm_back_kernel, (row_total, split)),
        [SMEM, ANY, ANY, VMEM, VMEM, VMEM],
        [(shape((rows, C3), half), ANY)] + half_outs,
        [
            table,
            table,
            pltpu.VMEM((rows, C3), half),
            wide_half,
            wide_half,
            picks,
            pltpu.SemaphoreType.DMA((2 * QUARTERS,)),
            pltpu.SemaphoreType.DMA((3 * QUARTERS,)),
        ],
        6,
        1,
    )(ids, grad_conv_one, conv_one, stats_two, stats_five, norm_rows, pairs_two[0][0])
    pairs_one = weight_grad(
        own_half_one, far_half_one, field_one, far_field_one, chunks_one, [pairs_two[0][0]]
    )
    begun_two = start_dp(pairs_two[0], [pairs_one[0][0]])
    grad_base, stats = back(
        0,
        [grad_one_half],
        [base, slope_one, stats_one],
        [pairs_one[0][0], begun_two[1]],
    )
    stats_six = exchange(stats)
    begun_one = start_dp(pairs_one[0], [stats_six])
    blocks = begun_one[0].shape[0]
    (part_two,) = end_dp(begun_two, [blocks], [stats_six])
    small = shape((split, 6, tall, 128), half)
    small_mine, small_other = call(
        functools.partial(trunk_kernel, (per, row_total, split)),
        [SMEM] + [VMEM] * 15,
        [(small, ANY), (small, ANY)],
        [
            pltpu.VMEM((rows, C3), half),
            pltpu.VMEM((rows, WIDE), half),
            pltpu.VMEM((rows, C1), half),
            pltpu.VMEM((rows, C1), half),
            pltpu.VMEM((rows, C0), half),
            pltpu.VMEM((rows, C0), half),
            pltpu.VMEM((C1, WIDE), half),
            pltpu.VMEM((C3, WIDE), half),
            pltpu.VMEM((C1, WIDE), half),
            pltpu.SemaphoreType.DMA((12 * split,)),
        ],
        0.1,
        2,
    )(
        ids,
        grad_base,
        grad_summed,
        base,
        stats_one,
        stats_six,
        norm_rows,
        proj_t,
        act_three,
        mid_two,
        mid_one,
        stem_out,
        patches,
        proj_a,
        proj_b,
        grad_head,
        begun_one[1],
        part_two,
    )
    crossed = over_filt(small_other, 1)
    pair = [add([small_mine[turn], crossed[turn]]) for turn in range(split)]
    small_sum = add([pair[0]] + [over_dp(pair[turn], turn) for turn in range(1, split)])
    (part_one,) = end_dp(begun_one, [blocks], [small_mine])
    half_two = to_middles(part_two, 1, [part_one])
    half_one = to_middles(part_one, 1, [half_two, small_sum])
    whole_two = between_middles(half_two, 1, [half_one])
    whole_two = over_more_chips(whole_two, 4)
    last = chips // 4
    small_sum = between_middles(to_middles(small_sum, 1, []), 1, [])
    small_sum = over_more_chips(small_sum, 4)

    arrived_two = outward(whole_two, last)
    terms = [half_one, lax.ppermute(half_one, "filt", chip_routes(1)[1])]
    if chips > 4:
        terms = [over_more_chips(add(terms), 4)]
    plan = [(place, 0, 0, blocks) for place in range(len(terms))]
    plan.append((len(terms), 0, blocks, 6))
    (whole_one,) = merge([*terms, small_sum], [(blocks + 6, plan)], [], 0.1)
    arrived_one = outward(whole_one, last)
    squares, grad_norm_p, loss = call(
        functools.partial(norm_kernel, (devices, chips, split)),
        [SMEM] + [VMEM] * 5,
        [
            (shape((devices, 1, 128)), VMEM),
            (shape((6, C3 // split)), VMEM),
            (shape((1, 128)), VMEM),
        ],
        [pltpu.VMEM((8, C3), full)],
        3,
    )(ids, whole_one, whole_two, stats_six, stats_five, stats_four)
    reduced_two = from_middles(whole_two, last, [squares], arrived_two)
    far_two = over_filt(reduced_two, 1)
    squares = exchange(squares)
    reduced_one = from_middles(whole_one, last, [squares, far_two], arrived_one)

    pieces = []
    places = []
    far_one = over_filt(reduced_one, 1)
    for owner, both in enumerate(((reduced_one, far_one), (reduced_two, far_two))):
        pieces += both
        places += [(owner, 0, blocks, side) for side in range(2)]
    whole_spec = pl.BlockSpec((1, 2 * tall, 1152), lambda layer, line: (layer, 0, line))
    conv_shape = shape(conv_w.shape)
    states = (
        (stem_w.T, stem_w_m.T, stem_w_v.T),
        (proj_a, proj_a_m, proj_a_v),
        (proj_b, proj_b_m, proj_b_v),
        (proj_c.T, proj_c_m.T, proj_c_v.T),
        (head_w.T, head_w_m.T, head_w_v.T),
        (norm_p, norm_p_m, norm_p_v),
    )
    rates = (
        0.7 / math.sqrt(27.0),
        0.7 / math.sqrt(C0),
        0.7 / math.sqrt(C1),
        0.7 / math.sqrt(C2),
        0.7 / math.sqrt(C3 / 8.0),
        0.8,
    )
    flat = [item for group in states for item in group]
    updated = pl.pallas_call(
        functools.partial(
            conv_update_kernel, (len(pieces), places, 0.7 / math.sqrt(9.0 * C3), rates)
        ),
        grid=(2, 5),
        in_specs=[SMEM, VMEM, whole_spec, whole_spec, whole_spec]
        + [VMEM] * 19
        + [ANY] * len(pieces),
        out_specs=[whole_spec] * 3 + [VMEM] * 19,
        out_shape=[conv_shape] * 3 + [shape(item.shape) for item in flat] + [shape((1, 128))],
        scratch_shapes=[
            pltpu.VMEM((2, 45, 2 * tall, 128), half),
            pltpu.VMEM((2, 6, tall, 128), half),
            pltpu.SemaphoreType.DMA((len(pieces),)),
            pltpu.SemaphoreType.DMA((2,)),
        ],
        compiler_params=pltpu.CompilerParams(vmem_limit_bytes=63 * MIB),
        cost_estimate=pl.CostEstimate(
            flops=20 * conv_w.size, bytes_accessed=26 * conv_w.size, transcendentals=0
        ),
    )(
        ids,
        squares,
        conv_w,
        conv_w_m,
        conv_w_v,
        grad_norm_p,
        *flat,
        *pieces,
    )
    conv_new, small_new = updated[0:3], updated[3:]
    size = small_new[18][0, 0]
    turned = [
        item.T if index // 3 in (0, 3, 4) else item for index, item in enumerate(small_new[:18])
    ]
    return (
        *turned[0:12],
        *conv_new,
        *turned[12:18],
        loss[0, 0],
        size,
    )


def solution(mesh):
    placed = (
        P("filt", None, None),
        P("filt"),
        P("filt", None),
        P("filt"),
        *([P()] * 9),
        *([P(None, "dp")] * 3),
        *([P(None, "dp", None)] * 3),
        *([P("dp", None)] * 3),
        *([P(None, "dp")] * 3),
    )
    return jax.shard_map(
        shards,
        mesh=mesh,
        in_specs=placed,
        out_specs=(
            *([P()] * 9),
            *([P(None, "dp")] * 3),
            *([P(None, "dp", None)] * 3),
            *([P("dp", None)] * 3),
            *([P(None, "dp")] * 3),
            P(),
            P(),
        ),
        check_vma=False,
    )
```
